32 devices in a mesh: grp: 2 (over y), ep: 4 (over x, core), sub: 4 (over z).
Axes of the slice: x: 2, y: 2, z: 4, core: 2. Of those that a mesh axis runs over, the one named last changes fastest.
Arguments:
- tokens: bfloat16 [2, 512, 2880], P(None, ('grp', 'ep', 'sub')), parts along dimension 1
- norm_gain: float32 [2880], replicated, may hold values from 0.25 to 1.75
- copy_ids: int32 [2, 512, 4], P(None, ('grp', 'ep', 'sub')), parts along dimension 1, may hold values from 0 to 7, as said below
- gate_scores: float32 [2, 512, 4], P(None, ('grp', 'ep', 'sub')), parts along dimension 1, may hold values from 0.05 to 1
- inner_codes: bfloat16 [8, 2880, 2, 2880], P('ep', None, None, 'sub'), may hold values from -6 to 6
- inner_scales: bfloat16 [8, 90, 2, 2880], P('ep', None, None, 'sub'), may hold values from 0.0099487305 to 0.029907227
- down_codes: bfloat16 [8, 2880, 2880], P('ep', None, 'sub'), may hold values from -6 to 6
- down_scales: bfloat16 [8, 90, 2880], P('ep', None, 'sub'), may hold values from 0.014953613 to 0.044921875
Outputs:
- moe_out: bfloat16 [2, 512, 2880], P(None, ('grp', 'ep', 'sub')), parts along dimension 1
The draws below stay inside these ranges and needn't reach their ends.
There are 2 independent parts, one for each index of `grp`. The reference program is written for one: setup_inputs(seed, part) draws one part's arguments, and reference() takes and returns one part's arrays. A program takes and returns all parts, laid end to end along the dimension named above; an argument that names none is the same for every part. Nothing has to cross between parts.
Inputs may be any that keep to these rules, and one draw needn't show every extreme that they name: `copy_ids`: each token names 4 different experts. Among the tokens of one device in one step (aligned blocks of 16 tokens) no expert is named more than 12 times, and in each step one expert is named exactly 12 times by the tokens of every device.
All inputs are finite; a program needn't handle non-finite values.
Results may differ from the reference program's by a relative error of at most 0.0085.
Values may be sent and summed in bfloat16 or wider, within the bound.
No kernel may reach another device: no remote copies, remote signals or barrier semaphores. Data moves between devices by JAX's collectives and lax.ppermute only.
A program may use at most 192 MiB of HBM per device.

```python
import math
import jax
import jax.numpy as jnp
from jax import lax

D = 2880
FF = 2880
TOP = 4
STEPS = 2
TOK_DEV = 16
EXPERTS = 8
COPIES = 8
CAP = 12
TOKENS = 256
N_EP = 4
N_SUB = 4


def draw_tokens(key, part):
    key = jax.random.fold_in(key, 5)
    subkeys = jax.random.split(key, 3)
    extent = (STEPS, TOKENS, D)
    random_part = jnp.clip(jax.random.normal(subkeys[0], extent, jnp.float32), -4.0, 4.0)
    smallest = 0.3
    row_scale = jnp.exp(jax.random.uniform(subkeys[1], (STEPS, TOKENS, 1), jnp.float32, math.log(smallest), math.log(3.0)))
    col_scale = jnp.exp(jax.random.uniform(subkeys[2], (1, 1, D), jnp.float32, math.log(0.3), math.log(3.0)))
    return (random_part * row_scale * col_scale).astype(jnp.bfloat16)


def draw_copy_ids(key, part):
    key = jax.random.fold_in(key, 11)
    blocks_count = STEPS * TOKENS // TOK_DEV
    per_step = TOKENS // TOK_DEV
    assignments = TOK_DEV * TOP
    others = COPIES - 1
    spread = max(TOP, (assignments - 1) // CAP)
    subkeys = jax.random.split(key, 3)
    hot_copy = jax.random.randint(subkeys[0], (STEPS,), 0, COPIES).astype(jnp.int32)
    hot_block = jnp.repeat(hot_copy, per_step)
    rotation = jax.random.randint(subkeys[1], (blocks_count, 1), 0, TOK_DEV).astype(jnp.int32)
    scores = jax.random.randint(subkeys[2], (blocks_count, others), 0, 1 << 20).astype(jnp.int32) * others + jnp.arange(others, dtype=jnp.int32)[None, :]
    ranking = jnp.argsort(scores, axis=1).astype(jnp.int32)
    chosen = ranking + (ranking >= hot_block[:, None]).astype(jnp.int32)
    row_range = jnp.arange(TOK_DEV, dtype=jnp.int32)[None, :]
    hot_row = (row_range - rotation) % TOK_DEV < CAP
    leading = jnp.arange(TOP, dtype=jnp.int32)[None, None, :] == 0
    is_hot = jnp.logical_and(hot_row[:, :, None], leading).reshape(blocks_count, assignments)
    drawn = 1 - is_hot.astype(jnp.int32)
    counter = jnp.cumsum(drawn, axis=1) - drawn
    looked_up = jnp.take_along_axis(chosen, counter % spread, axis=1)
    result = jnp.where(is_hot, hot_block[:, None], looked_up)
    return result.reshape(STEPS, TOKENS, TOP).astype(jnp.int32)


def levels(stream_key, shape, shards, low, high):
    gain, own = 1.0, jax.random.fold_in(stream_key, 6)
    for axis_at, parts in shards:
        steps = jnp.exp(jax.random.uniform(jax.random.fold_in(own, axis_at), (parts,), jnp.float32, low / len(shards), high / len(shards)))
        gain = gain * jnp.repeat(steps, shape[axis_at] // parts).reshape([-1 if axis == axis_at else 1 for axis in range(len(shape))])
    return gain


def normal_values(stream_key, dims, scale, most, shards=(), kind=jnp.bfloat16):
    array = scale * jax.random.normal(stream_key, dims, jnp.float32)
    if shards:
        array = array * levels(stream_key, dims, shards, -0.22, 0.18)
    return jnp.clip(array, -most, most).astype(kind)


def setup_inputs(seed: int = 0, part: int = 0) -> dict:
    seeds = jax.random.split(jax.random.key(seed), 9)
    own_keys = jax.random.split(jax.random.fold_in(seeds[8], part), 9)
    return {
        "tokens": draw_tokens(jax.random.fold_in(jax.random.fold_in(seeds[8], part), 71), part),
        "norm_gain": jnp.clip(1.0 + 0.15 * jax.random.normal(seeds[1], (D,), jnp.float32), 0.25, 1.75),
        "copy_ids": draw_copy_ids(jax.random.fold_in(jax.random.fold_in(seeds[8], part), 71), part),
        "gate_scores": jnp.clip(jnp.exp(math.log(1.0) - 2.9957323 * jax.random.uniform(own_keys[3], (STEPS, TOKENS, TOP), jnp.float32) ** levels(own_keys[3], (STEPS, TOKENS, TOP), ((1, 16),), -0.2, 0.2)), 0.05, 1.0),
        "inner_codes": normal_values(seeds[4], (EXPERTS, D, 2, FF), 1.0, 6.0, ((0, 4), (3, 4))),
        "inner_scales": jnp.clip(jnp.exp(math.log(0.029907227) - 1.1006552 * jax.random.uniform(seeds[5], (EXPERTS, D // 32, 2, FF), jnp.float32) ** levels(seeds[5], (EXPERTS, D // 32, 2, FF), ((0, 4), (3, 4)), -0.2, 0.2)), 0.0099487305, 0.029907227).astype(jnp.bfloat16),
        "down_codes": normal_values(seeds[6], (EXPERTS, FF, D), 1.0, 6.0, ((0, 4), (2, 4))),
        "down_scales": jnp.clip(jnp.exp(math.log(0.044921875) - 1.0999719 * jax.random.uniform(seeds[7], (EXPERTS, FF // 32, D), jnp.float32) ** levels(seeds[7], (EXPERTS, FF // 32, D), ((0, 4), (2, 4)), -0.2, 0.2)), 0.014953613, 0.044921875).astype(jnp.bfloat16),
    }


epsilon = 1e-05
swish_beta = 1.702

def dequantize(codes, scales):
    widened = jnp.repeat(scales.astype(jnp.float32), 32, axis=0)
    return (codes.astype(jnp.float32) * widened).astype(jnp.bfloat16)

def expert_apply(bucket, inner_part, inner_scale_part, down_part, down_scale_part):
    inner = dequantize(inner_part, inner_scale_part).reshape(D, 2 * FF)
    hidden = jnp.dot(bucket, inner, preferred_element_type=jnp.float32)
    gating = hidden[:, :FF]
    upward = hidden[:, FF:]
    activation = (gating * jax.nn.sigmoid(swish_beta * gating) * (upward + 1.0)).astype(jnp.bfloat16)
    outer = dequantize(down_part, down_scale_part)
    return jnp.dot(activation, outer, preferred_element_type=jnp.float32).astype(jnp.bfloat16)

def slot_rows(step_ids):
    devices = N_EP * N_SUB
    blocks = step_ids.reshape(devices, TOK_DEV * TOP)
    onehot = (blocks[:, :, None] == jnp.arange(COPIES, dtype=jnp.int32)[None, None, :]).astype(jnp.int32)
    earlier = jnp.cumsum(onehot, axis=1) - onehot
    within = lax.optimization_barrier(jnp.sum(earlier * onehot, axis=2)).astype(jnp.int32)
    row_index = jnp.arange(devices, dtype=jnp.int32)[:, None] * CAP + within
    return row_index.reshape(TOKENS, TOP).astype(jnp.int32)

def reference(tokens, norm_gain, copy_ids, gate_scores, inner_codes, inner_scales, down_codes, down_scales):
    copy_range = jnp.arange(COPIES, dtype=jnp.int32)
    results = []
    for step_index in range(STEPS):
        values = tokens[step_index].astype(jnp.float32)
        normed = (values * lax.rsqrt(lax.optimization_barrier(jnp.mean(values * values, axis=-1, keepdims=True)) + epsilon) * norm_gain).astype(jnp.bfloat16)
        step_ids = copy_ids[step_index]
        row_index = slot_rows(step_ids)
        spread_rows = jnp.broadcast_to(normed[:, None, :], (TOKENS, TOP, D))
        buckets = jnp.zeros((COPIES, N_EP * N_SUB * CAP, D), jnp.bfloat16).at[step_ids, row_index].set(spread_rows)

        def per_copy(expert):
            return expert_apply(buckets[expert], inner_codes[expert], inner_scales[expert], down_codes[expert], down_scales[expert])
        answers = lax.map(per_copy, copy_range)
        picked = answers[step_ids, row_index].astype(jnp.float32)
        scores = gate_scores[step_index]
        weights = scores / lax.optimization_barrier(jnp.sum(scores, axis=-1, keepdims=True))
        results.append(lax.optimization_barrier(jnp.sum(weights[:, :, None] * picked, axis=1)).astype(jnp.bfloat16))
    return jnp.stack(results)
```

```python
import functools

import jax
import jax.numpy as jnp
from jax import lax
from jax.experimental import pallas as pl
from jax.experimental.pallas import tpu as pltpu
from jax.sharding import PartitionSpec as P

epsilon = 1e-05
swish_beta = 1.702
META = 64
LANES = 128
VMEM_LIMIT = 56 * 1024 * 1024
F32 = jnp.float32
BF16 = jnp.bfloat16


def params():
    return pltpu.CompilerParams(vmem_limit_bytes=VMEM_LIMIT)


def dot(a, b, contract):
    return lax.dot_general(a, b, (contract, ((), ())), preferred_element_type=F32)


def pack_kernel(tokens_ref, gain_ref, ids_ref, scores_ref, out_ref):
    steps, rows, width = tokens_ref.shape
    top = ids_ref.shape[2]
    for s in range(steps):
        values = tokens_ref[s].astype(F32)
        mean = jnp.mean(values * values, axis=-1, keepdims=True)
        normed = (values * lax.rsqrt(mean + epsilon) * gain_ref[...]).astype(BF16)
        at = slice(s * rows, (s + 1) * rows)
        out_ref[at, :width] = normed
        scores = scores_ref[s]
        weights = scores / jnp.sum(scores, axis=-1, keepdims=True)
        high = weights.astype(BF16)
        rest = weights - high.astype(F32)
        middle = rest.astype(BF16)
        low = (rest - middle.astype(F32)).astype(BF16)
        lane = lax.broadcasted_iota(jnp.int32, (rows, META), 1)
        meta = jnp.zeros((rows, META), F32)
        parts = (ids_ref[s].astype(F32), high.astype(F32), middle.astype(F32), low.astype(F32))
        for p, part in enumerate(parts):
            for k in range(top):
                meta = jnp.where(lane == p * top + k, part[:, k : k + 1], meta)
        out_ref[at, width:] = meta.astype(BF16)


def pack(tokens, gain, ids, scores):
    steps, rows, width = tokens.shape
    return pl.pallas_call(
        pack_kernel,
        out_shape=jax.ShapeDtypeStruct((steps * rows, width + META), BF16),
        compiler_params=params(),
    )(tokens, gain.reshape(1, width), ids, scores)


def dequant_kernel(codes_ref, scales_ref, spread_ref, out_ref):
    width = codes_ref.shape[2]
    chunk = 256
    scales = scales_ref[0]
    for at in range(0, width, chunk):
        end = min(at + chunk, width)
        wide = dot(scales, spread_ref[:, at:end], ((1,), (0,)))
        out_ref[0, :, at:end] = (codes_ref[0, :, at:end].astype(F32) * wide).astype(BF16)


def dequant(codes, scales):
    count, rows, width = codes.shape
    blocks = scales.shape[2]
    spread = (
        jnp.arange(blocks)[:, None] == jnp.arange(width)[None, :] // (width // blocks)
    ).astype(BF16)
    return pl.pallas_call(
        dequant_kernel,
        grid=(count,),
        in_specs=[
            pl.BlockSpec((1, rows, width), lambda i: (i, 0, 0)),
            pl.BlockSpec((1, rows, blocks), lambda i: (i, 0, 0)),
            pl.BlockSpec((blocks, width), lambda i: (0, 0)),
        ],
        out_specs=pl.BlockSpec((1, rows, width), lambda i: (i, 0, 0)),
        out_shape=jax.ShapeDtypeStruct(codes.shape, BF16),
        compiler_params=params(),
        cost_estimate=pl.CostEstimate(
            flops=2 * count * rows * width * 128,
            bytes_accessed=4 * count * rows * width,
            transcendentals=0,
        ),
    )(codes, scales, spread)


class Plan:
    def __init__(self, first, rows, holds, slots, subs, group, top, eps):
        self.first, self.rows = first, rows
        self.holds = holds
        self.slots, self.subs, self.group, self.top, self.eps = slots, subs, group, top, eps


def chosen(meta, expert, top):
    named = jnp.zeros((meta.shape[0], 1), F32)
    weight = jnp.zeros((meta.shape[0], 1), F32)
    for k in range(top):
        hit = (meta[:, META + k : META + k + 1] == expert).astype(F32)
        at = META + k
        total = (
            meta[:, at + top : at + top + 1]
            + meta[:, at + 2 * top : at + 2 * top + 1]
            + meta[:, at + 3 * top : at + 3 * top + 1]
        )
        named = named + hit
        weight = weight + hit * total
    return named, weight


def order_mask(count, plan, sub):
    def key(dim):
        t = lax.broadcasted_iota(jnp.int32, (count, count), dim)
        block = lax.rem(lax.div(t, plan.group), plan.subs)
        return t + (jnp.bitwise_xor(block, sub) - block) * plan.group

    return (key(1) < key(0)).astype(BF16)


def route(metas, plan, ep, sub):
    count = metas[0].shape[0]
    earlier = order_mask(count, plan, sub)
    lane = lax.broadcasted_iota(jnp.int32, (count, LANES), 1)
    start = jnp.zeros((1, 1), F32)
    result = []
    bounds = []
    for column, meta in enumerate(metas):
        if column:
            start = jnp.maximum(start, float(plan.holds[column - 1]))
        found = []
        flags = jnp.zeros((count, LANES), F32)
        for slot in range(plan.slots):
            named, weight = chosen(meta, (ep * plan.slots + slot).astype(F32), plan.top)
            found.append((named, weight))
            flags = jnp.where(lane == slot, named, flags)
        prefix = dot(earlier, flags.astype(BF16), ((1,), (0,)))
        places = []
        for slot, (named, weight) in enumerate(found):
            place = jnp.where(named > 0.0, prefix[:, slot : slot + 1] + start, -1.0)
            places.append((place, weight))
            end = start + jnp.sum(named, axis=0, keepdims=True)
            bounds.append((slot, start, end))
            start = end
        result.append(places)
    return result, bounds


def slot_masks(bounds, plan):
    row = lax.broadcasted_iota(jnp.int32, (1, plan.rows), 1).astype(F32) + float(plan.first)
    masks = []
    for slot in range(plan.slots):
        mask = jnp.zeros((1, plan.rows), F32)
        for which, start, end in bounds:
            if which == slot:
                mask = mask + jnp.logical_and(row >= start, row < end).astype(F32)
        masks.append(mask)
    return masks


def rows_of(places, plan):
    return (
        lax.broadcasted_iota(jnp.int32, (places.shape[0], plan.rows), 1).astype(F32)
        + float(plan.first)
        == places
    )


def inner_kernel(plan, arrays, place_ref, *refs):
    tokens = refs[:arrays]
    weight_ref = refs[arrays]
    act_ref, most_ref = refs[arrays + 1], refs[arrays + 2]
    rows_ref, mask_ref = refs[arrays + 3], refs[arrays + 4]
    width = weight_ref.shape[3]

    @pl.when(pl.program_id(0) == 0)
    def _():
        ep, sub = place_ref[0], place_ref[1]
        metas = []
        for c in range(arrays // 2):
            pair = [tokens[2 * c + h][:, width - META :].astype(F32) for h in range(2)]
            metas.append(jnp.concatenate(pair, axis=0))
        columns, bounds = route(metas, plan, ep, sub)
        for slot, mask in enumerate(slot_masks(bounds, plan)):
            mask_ref[slot : slot + 1] = mask
        half = tokens[0].shape[0]
        hots = []
        for places in columns:
            hot = None
            for place, _w in places:
                hit = rows_of(place, plan).astype(F32)
                hot = hit if hot is None else hot + hit
            hots.append(hot.astype(BF16))
        chunk = 256
        for at in range(0, width, chunk):
            end = min(at + chunk, width)
            total = None
            for c, hot in enumerate(hots):
                for h in range(2):
                    part = dot(
                        tokens[2 * c + h][:, at:end], hot[h * half : (h + 1) * half], ((0,), (0,))
                    )
                    total = part if total is None else total + part
            rows_ref[at:end] = total.astype(BF16)
        lane = lax.broadcasted_iota(jnp.int32, (metas[0].shape[0], LANES), 1).astype(F32)
        start = [jnp.zeros((1, 1), F32)] * plan.eps
        owner = lax.div(lax.broadcasted_iota(jnp.int32, (1, LANES), 1), plan.slots)
        for column, meta in enumerate(metas):
            flags = jnp.zeros((meta.shape[0], LANES), F32)
            for k in range(plan.top):
                flags = flags + (meta[:, META + k : META + k + 1] == lane).astype(F32)
            counts = jnp.sum(flags, axis=0, keepdims=True)
            for e in range(plan.eps):
                if column:
                    start[e] = jnp.maximum(start[e], float(plan.holds[column - 1]))
                start[e] = start[e] + jnp.sum(
                    jnp.where(owner == e, counts, 0.0), axis=1, keepdims=True
                )
        most_ref[...] = jnp.broadcast_to(functools.reduce(jnp.maximum, start), most_ref.shape)

    gating = upward = None
    x = rows_ref[...]
    for slot in range(plan.slots):
        gate = dot(weight_ref[slot, 0], x, ((1,), (0,)))
        up = dot(weight_ref[slot, 1], x, ((1,), (0,)))
        if slot == 0:
            gating, upward = gate, up
        else:
            mine = mask_ref[slot : slot + 1] > 0.0
            gating = jnp.where(mine, gate, gating)
            upward = jnp.where(mine, up, upward)
    act_ref[...] = (gating * jax.nn.sigmoid(swish_beta * gating) * (upward + 1.0)).astype(BF16)


def piece(total):
    for size in (144, 120, 72, 40, 24, 16, 8):
        if total % size == 0:
            return size
    return total


def inner(plan, place, tokens, weights):
    slots, _two, units, width = weights.shape
    block = piece(units)
    arrays = len(tokens)
    return pl.pallas_call(
        functools.partial(inner_kernel, plan, arrays),
        grid=(units // block,),
        in_specs=[pl.BlockSpec(memory_space=pltpu.SMEM)]
        + [pl.BlockSpec(t.shape, lambda i: (0, 0)) for t in tokens]
        + [pl.BlockSpec((slots, 2, block, width), lambda i: (0, 0, i, 0))],
        out_specs=[
            pl.BlockSpec((block, plan.rows), lambda i: (i, 0)),
            pl.BlockSpec((8, LANES), lambda i: (0, 0)),
        ],
        out_shape=[
            jax.ShapeDtypeStruct((units, plan.rows), BF16),
            jax.ShapeDtypeStruct((8, LANES), F32),
        ],
        scratch_shapes=[
            pltpu.VMEM((width, plan.rows), BF16),
            pltpu.VMEM((8, plan.rows), F32),
        ],
        compiler_params=params(),
        cost_estimate=pl.CostEstimate(
            flops=2 * plan.rows * slots * 2 * units * width,
            bytes_accessed=slots * 2 * units * width * 2,
            transcendentals=units * plan.rows,
        ),
    )(place, *tokens, weights)


def outer_kernel(plan, arrays, before, blocks, place_ref, *refs):
    metas_in = refs[:arrays]
    parts = refs[arrays : arrays + blocks]
    befores = refs[arrays + blocks : arrays + blocks + before]
    rest = refs[arrays + blocks + before :]
    weight_ref, keep_ref, send_ref, act_ref, sum_ref = rest
    sub = place_ref[1]
    units = parts[0].shape[0]
    slot = pl.program_id(0)

    @pl.when(slot == 0)
    def _():
        for b in range(plan.subs):
            for k in range(plan.subs):

                @pl.when(jnp.bitwise_xor(sub, k) == b)
                def _():
                    at = slice(b * units, (b + 1) * units)
                    if k == 3 and blocks == 5:
                        inside = jnp.logical_or(sub == 1, sub == 2)

                        @pl.when(inside)
                        def _():
                            act_ref[at] = parts[3][...]

                        @pl.when(jnp.logical_not(inside))
                        def _():
                            act_ref[at] = parts[4][...]
                    else:
                        act_ref[at] = parts[k][...]

    ep = place_ref[0]

    def routed():
        metas = []
        for c in range(arrays // 2):
            pair = [metas_in[2 * c + h][...].astype(F32) for h in range(2)]
            metas.append(jnp.concatenate(pair, axis=0))
        return route(metas, plan, ep, sub)

    out = dot(weight_ref[0], act_ref[...], ((1,), (0,)))

    @pl.when(slot == 0)
    def _():
        sum_ref[...] = out.astype(BF16)

    @pl.when(slot > 0)
    def _():
        _columns, bounds = routed()
        masks = slot_masks(bounds, plan)
        mine = masks[0]
        for s in range(1, plan.slots):
            mine = jnp.where(slot == s, masks[s], mine)
        sum_ref[...] = jnp.where(mine > 0.0, out.astype(BF16), sum_ref[...])

    @pl.when(slot == plan.slots - 1)
    def _():
        columns, _bounds = routed()
        done = sum_ref[...]
        for c, places in enumerate(columns):
            mix = None
            for place, weight in places:
                part = jnp.where(rows_of(place, plan), weight, 0.0)
                mix = part if mix is None else mix + part
            high = mix.astype(BF16)
            low = (mix - high.astype(F32)).astype(BF16)
            total = dot(high, done, ((1,), (1,))) + dot(low, done, ((1,), (1,)))
            half = total.shape[0] // 2
            for h, ref in enumerate((keep_ref, send_ref)):
                value = total[h * half : (h + 1) * half]
                if before and c < befores[h].shape[0]:
                    value = value + befores[h][c].astype(F32)
                ref[c] = value.astype(BF16)


def outer(plan, place, tokens, parts, befores, weights):
    slots, columns_out, width = weights.shape
    arrays, blocks = len(tokens), len(parts)
    half = tokens[0].shape[0]
    last = tokens[0].shape[1] // LANES - 1
    result = jax.ShapeDtypeStruct((arrays // 2, half, columns_out), BF16)
    return pl.pallas_call(
        functools.partial(outer_kernel, plan, arrays, len(befores), blocks),
        grid=(slots,),
        in_specs=[pl.BlockSpec(memory_space=pltpu.SMEM)]
        + [pl.BlockSpec((half, LANES), lambda i: (0, last)) for t in tokens]
        + [pl.BlockSpec(p.shape, lambda i: (0, 0)) for p in parts]
        + [pl.BlockSpec(b.shape, lambda i: (0, 0, 0)) for b in befores]
        + [pl.BlockSpec((1, columns_out, width), lambda i: (i, 0, 0))],
        out_specs=[pl.BlockSpec(result.shape, lambda i: (0, 0, 0))] * 2,
        out_shape=[result, result],
        scratch_shapes=[
            pltpu.VMEM((width, plan.rows), BF16),
            pltpu.VMEM((columns_out, plan.rows), BF16),
        ],
        compiler_params=params(),
        cost_estimate=pl.CostEstimate(
            flops=2 * plan.rows * slots * columns_out * width,
            bytes_accessed=slots * columns_out * width * 2,
            transcendentals=0,
        ),
    )(place, *tokens, *parts, *befores, weights)


def finish_kernel(subs, place_ref, *refs):
    parts, out_ref = refs[:subs], refs[subs]
    sub = place_ref[1]
    width = parts[0].shape[1]
    steps, rows, _ = out_ref.shape
    for b in range(subs):
        value = parts[0][...]
        for k in range(1, subs):
            value = jnp.where(jnp.bitwise_xor(sub, k) == b, parts[k][...], value)
        for s in range(steps):
            out_ref[s, :, b * width : (b + 1) * width] = value[s * rows : (s + 1) * rows]


def finish(place, parts, steps):
    rows, width = parts[0].shape
    subs = len(parts)
    return pl.pallas_call(
        functools.partial(finish_kernel, subs),
        in_specs=[pl.BlockSpec(memory_space=pltpu.SMEM)]
        + [pl.BlockSpec(memory_space=pltpu.VMEM)] * subs,
        out_specs=pl.BlockSpec(memory_space=pltpu.VMEM),
        out_shape=jax.ShapeDtypeStruct((steps, rows // steps, width * subs), BF16),
        compiler_params=params(),
    )(place, *parts)


def swap(x, axis, offset, count):
    return lax.ppermute(x, axis, [(i, i ^ offset) for i in range(count)])


def gather_sub(x, subs):
    if subs != 4:
        return [x] + [swap(x, "sub", k, subs) for k in range(1, subs)]
    two = swap(x, "sub", 2, subs)
    one = swap(x, "sub", 1, subs)
    middle = lax.ppermute(x, "sub", [(1, 2), (2, 1)])
    ends = lax.ppermute(two, "sub", [(2, 3), (1, 0)])
    return [x, one, two, middle, ends]


def add(a, b):
    return (a.astype(F32) + b.astype(F32)).astype(BF16)


def local(
    tokens, norm_gain, copy_ids, gate_scores, inner_codes, inner_scales, down_codes, down_scales
):
    eps, subs, groups = lax.axis_size("ep"), lax.axis_size("sub"), lax.axis_size("grp")
    slots = inner_codes.shape[0]
    steps, rows, top = copy_ids.shape
    units = inner_codes.shape[3]
    experts = eps * slots
    capacity = (3 * rows * top + 2 * experts - 1) // (2 * experts)
    columns = eps // 2
    place = jnp.stack([lax.axis_index("ep"), lax.axis_index("sub")]).astype(jnp.int32)
    group = steps * rows

    packed = pack(tokens, norm_gain, copy_ids, gate_scores)
    near = [packed] + [swap(packed, "sub", k, subs) for k in range(1, subs)]
    codes = jnp.transpose(inner_codes, (0, 2, 3, 1)).reshape(slots * 2, units, -1)
    scales = jnp.transpose(inner_scales, (0, 2, 3, 1)).reshape(slots * 2, units, -1)
    inner_weights = dequant(codes, scales).reshape(slots, 2, units, -1)
    outer_weights = dequant(
        jnp.transpose(down_codes, (0, 2, 1)), jnp.transpose(down_scales, (0, 2, 1))
    )
    own = jnp.concatenate(near, axis=0)
    other = swap(own, "ep", 1, eps)
    held = [[own, other]]
    for j in range(1, columns):
        arrived = swap(own, "ep", 2 * j, eps)
        held.append([arrived, swap(arrived, "ep", 1, eps)])

    capacity_rows = group * subs * 2 // rows * slots * capacity

    def plan(first, count, holds):
        return Plan(first, count, holds, slots, subs, group, top, eps)

    if columns == 2 and capacity_rows % 384 == 0:
        most = 2 * capacity_rows
        first = capacity_rows // 384 * 256
        second = capacity_rows
        last = most - first - second
        holds = (first,)
        plan0, plan1 = plan(0, first, holds), plan(first, second, holds)
        plan2 = plan(first + second, last, holds)
        everything = held[0] + held[1]
        act0, _ = inner(plan0, place, held[0], inner_weights)
        parts0 = gather_sub(act0, subs)
        act1, longest = inner(plan1, place, everything, inner_weights)
        parts1 = gather_sub(act1, subs)
        for shift in range(1, groups):
            moved = lax.ppermute(
                longest, "grp", [(i, (i + shift) % groups) for i in range(groups)]
            )
            longest = jnp.maximum(longest, moved)
        sums = outer(plan0, place, held[0], parts0, [], outer_weights)
        sums = outer(plan1, place, everything, parts1, sums, outer_weights)

        def more(kept, sent):
            act, _ = inner(plan2, place, everything, inner_weights)
            return tuple(
                outer(
                    plan2, place, everything, gather_sub(act, subs), [kept, sent], outer_weights
                )
            )

        keep, send = lax.cond(
            longest[0, 0] > float(first + second), more, lambda a, b: (a, b), *sums
        )
    else:
        count = -(-capacity_rows // LANES) * LANES
        each = plan(0, count, ())
        keeps, sends = [], []
        for pair in held:
            act, _ = inner(each, place, pair, inner_weights)
            kept, sent = outer(each, place, pair, gather_sub(act, subs), [], outer_weights)
            keeps.append(kept)
            sends.append(sent)
        keep, send = jnp.concatenate(keeps, axis=0), jnp.concatenate(sends, axis=0)

    chip = add(keep, swap(send, "ep", 1, eps))
    total = chip[0].astype(F32)
    for j in range(1, columns):
        total = total + swap(chip[j], "ep", 2 * j, eps).astype(F32)
    total = total.astype(BF16).reshape(subs, group, -1)
    arrived = [total[0]] + [swap(total[k], "sub", k, subs) for k in range(1, subs)]
    return finish(place, arrived, steps)


def solution(mesh):
    return jax.shard_map(
        local,
        mesh=mesh,
        in_specs=(
            P(None, ("grp", "ep", "sub"), None),
            P(),
            P(None, ("grp", "ep", "sub"), None),
            P(None, ("grp", "ep", "sub"), None),
            P("ep", None, None, "sub"),
            P("ep", None, None, "sub"),
            P("ep", None, "sub"),
            P("ep", None, "sub"),
        ),
        out_specs=P(None, ("grp", "ep", "sub"), None),
        check_vma=False,
    )
```

```python
import functools

import jax
import jax.numpy as jnp
from jax import lax
from jax.experimental import pallas as pl
from jax.experimental.pallas import tpu as pltpu
from jax.sharding import PartitionSpec as P

epsilon = 1e-05
swish_beta = 1.702
META = 64
LANES = 128
VMEM_LIMIT = 26 * 1024 * 1024
HINT = pl.CostEstimate(flops=1024, bytes_accessed=1024, transcendentals=0)
F32 = jnp.float32
BF16 = jnp.bfloat16


def params():
    return pltpu.CompilerParams(vmem_limit_bytes=VMEM_LIMIT)


def dot(a, b, contract):
    return lax.dot_general(a, b, (contract, ((), ())), preferred_element_type=F32)


def pack_kernel(tokens_ref, gain_ref, ids_ref, scores_ref, out_ref):
    steps, rows, width = tokens_ref.shape
    top = ids_ref.shape[1]
    gain = gain_ref[...].reshape(1, width)
    eye = (
        lax.broadcasted_iota(jnp.int32, (rows, rows), 0)
        == lax.broadcasted_iota(jnp.int32, (rows, rows), 1)
    ).astype(F32)

    def column(row):
        return jnp.sum(eye * row, axis=1, keepdims=True)

    for s in range(steps):
        values = tokens_ref[s].astype(F32)
        mean = jnp.mean(values * values, axis=-1, keepdims=True)
        normed = (values * lax.rsqrt(mean + epsilon) * gain).astype(BF16)
        at = slice(s * rows, (s + 1) * rows)
        out_ref[at, :width] = normed
        scores = scores_ref[s]
        weights = scores / jnp.sum(scores, axis=0, keepdims=True)
        high = weights.astype(BF16)
        rest = weights - high.astype(F32)
        middle = rest.astype(BF16)
        low = (rest - middle.astype(F32)).astype(BF16)
        lane = lax.broadcasted_iota(jnp.int32, (rows, META), 1)
        meta = jnp.zeros((rows, META), F32)
        parts = (ids_ref[s].astype(F32), high.astype(F32), middle.astype(F32), low.astype(F32))
        for p, part in enumerate(parts):
            for k in range(top):
                meta = jnp.where(lane == p * top + k, column(part[k : k + 1]), meta)
        out_ref[at, width:] = meta.astype(BF16)


def pack(tokens, gain, ids, scores):
    steps, rows, width = tokens.shape
    return pl.pallas_call(
        pack_kernel,
        out_shape=jax.ShapeDtypeStruct((steps * rows, width + META), BF16),
        compiler_params=params(),
    )(
        tokens, gain, jnp.transpose(ids, (0, 2, 1)), jnp.transpose(scores, (0, 2, 1))
    )


def dequant_kernel(codes_ref, scales_ref, _after_ref, out_ref):
    width = codes_ref.shape[2]
    scales = scales_ref[0]
    blocks = scales.shape[1]
    chunk = 256
    for at in range(0, width, chunk):
        end = min(at + chunk, width)
        column = lax.broadcasted_iota(jnp.int32, (blocks, end - at), 1) + at
        block = lax.broadcasted_iota(jnp.int32, (blocks, end - at), 0)
        first = block * (width // blocks)
        inside = jnp.logical_and(column >= first, column < first + width // blocks)
        wide = dot(scales, inside.astype(F32).astype(BF16), ((1,), (0,)))
        out_ref[0, :, at:end] = (codes_ref[0, :, at:end].astype(F32) * wide).astype(BF16)


def dequant(codes, scales, after):
    count, rows, width = codes.shape
    blocks = scales.shape[2]
    return pl.pallas_call(
        dequant_kernel,
        grid=(count,),
        in_specs=[
            pl.BlockSpec((1, rows, width), lambda i: (i, 0, 0)),
            pl.BlockSpec((1, rows, blocks), lambda i: (i, 0, 0)),
            pl.BlockSpec(memory_space=pl.ANY),
        ],
        out_specs=pl.BlockSpec((1, rows, width), lambda i: (i, 0, 0)),
        out_shape=jax.ShapeDtypeStruct(codes.shape, BF16),
        compiler_params=params(),
        cost_estimate=HINT,
    )(codes, scales, after)


def join_kernel(count, *refs):
    out_ref = refs[count + 1]
    rows = refs[0].shape[0]
    for k in range(count):
        out_ref[k * rows : (k + 1) * rows] = refs[k][...]


def join(parts, after):
    rows, width = parts[0].shape
    count = len(parts)
    return pl.pallas_call(
        functools.partial(join_kernel, count),
        grid=(1,),
        in_specs=[pl.BlockSpec((rows, width), lambda i: (0, 0))] * count
        + [pl.BlockSpec(memory_space=pl.ANY)],
        out_specs=pl.BlockSpec((count * rows, width), lambda i: (0, 0)),
        out_shape=jax.ShapeDtypeStruct((count * rows, width), BF16),
        compiler_params=params(),
    )(*parts, after)


class Plan:
    def __init__(self, first, rows, holds, slots, subs, group, top, eps):
        self.first, self.rows = first, rows
        self.holds = holds
        self.slots, self.subs, self.group, self.top, self.eps = slots, subs, group, top, eps


def chosen(meta, expert, top):
    named = jnp.zeros((meta.shape[0], 1), F32)
    weight = jnp.zeros((meta.shape[0], 1), F32)
    for k in range(top):
        hit = (meta[:, META + k : META + k + 1] == expert).astype(F32)
        at = META + k
        total = (
            meta[:, at + top : at + top + 1]
            + meta[:, at + 2 * top : at + 2 * top + 1]
            + meta[:, at + 3 * top : at + 3 * top + 1]
        )
        named = named + hit
        weight = weight + hit * total
    return named, weight


def order_mask(count, plan, sub):
    def key(dim):
        t = lax.broadcasted_iota(jnp.int32, (count, count), dim)
        block = lax.rem(lax.div(t, plan.group), plan.subs)
        return t + (jnp.bitwise_xor(block, sub) - block) * plan.group

    return (key(1) < key(0)).astype(BF16)


def route(metas, plan, ep, sub):
    count = metas[0].shape[0]
    earlier = order_mask(count, plan, sub)
    lane = lax.broadcasted_iota(jnp.int32, (count, LANES), 1)
    start = jnp.zeros((1, 1), F32)
    result = []
    bounds = []
    for column, meta in enumerate(metas):
        if column:
            start = jnp.maximum(start, float(plan.holds[column - 1]))
        found = []
        flags = jnp.zeros((count, LANES), F32)
        for slot in range(plan.slots):
            named, weight = chosen(meta, (ep * plan.slots + slot).astype(F32), plan.top)
            found.append((named, weight))
            flags = jnp.where(lane == slot, named, flags)
        prefix = dot(earlier, flags.astype(BF16), ((1,), (0,)))
        places = []
        for slot, (named, weight) in enumerate(found):
            place = jnp.where(named > 0.0, prefix[:, slot : slot + 1] + start, -1.0)
            places.append((place, weight))
            end = start + jnp.sum(named, axis=0, keepdims=True)
            bounds.append((slot, start, end))
            start = end
        result.append(places)
    return result, bounds


def slot_masks(bounds, plan):
    row = lax.broadcasted_iota(jnp.int32, (1, plan.rows), 1).astype(F32) + float(plan.first)
    masks = []
    for slot in range(plan.slots):
        mask = jnp.zeros((1, plan.rows), F32)
        for which, start, end in bounds:
            if which == slot:
                mask = mask + jnp.logical_and(row >= start, row < end).astype(F32)
        masks.append(mask)
    return masks


def rows_of(places, plan):
    return (
        lax.broadcasted_iota(jnp.int32, (places.shape[0], plan.rows), 1).astype(F32)
        + float(plan.first)
        == places
    )


def inner_kernel(plan, arrays, place_ref, *refs):
    tokens = refs[:arrays]
    weight_ref = refs[arrays]
    act_ref, most_ref, rows_ref, mask_ref = refs[arrays + 2 :]
    width = weight_ref.shape[3]

    @pl.when(pl.program_id(0) == 0)
    def _():
        ep, sub = place_ref[0], place_ref[1]
        metas = []
        for c in range(arrays // 2):
            pair = [tokens[2 * c + h][:, width - META :].astype(F32) for h in range(2)]
            metas.append(jnp.concatenate(pair, axis=0))
        columns, bounds = route(metas, plan, ep, sub)
        for slot, mask in enumerate(slot_masks(bounds, plan)):
            mask_ref[slot : slot + 1] = mask
        half = tokens[0].shape[0]
        hots = []
        for places in columns:
            hot = None
            for place, _w in places:
                hit = rows_of(place, plan).astype(F32)
                hot = hit if hot is None else hot + hit
            hots.append(hot.astype(BF16))
        chunk = 256
        for at in range(0, width, chunk):
            end = min(at + chunk, width)
            total = None
            for c, hot in enumerate(hots):
                for h in range(2):
                    part = dot(
                        tokens[2 * c + h][:, at:end], hot[h * half : (h + 1) * half], ((0,), (0,))
                    )
                    total = part if total is None else total + part
            rows_ref[at:end] = total.astype(BF16)
        lane = lax.broadcasted_iota(jnp.int32, (metas[0].shape[0], LANES), 1).astype(F32)
        start = [jnp.zeros((1, 1), F32)] * plan.eps
        owner = lax.div(lax.broadcasted_iota(jnp.int32, (1, LANES), 1), plan.slots)
        for column, meta in enumerate(metas):
            flags = jnp.zeros((meta.shape[0], LANES), F32)
            for k in range(plan.top):
                flags = flags + (meta[:, META + k : META + k + 1] == lane).astype(F32)
            counts = jnp.sum(flags, axis=0, keepdims=True)
            for e in range(plan.eps):
                if column:
                    start[e] = jnp.maximum(start[e], float(plan.holds[column - 1]))
                start[e] = start[e] + jnp.sum(
                    jnp.where(owner == e, counts, 0.0), axis=1, keepdims=True
                )
        most_ref[...] = jnp.broadcast_to(functools.reduce(jnp.maximum, start), most_ref.shape)

    slots, _two, block, _width = weight_ref.shape
    both = dot(weight_ref[...].reshape(slots * 2 * block, width), rows_ref[...], ((1,), (0,)))
    gating, upward = both[:block], both[block : 2 * block]
    for slot in range(1, plan.slots):
        mine = mask_ref[slot : slot + 1] > 0.0
        at = 2 * slot * block
        gating = jnp.where(mine, both[at : at + block], gating)
        upward = jnp.where(mine, both[at + block : at + 2 * block], upward)
    act_ref[...] = (gating * jax.nn.sigmoid(swish_beta * gating) * (upward + 1.0)).astype(BF16)


def piece(total):
    for size in (240, 120, 72, 40, 24, 16, 8):
        if total % size == 0:
            return size
    return total


def inner(plan, place, tokens, weights, after):
    slots, _two, units, width = weights.shape
    block = piece(units)
    arrays = len(tokens)
    return pl.pallas_call(
        functools.partial(inner_kernel, plan, arrays),
        grid=(units // block,),
        in_specs=[pl.BlockSpec(memory_space=pltpu.SMEM)]
        + [pl.BlockSpec(t.shape, lambda i: (0, 0)) for t in tokens]
        + [pl.BlockSpec((slots, 2, block, width), lambda i: (0, 0, i, 0))]
        + [pl.BlockSpec(memory_space=pl.ANY)],
        out_specs=[
            pl.BlockSpec((block, plan.rows), lambda i: (i, 0)),
            pl.BlockSpec((8, LANES), lambda i: (0, 0)),
        ],
        out_shape=[
            jax.ShapeDtypeStruct((units, plan.rows), BF16),
            jax.ShapeDtypeStruct((8, LANES), F32),
        ],
        scratch_shapes=[
            pltpu.VMEM((width, plan.rows), BF16),
            pltpu.VMEM((8, plan.rows), F32),
        ],
        compiler_params=params(),
        cost_estimate=HINT,
    )(place, *tokens, weights, after)


def outer_kernel(plan, arrays, before, blocks, place_ref, *refs):
    metas_in = refs[:arrays]
    parts = refs[arrays : arrays + blocks]
    befores = refs[arrays + blocks : arrays + blocks + before]
    rest = refs[arrays + blocks + before :]
    weight_ref, keep_ref, send_ref, act_ref, sum_ref = rest
    sub = place_ref[1]
    units = parts[0].shape[0]
    slot = pl.program_id(0)

    @pl.when(slot == 0)
    def _():
        for b in range(plan.subs):
            for k in range(plan.subs):

                @pl.when(jnp.bitwise_xor(sub, k) == b)
                def _():
                    at = slice(b * units, (b + 1) * units)
                    if k == 3 and blocks == 5:
                        inside = jnp.logical_or(sub == 1, sub == 2)

                        @pl.when(inside)
                        def _():
                            act_ref[at] = parts[3][...]

                        @pl.when(jnp.logical_not(inside))
                        def _():
                            act_ref[at] = parts[4][...]
                    else:
                        act_ref[at] = parts[k][...]

    ep = place_ref[0]

    def routed():
        metas = []
        for c in range(arrays // 2):
            pair = [metas_in[2 * c + h][...].astype(F32) for h in range(2)]
            metas.append(jnp.concatenate(pair, axis=0))
        return route(metas, plan, ep, sub)

    out = dot(weight_ref[0], act_ref[...], ((1,), (0,)))

    @pl.when(slot == 0)
    def _():
        sum_ref[...] = out.astype(BF16)

    @pl.when(slot > 0)
    def _():
        _columns, bounds = routed()
        masks = slot_masks(bounds, plan)
        mine = masks[0]
        for s in range(1, plan.slots):
            mine = jnp.where(slot == s, masks[s], mine)
        sum_ref[...] = jnp.where(mine > 0.0, out.astype(BF16), sum_ref[...])

    @pl.when(slot == plan.slots - 1)
    def _():
        columns, _bounds = routed()
        done = sum_ref[...]
        for c, places in enumerate(columns):
            mix = None
            for place, weight in places:
                part = jnp.where(rows_of(place, plan), weight, 0.0)
                mix = part if mix is None else mix + part
            high = mix.astype(BF16)
            low = (mix - high.astype(F32)).astype(BF16)
            total = dot(high, done, ((1,), (1,))) + dot(low, done, ((1,), (1,)))
            half = total.shape[0] // 2
            for h, ref in enumerate((keep_ref, send_ref)):
                value = total[h * half : (h + 1) * half]
                if before and c < befores[h].shape[0]:
                    value = value + befores[h][c].astype(F32)
                ref[c] = value.astype(BF16)


def outer(plan, place, tokens, parts, befores, weights):
    slots, columns_out, width = weights.shape
    arrays, blocks = len(tokens), len(parts)
    half = tokens[0].shape[0]
    last = tokens[0].shape[1] // LANES - 1
    result = jax.ShapeDtypeStruct((arrays // 2, half, columns_out), BF16)
    return pl.pallas_call(
        functools.partial(outer_kernel, plan, arrays, len(befores), blocks),
        grid=(slots,),
        in_specs=[pl.BlockSpec(memory_space=pltpu.SMEM)]
        + [pl.BlockSpec((half, LANES), lambda i: (0, last)) for t in tokens]
        + [pl.BlockSpec(p.shape, lambda i: (0, 0)) for p in parts]
        + [pl.BlockSpec(b.shape, lambda i: (0, 0, 0)) for b in befores]
        + [pl.BlockSpec((1, columns_out, width), lambda i: (i, 0, 0))],
        out_specs=[pl.BlockSpec(result.shape, lambda i: (0, 0, 0))] * 2,
        out_shape=[result, result],
        scratch_shapes=[
            pltpu.VMEM((width, plan.rows), BF16),
            pltpu.VMEM((columns_out, plan.rows), BF16),
        ],
        compiler_params=params(),
        cost_estimate=HINT,
    )(place, *tokens, *parts, *befores, weights)


def finish_kernel(subs, columns, place_ref, *refs):
    out_ref = refs[-1]
    sub = place_ref[1]
    width = refs[0].shape[1]
    steps, rows, _ = out_ref.shape
    sums = []
    for k in range(subs):
        value = refs[k * columns][...].astype(F32)
        for j in range(1, columns):
            value = value + refs[k * columns + j][...].astype(F32)
        sums.append(value)
    for b in range(subs):
        value = sums[0]
        for k in range(1, subs):
            value = jnp.where(jnp.bitwise_xor(sub, k) == b, sums[k], value)
        value = value.astype(BF16)
        for s in range(steps):
            out_ref[s, :, b * width : (b + 1) * width] = value[s * rows : (s + 1) * rows]


def finish(place, parts, steps):
    subs, columns = len(parts), len(parts[0])
    rows, width = parts[0][0].shape
    return pl.pallas_call(
        functools.partial(finish_kernel, subs, columns),
        grid=(1,),
        in_specs=[pl.BlockSpec(memory_space=pltpu.SMEM)]
        + [pl.BlockSpec((rows, width), lambda i: (0, 0))] * (subs * columns),
        out_specs=pl.BlockSpec((steps, rows // steps, width * subs), lambda i: (0, 0, 0)),
        out_shape=jax.ShapeDtypeStruct((steps, rows // steps, width * subs), BF16),
        compiler_params=params(),
    )(place, *[p for several in parts for p in several])


def swap(x, axis, offset, count):
    return lax.ppermute(x, axis, [(i, i ^ offset) for i in range(count)])


def gather_sub(x, subs):
    if subs != 4:
        return [x] + [swap(x, "sub", k, subs) for k in range(1, subs)]
    two = swap(x, "sub", 2, subs)
    one = swap(x, "sub", 1, subs)
    middle = lax.ppermute(x, "sub", [(1, 2), (2, 1)])
    ends = lax.ppermute(two, "sub", [(2, 3), (1, 0)])
    return [x, one, two, middle, ends]


def add(a, b):
    return (a.astype(F32) + b.astype(F32)).astype(BF16)


def local(
    tokens, norm_gain, copy_ids, gate_scores, inner_codes, inner_scales, down_codes, down_scales
):
    eps, subs, groups = lax.axis_size("ep"), lax.axis_size("sub"), lax.axis_size("grp")
    slots = inner_codes.shape[0]
    steps, rows, top = copy_ids.shape
    units = inner_codes.shape[3]
    experts = eps * slots
    capacity = (3 * rows * top + 2 * experts - 1) // (2 * experts)
    columns = eps // 2
    place = jnp.stack([lax.axis_index("ep"), lax.axis_index("sub")]).astype(jnp.int32)
    group = steps * rows

    packed = pack(tokens, norm_gain, copy_ids, gate_scores)
    near = [packed] + [swap(packed, "sub", k, subs) for k in range(1, subs)]
    codes = jnp.transpose(inner_codes, (0, 2, 3, 1)).reshape(slots * 2, units, -1)
    scales = jnp.transpose(inner_scales, (0, 2, 3, 1)).reshape(slots * 2, units, -1)
    inner_weights = dequant(codes, scales, packed).reshape(slots, 2, units, -1)
    outer_codes = jnp.transpose(down_codes, (0, 2, 1))
    outer_scales = jnp.transpose(down_scales, (0, 2, 1))
    own = join(near, inner_weights)
    other = swap(own, "ep", 1, eps)
    held = [[own, other]]
    for j in range(1, columns):
        arrived = swap(own, "ep", 2 * j, eps)
        held.append([arrived, swap(arrived, "ep", 1, eps)])

    capacity_rows = group * subs * 2 // rows * slots * capacity

    def plan(first, count, holds):
        return Plan(first, count, holds, slots, subs, group, top, eps)

    if columns == 2 and capacity_rows % 384 == 0:
        most = 2 * capacity_rows
        first = capacity_rows // 384 * 256
        second = capacity_rows
        last = most - first - second
        holds = (first,)
        plan0, plan1 = plan(0, first, holds), plan(first, second, holds)
        plan2 = plan(first + second, last, holds)
        everything = held[0] + held[1]
        act0, mark = inner(plan0, place, held[0], inner_weights, own)
        mark = swap(mark, "ep", 1, eps)
        parts0 = gather_sub(act0, subs)
        act1, longest = inner(plan1, place, everything, inner_weights, mark)
        parts1 = gather_sub(act1, subs)
        for shift in range(1, groups):
            moved = lax.ppermute(
                longest, "grp", [(i, (i + shift) % groups) for i in range(groups)]
            )
            longest = jnp.maximum(longest, moved)
        outer_weights = dequant(outer_codes, outer_scales, longest)
        sums = outer(plan0, place, held[0], parts0, [], outer_weights)
        sums = outer(plan1, place, everything, parts1, sums, outer_weights)

        def more(kept, sent):
            act, _ = inner(plan2, place, everything, inner_weights, kept)
            return tuple(
                outer(
                    plan2, place, everything, gather_sub(act, subs), [kept, sent], outer_weights
                )
            )

        keep, send = lax.cond(
            longest[0, 0] > float(first + second), more, lambda a, b: (a, b), *sums
        )
    else:
        count = -(-capacity_rows // LANES) * LANES
        each = plan(0, count, ())
        outer_weights = dequant(outer_codes, outer_scales, own)
        keeps, sends = [], []
        for pair in held:
            act, _ = inner(each, place, pair, inner_weights, own)
            kept, sent = outer(each, place, pair, gather_sub(act, subs), [], outer_weights)
            keeps.append(kept)
            sends.append(sent)
        keep, send = jnp.concatenate(keeps, axis=0), jnp.concatenate(sends, axis=0)

    chip = add(keep, swap(send, "ep", 1, eps))
    chip = chip.reshape(columns, subs, group, -1)
    arrived = []
    for k in range(subs):
        arrived.append([])
        for j in range(columns):
            pairs = []
            for e in range(eps):
                for z in range(subs):
                    pairs.append((e * subs + z, (e ^ (2 * j)) * subs + (z ^ k)))
            block = chip[j, k]
            arrived[-1].append(lax.ppermute(block, ("ep", "sub"), pairs) if j + k else block)
    return finish(place, arrived, steps)


def solution(mesh):
    return jax.shard_map(
        local,
        mesh=mesh,
        in_specs=(
            P(None, ("grp", "ep", "sub"), None),
            P(),
            P(None, ("grp", "ep", "sub"), None),
            P(None, ("grp", "ep", "sub"), None),
            P("ep", None, None, "sub"),
            P("ep", None, None, "sub"),
            P("ep", None, "sub"),
            P("ep", None, "sub"),
        ),
        out_specs=P(None, ("grp", "ep", "sub"), None),
        check_vma=False,
    )
```

```python
import functools

import jax
import jax.numpy as jnp
from jax import lax
from jax.experimental import pallas as pl
from jax.experimental.pallas import tpu as pltpu
from jax.sharding import PartitionSpec as P

epsilon = 1e-05
swish_beta = 1.702
META = 64
LANES = 128
VMEM_LIMIT = 26 * 1024 * 1024
HINT = pl.CostEstimate(flops=1024, bytes_accessed=1024, transcendentals=0)
F32 = jnp.float32
BF16 = jnp.bfloat16


def params():
    return pltpu.CompilerParams(vmem_limit_bytes=VMEM_LIMIT)


def dot(a, b, contract):
    return lax.dot_general(a, b, (contract, ((), ())), preferred_element_type=F32)


def pack_kernel(tokens_ref, gain_ref, ids_ref, scores_ref, out_ref):
    steps, rows, width = tokens_ref.shape
    top = ids_ref.shape[1]
    gain = gain_ref[...].reshape(1, width)
    eye = (
        lax.broadcasted_iota(jnp.int32, (rows, rows), 0)
        == lax.broadcasted_iota(jnp.int32, (rows, rows), 1)
    ).astype(F32)

    def column(row):
        return jnp.sum(eye * row, axis=1, keepdims=True)

    for s in range(steps):
        values = tokens_ref[s].astype(F32)
        mean = jnp.mean(values * values, axis=-1, keepdims=True)
        normed = (values * lax.rsqrt(mean + epsilon) * gain).astype(BF16)
        at = slice(s * rows, (s + 1) * rows)
        out_ref[at, :width] = normed
        scores = scores_ref[s]
        weights = scores / jnp.sum(scores, axis=0, keepdims=True)
        high = weights.astype(BF16)
        rest = weights - high.astype(F32)
        middle = rest.astype(BF16)
        low = (rest - middle.astype(F32)).astype(BF16)
        lane = lax.broadcasted_iota(jnp.int32, (rows, META), 1)
        meta = jnp.zeros((rows, META), F32)
        parts = (ids_ref[s].astype(F32), high.astype(F32), middle.astype(F32), low.astype(F32))
        for p, part in enumerate(parts):
            for k in range(top):
                meta = jnp.where(lane == p * top + k, column(part[k : k + 1]), meta)
        out_ref[at, width:] = meta.astype(BF16)


def pack(tokens, gain, ids, scores):
    steps, rows, width = tokens.shape
    return pl.pallas_call(
        pack_kernel,
        out_shape=jax.ShapeDtypeStruct((steps * rows, width + META), BF16),
        compiler_params=params(),
    )(
        tokens, gain, jnp.transpose(ids, (0, 2, 1)), jnp.transpose(scores, (0, 2, 1))
    )


def dequant_kernel(codes_ref, scales_ref, _after_ref, out_ref):
    width = codes_ref.shape[2]
    scales = scales_ref[0]
    blocks = scales.shape[1]
    chunk = 256
    for at in range(0, width, chunk):
        end = min(at + chunk, width)
        column = lax.broadcasted_iota(jnp.int32, (blocks, end - at), 1) + at
        block = lax.broadcasted_iota(jnp.int32, (blocks, end - at), 0)
        first = block * (width // blocks)
        inside = jnp.logical_and(column >= first, column < first + width // blocks)
        wide = dot(scales, inside.astype(F32).astype(BF16), ((1,), (0,)))
        out_ref[0, :, at:end] = (codes_ref[0, :, at:end].astype(F32) * wide).astype(BF16)


def dequant(codes, scales, after):
    count, rows, width = codes.shape
    blocks = scales.shape[2]
    return pl.pallas_call(
        dequant_kernel,
        grid=(count,),
        in_specs=[
            pl.BlockSpec((1, rows, width), lambda i: (i, 0, 0)),
            pl.BlockSpec((1, rows, blocks), lambda i: (i, 0, 0)),
            pl.BlockSpec(memory_space=pl.ANY),
        ],
        out_specs=pl.BlockSpec((1, rows, width), lambda i: (i, 0, 0)),
        out_shape=jax.ShapeDtypeStruct(codes.shape, BF16),
        compiler_params=params(),
        cost_estimate=HINT,
    )(codes, scales, after)


def join_kernel(count, *refs):
    out_ref = refs[count + 1]
    rows = refs[0].shape[0]
    for k in range(count):
        out_ref[k * rows : (k + 1) * rows] = refs[k][...]


def join(parts, after):
    rows, width = parts[0].shape
    count = len(parts)
    return pl.pallas_call(
        functools.partial(join_kernel, count),
        grid=(1,),
        in_specs=[pl.BlockSpec((rows, width), lambda i: (0, 0))] * count
        + [pl.BlockSpec(memory_space=pl.ANY)],
        out_specs=pl.BlockSpec((count * rows, width), lambda i: (0, 0)),
        out_shape=jax.ShapeDtypeStruct((count * rows, width), BF16),
        compiler_params=params(),
    )(*parts, after)


class Plan:
    def __init__(self, first, rows, holds, slots, subs, group, top, eps):
        self.first, self.rows = first, rows
        self.holds = holds
        self.slots, self.subs, self.group, self.top, self.eps = slots, subs, group, top, eps


def chosen(meta, expert, top):
    named = jnp.zeros((meta.shape[0], 1), F32)
    weight = jnp.zeros((meta.shape[0], 1), F32)
    for k in range(top):
        hit = (meta[:, META + k : META + k + 1] == expert).astype(F32)
        at = META + k
        total = (
            meta[:, at + top : at + top + 1]
            + meta[:, at + 2 * top : at + 2 * top + 1]
            + meta[:, at + 3 * top : at + 3 * top + 1]
        )
        named = named + hit
        weight = weight + hit * total
    return named, weight


def order_mask(count, plan, sub):
    def key(dim):
        t = lax.broadcasted_iota(jnp.int32, (count, count), dim)
        block = lax.rem(lax.div(t, plan.group), plan.subs)
        return t + (jnp.bitwise_xor(block, sub) - block) * plan.group

    return (key(1) < key(0)).astype(BF16)


def route(metas, plan, ep, sub):
    count = metas[0].shape[0]
    earlier = order_mask(count, plan, sub)
    lane = lax.broadcasted_iota(jnp.int32, (count, LANES), 1)
    start = jnp.zeros((1, 1), F32)
    result = []
    bounds = []
    for column, meta in enumerate(metas):
        if column:
            start = jnp.maximum(start, float(plan.holds[column - 1]))
        found = []
        flags = jnp.zeros((count, LANES), F32)
        for slot in range(plan.slots):
            named, weight = chosen(meta, (ep * plan.slots + slot).astype(F32), plan.top)
            found.append((named, weight))
            flags = jnp.where(lane == slot, named, flags)
        prefix = dot(earlier, flags.astype(BF16), ((1,), (0,)))
        places = []
        for slot, (named, weight) in enumerate(found):
            place = jnp.where(named > 0.0, prefix[:, slot : slot + 1] + start, -1.0)
            places.append((place, weight))
            end = start + jnp.sum(named, axis=0, keepdims=True)
            bounds.append((slot, start, end))
            start = end
        result.append(places)
    return result, bounds


def slot_masks(bounds, plan):
    row = lax.broadcasted_iota(jnp.int32, (1, plan.rows), 1).astype(F32) + float(plan.first)
    masks = []
    for slot in range(plan.slots):
        mask = jnp.zeros((1, plan.rows), F32)
        for which, start, end in bounds:
            if which == slot:
                mask = mask + jnp.logical_and(row >= start, row < end).astype(F32)
        masks.append(mask)
    return masks


def rows_of(places, plan):
    return (
        lax.broadcasted_iota(jnp.int32, (places.shape[0], plan.rows), 1).astype(F32)
        + float(plan.first)
        == places
    )


def inner_kernel(plan, arrays, place_ref, *refs):
    tokens = refs[:arrays]
    weight_ref = refs[arrays]
    act_ref, most_ref, rows_ref, mask_ref = refs[-4:]
    width = weight_ref.shape[3]

    @pl.when(pl.program_id(0) == 0)
    def _():
        ep, sub = place_ref[0], place_ref[1]
        metas = []
        for c in range(arrays // 2):
            pair = [tokens[2 * c + h][:, width - META :].astype(F32) for h in range(2)]
            metas.append(jnp.concatenate(pair, axis=0))
        columns, bounds = route(metas, plan, ep, sub)
        for slot, mask in enumerate(slot_masks(bounds, plan)):
            mask_ref[slot : slot + 1] = mask
        half = tokens[0].shape[0]
        hots = []
        for places in columns:
            hot = None
            for place, _w in places:
                hit = rows_of(place, plan).astype(F32)
                hot = hit if hot is None else hot + hit
            hots.append(hot.astype(BF16))
        chunk = 256
        for at in range(0, width, chunk):
            end = min(at + chunk, width)
            total = None
            for c, hot in enumerate(hots):
                for h in range(2):
                    part = dot(
                        tokens[2 * c + h][:, at:end], hot[h * half : (h + 1) * half], ((0,), (0,))
                    )
                    total = part if total is None else total + part
            rows_ref[at:end] = total.astype(BF16)
        lane = lax.broadcasted_iota(jnp.int32, (metas[0].shape[0], LANES), 1).astype(F32)
        start = [jnp.zeros((1, 1), F32)] * plan.eps
        owner = lax.div(lax.broadcasted_iota(jnp.int32, (1, LANES), 1), plan.slots)
        for column, meta in enumerate(metas):
            flags = jnp.zeros((meta.shape[0], LANES), F32)
            for k in range(plan.top):
                flags = flags + (meta[:, META + k : META + k + 1] == lane).astype(F32)
            counts = jnp.sum(flags, axis=0, keepdims=True)
            for e in range(plan.eps):
                if column:
                    start[e] = jnp.maximum(start[e], float(plan.holds[column - 1]))
                start[e] = start[e] + jnp.sum(
                    jnp.where(owner == e, counts, 0.0), axis=1, keepdims=True
                )
        most_ref[...] = jnp.broadcast_to(functools.reduce(jnp.maximum, start), most_ref.shape)

    slots, _two, block, _width = weight_ref.shape
    both = dot(weight_ref[...].reshape(slots * 2 * block, width), rows_ref[...], ((1,), (0,)))
    gating, upward = both[:block], both[block : 2 * block]
    for slot in range(1, plan.slots):
        mine = mask_ref[slot : slot + 1] > 0.0
        at = 2 * slot * block
        gating = jnp.where(mine, both[at : at + block], gating)
        upward = jnp.where(mine, both[at + block : at + 2 * block], upward)
    act_ref[...] = (gating * jax.nn.sigmoid(swish_beta * gating) * (upward + 1.0)).astype(BF16)


def piece(total):
    for size in (240, 120, 72, 40, 24, 16, 8):
        if total % size == 0:
            return size
    return total


def inner(plan, place, tokens, weights, after):
    slots, _two, units, width = weights.shape
    block = piece(units)
    arrays = len(tokens)
    return pl.pallas_call(
        functools.partial(inner_kernel, plan, arrays),
        grid=(units // block,),
        in_specs=[pl.BlockSpec(memory_space=pltpu.SMEM)]
        + [pl.BlockSpec(t.shape, lambda i: (0, 0)) for t in tokens]
        + [pl.BlockSpec((slots, 2, block, width), lambda i: (0, 0, i, 0))]
        + [pl.BlockSpec(memory_space=pl.ANY)] * len(after),
        out_specs=[
            pl.BlockSpec((block, plan.rows), lambda i: (i, 0)),
            pl.BlockSpec((8, LANES), lambda i: (0, 0)),
        ],
        out_shape=[
            jax.ShapeDtypeStruct((units, plan.rows), BF16),
            jax.ShapeDtypeStruct((8, LANES), F32),
        ],
        scratch_shapes=[
            pltpu.VMEM((width, plan.rows), BF16),
            pltpu.VMEM((8, plan.rows), F32),
        ],
        compiler_params=params(),
        cost_estimate=HINT,
    )(place, *tokens, weights, *after)


def outer_kernel(plan, arrays, before, blocks, place_ref, *refs):
    metas_in = refs[:arrays]
    parts = refs[arrays : arrays + blocks]
    befores = refs[arrays + blocks : arrays + blocks + before]
    rest = refs[arrays + blocks + before :]
    weight_ref, keep_ref, send_ref, act_ref, sum_ref = rest
    sub = place_ref[1]
    units = parts[0].shape[0]
    slot = pl.program_id(0)

    @pl.when(slot == 0)
    def _():
        for b in range(plan.subs):
            for k in range(plan.subs):

                @pl.when(jnp.bitwise_xor(sub, k) == b)
                def _():
                    at = slice(b * units, (b + 1) * units)
                    if k == 3 and blocks == 5:
                        inside = jnp.logical_or(sub == 1, sub == 2)

                        @pl.when(inside)
                        def _():
                            act_ref[at] = parts[3][...]

                        @pl.when(jnp.logical_not(inside))
                        def _():
                            act_ref[at] = parts[4][...]
                    else:
                        act_ref[at] = parts[k][...]

    ep = place_ref[0]

    def routed():
        metas = []
        for c in range(arrays // 2):
            pair = [metas_in[2 * c + h][...].astype(F32) for h in range(2)]
            metas.append(jnp.concatenate(pair, axis=0))
        return route(metas, plan, ep, sub)

    out = dot(weight_ref[0], act_ref[...], ((1,), (0,)))

    @pl.when(slot == 0)
    def _():
        sum_ref[...] = out.astype(BF16)

    @pl.when(slot > 0)
    def _():
        _columns, bounds = routed()
        masks = slot_masks(bounds, plan)
        mine = masks[0]
        for s in range(1, plan.slots):
            mine = jnp.where(slot == s, masks[s], mine)
        sum_ref[...] = jnp.where(mine > 0.0, out.astype(BF16), sum_ref[...])

    @pl.when(slot == plan.slots - 1)
    def _():
        columns, _bounds = routed()
        done = sum_ref[...]
        for c, places in enumerate(columns):
            mix = None
            for place, weight in places:
                part = jnp.where(rows_of(place, plan), weight, 0.0)
                mix = part if mix is None else mix + part
            high = mix.astype(BF16)
            low = (mix - high.astype(F32)).astype(BF16)
            total = dot(high, done, ((1,), (1,))) + dot(low, done, ((1,), (1,)))
            half = total.shape[0] // 2
            for h, ref in enumerate((keep_ref, send_ref)):
                value = total[h * half : (h + 1) * half]
                if before and c < befores[h].shape[0]:
                    value = value + befores[h][c].astype(F32)
                ref[c] = value.astype(BF16)


def outer(plan, place, tokens, parts, befores, weights):
    slots, columns_out, width = weights.shape
    arrays, blocks = len(tokens), len(parts)
    half = tokens[0].shape[0]
    last = tokens[0].shape[1] // LANES - 1
    result = jax.ShapeDtypeStruct((arrays // 2, half, columns_out), BF16)
    return pl.pallas_call(
        functools.partial(outer_kernel, plan, arrays, len(befores), blocks),
        grid=(slots,),
        in_specs=[pl.BlockSpec(memory_space=pltpu.SMEM)]
        + [pl.BlockSpec((half, LANES), lambda i: (0, last)) for t in tokens]
        + [pl.BlockSpec(p.shape, lambda i: (0, 0)) for p in parts]
        + [pl.BlockSpec(b.shape, lambda i: (0, 0, 0)) for b in befores]
        + [pl.BlockSpec((1, columns_out, width), lambda i: (i, 0, 0))],
        out_specs=[pl.BlockSpec(result.shape, lambda i: (0, 0, 0))] * 2,
        out_shape=[result, result],
        scratch_shapes=[
            pltpu.VMEM((width, plan.rows), BF16),
            pltpu.VMEM((columns_out, plan.rows), BF16),
        ],
        compiler_params=params(),
        cost_estimate=HINT,
    )(place, *tokens, *parts, *befores, weights)


def finish_kernel(subs, columns, place_ref, *refs):
    out_ref = refs[-1]
    sub = place_ref[1]
    width = refs[0].shape[1]
    steps, rows, _ = out_ref.shape
    sums = []
    for k in range(subs):
        value = refs[k * columns][...].astype(F32)
        for j in range(1, columns):
            value = value + refs[k * columns + j][...].astype(F32)
        sums.append(value)
    for b in range(subs):
        value = sums[0]
        for k in range(1, subs):
            value = jnp.where(jnp.bitwise_xor(sub, k) == b, sums[k], value)
        value = value.astype(BF16)
        for s in range(steps):
            out_ref[s, :, b * width : (b + 1) * width] = value[s * rows : (s + 1) * rows]


def finish(place, parts, steps):
    subs, columns = len(parts), len(parts[0])
    rows, width = parts[0][0].shape
    return pl.pallas_call(
        functools.partial(finish_kernel, subs, columns),
        grid=(1,),
        in_specs=[pl.BlockSpec(memory_space=pltpu.SMEM)]
        + [pl.BlockSpec((rows, width), lambda i: (0, 0))] * (subs * columns),
        out_specs=pl.BlockSpec((steps, rows // steps, width * subs), lambda i: (0, 0, 0)),
        out_shape=jax.ShapeDtypeStruct((steps, rows // steps, width * subs), BF16),
        compiler_params=params(),
    )(place, *[p for several in parts for p in several])


def swap(x, axis, offset, count):
    return lax.ppermute(x, axis, [(i, i ^ offset) for i in range(count)])


def gather_direct(x, subs):
    if subs != 4:
        return [x] + [swap(x, "sub", k, subs) for k in range(1, subs)]
    one = swap(x, "sub", 1, subs)
    two = swap(x, "sub", 2, subs)
    middle = lax.ppermute(x, "sub", [(1, 2), (2, 1)])
    return [x, one, two, middle]


def gather_ends(parts):
    if len(parts) != 4:
        return parts
    return parts + [lax.ppermute(parts[2], "sub", [(2, 3), (1, 0)])]


def gather_sub(x, subs):
    parts = gather_direct(x, subs)
    return gather_ends(parts) if subs == 4 else parts


def add(a, b):
    return (a.astype(F32) + b.astype(F32)).astype(BF16)


def local(
    tokens, norm_gain, copy_ids, gate_scores, inner_codes, inner_scales, down_codes, down_scales
):
    eps, subs, groups = lax.axis_size("ep"), lax.axis_size("sub"), lax.axis_size("grp")
    slots = inner_codes.shape[0]
    steps, rows, top = copy_ids.shape
    units = inner_codes.shape[3]
    experts = eps * slots
    capacity = (3 * rows * top + 2 * experts - 1) // (2 * experts)
    columns = eps // 2
    place = jnp.stack([lax.axis_index("ep"), lax.axis_index("sub")]).astype(jnp.int32)
    group = steps * rows

    packed = pack(tokens, norm_gain, copy_ids, gate_scores)
    near = [packed] + [swap(packed, "sub", k, subs) for k in range(1, subs)]
    codes = jnp.transpose(inner_codes, (0, 2, 3, 1)).reshape(slots * 2, units, -1)
    scales = jnp.transpose(inner_scales, (0, 2, 3, 1)).reshape(slots * 2, units, -1)
    inner_weights = dequant(codes, scales, packed).reshape(slots, 2, units, -1)
    outer_codes = jnp.transpose(down_codes, (0, 2, 1))
    outer_scales = jnp.transpose(down_scales, (0, 2, 1))
    own = join(near, inner_weights)
    other = swap(own, "ep", 1, eps)
    across = [swap(own, "ep", 2 * j, eps) for j in range(1, columns)]

    capacity_rows = group * subs * 2 // rows * slots * capacity

    def plan(first, count, holds):
        return Plan(first, count, holds, slots, subs, group, top, eps)

    if columns == 2 and subs == 4 and capacity_rows % 384 == 0:
        most = 2 * capacity_rows
        first = capacity_rows // 384 * 256
        second = capacity_rows
        last = most - first - second
        holds = (first,)
        plan0, plan1 = plan(0, first, holds), plan(first, second, holds)
        plan2 = plan(first + second, last, holds)
        act0, mark = inner(plan0, place, [own, other], inner_weights, [own])
        parts0 = gather_direct(act0, subs)
        outer_weights = dequant(outer_codes, outer_scales, mark)
        moved = join(across, mark)
        everything = [own, other, moved, swap(moved, "ep", 1, eps)]
        act1, longest = inner(
            plan1, place, everything, inner_weights, [parts0[1], parts0[3], outer_weights]
        )
        parts0 = gather_ends(parts0)
        sums = outer(plan0, place, [own, other], parts0, [], outer_weights)
        parts1 = gather_direct(act1, subs)
        passed = [parts1[0], parts1[1], join(parts1[2:3], sums[0]), parts1[3]]
        parts1 = parts1 + gather_ends(passed)[4:]
        for shift in range(1, groups):
            moved = lax.ppermute(
                longest, "grp", [(i, (i + shift) % groups) for i in range(groups)]
            )
            longest = jnp.maximum(longest, moved)
        sums = outer(plan1, place, everything, parts1, sums, outer_weights)

        def more(kept, sent):
            act, _ = inner(plan2, place, everything, inner_weights, [kept])
            return tuple(
                outer(
                    plan2, place, everything, gather_sub(act, subs), [kept, sent], outer_weights
                )
            )

        keep, send = lax.cond(
            longest[0, 0] > float(first + second), more, lambda a, b: (a, b), *sums
        )
    else:
        count = -(-capacity_rows // LANES) * LANES
        each = plan(0, count, ())
        outer_weights = dequant(outer_codes, outer_scales, own)
        keeps, sends = [], []
        held = [[own, other]] + [[a, swap(a, "ep", 1, eps)] for a in across]
        for pair in held:
            act, _ = inner(each, place, pair, inner_weights, [own])
            kept, sent = outer(each, place, pair, gather_sub(act, subs), [], outer_weights)
            keeps.append(kept)
            sends.append(sent)
        keep, send = jnp.concatenate(keeps, axis=0), jnp.concatenate(sends, axis=0)

    chip = add(keep, swap(send, "ep", 1, eps))
    chip = chip.reshape(columns, subs, group, -1)
    arrived = []
    for k in range(subs):
        arrived.append([])
        for j in range(columns):
            pairs = []
            for e in range(eps):
                for z in range(subs):
                    pairs.append((e * subs + z, (e ^ (2 * j)) * subs + (z ^ k)))
            block = chip[j, k]
            arrived[-1].append(lax.ppermute(block, ("ep", "sub"), pairs) if j + k else block)
    return finish(place, arrived, steps)


def solution(mesh):
    return jax.shard_map(
        local,
        mesh=mesh,
        in_specs=(
            P(None, ("grp", "ep", "sub"), None),
            P(),
            P(None, ("grp", "ep", "sub"), None),
            P(None, ("grp", "ep", "sub"), None),
            P("ep", None, None, "sub"),
            P("ep", None, None, "sub"),
            P("ep", None, "sub"),
            P("ep", None, "sub"),
        ),
        out_specs=P(None, ("grp", "ep", "sub"), None),
        check_vma=False,
    )
```

```python
import functools

import jax
import jax.numpy as jnp
from jax import lax
from jax.experimental import pallas as pl
from jax.experimental.pallas import tpu as pltpu
from jax.sharding import PartitionSpec as P

epsilon = 1e-05
swish_beta = 1.702
META = 64
LANES = 128
VMEM_LIMIT = 24 * 1024 * 1024
HINT = pl.CostEstimate(flops=1024, bytes_accessed=1024, transcendentals=0)
F32 = jnp.float32
BF16 = jnp.bfloat16


def params():
    return pltpu.CompilerParams(vmem_limit_bytes=VMEM_LIMIT)


def dot(a, b, contract):
    return lax.dot_general(a, b, (contract, ((), ())), preferred_element_type=F32)


def pack_kernel(tokens_ref, gain_ref, ids_ref, scores_ref, out_ref):
    steps, rows, width = tokens_ref.shape
    top = ids_ref.shape[1]
    gain = gain_ref[...].reshape(1, width)
    eye = (
        lax.broadcasted_iota(jnp.int32, (rows, rows), 0)
        == lax.broadcasted_iota(jnp.int32, (rows, rows), 1)
    ).astype(F32)

    def column(row):
        return jnp.sum(eye * row, axis=1, keepdims=True)

    for s in range(steps):
        values = tokens_ref[s].astype(F32)
        mean = jnp.mean(values * values, axis=-1, keepdims=True)
        normed = (values * lax.rsqrt(mean + epsilon) * gain).astype(BF16)
        at = slice(s * rows, (s + 1) * rows)
        out_ref[at, :width] = normed
        scores = scores_ref[s]
        weights = scores / jnp.sum(scores, axis=0, keepdims=True)
        high = weights.astype(BF16)
        rest = weights - high.astype(F32)
        middle = rest.astype(BF16)
        low = (rest - middle.astype(F32)).astype(BF16)
        lane = lax.broadcasted_iota(jnp.int32, (rows, META), 1)
        meta = jnp.zeros((rows, META), F32)
        parts = (ids_ref[s].astype(F32), high.astype(F32), middle.astype(F32), low.astype(F32))
        for p, part in enumerate(parts):
            for k in range(top):
                meta = jnp.where(lane == p * top + k, column(part[k : k + 1]), meta)
        out_ref[at, width:] = meta.astype(BF16)


def pack(tokens, gain, ids, scores):
    steps, rows, width = tokens.shape
    return pl.pallas_call(
        pack_kernel,
        out_shape=jax.ShapeDtypeStruct((steps * rows, width + META), BF16),
        compiler_params=params(),
    )(
        tokens, gain, jnp.transpose(ids, (0, 2, 1)), jnp.transpose(scores, (0, 2, 1))
    )


def dequant_kernel(codes_ref, scales_ref, _after_ref, out_ref, mark_ref):
    width = codes_ref.shape[2]
    scales = scales_ref[0]
    blocks = scales.shape[1]
    chunk = 256
    for at in range(0, width, chunk):
        end = min(at + chunk, width)
        column = lax.broadcasted_iota(jnp.int32, (blocks, end - at), 1) + at
        block = lax.broadcasted_iota(jnp.int32, (blocks, end - at), 0)
        first = block * (width // blocks)
        inside = jnp.logical_and(column >= first, column < first + width // blocks)
        wide = dot(scales, inside.astype(F32).astype(BF16), ((1,), (0,)))
        out_ref[0, :, at:end] = (codes_ref[0, :, at:end].astype(F32) * wide).astype(BF16)
    mark_ref[...] = jnp.zeros_like(mark_ref)


def dequant(codes, scales, after):
    count, rows, width = codes.shape
    blocks = scales.shape[2]
    return pl.pallas_call(
        dequant_kernel,
        grid=(count,),
        in_specs=[
            pl.BlockSpec((1, rows, width), lambda i: (i, 0, 0)),
            pl.BlockSpec((1, rows, blocks), lambda i: (i, 0, 0)),
            pl.BlockSpec(memory_space=pl.ANY),
        ],
        out_specs=[
            pl.BlockSpec((1, rows, width), lambda i: (i, 0, 0)),
            pl.BlockSpec((8, LANES), lambda i: (0, 0)),
        ],
        out_shape=[
            jax.ShapeDtypeStruct(codes.shape, BF16),
            jax.ShapeDtypeStruct((8, LANES), F32),
        ],
        compiler_params=params(),
        cost_estimate=HINT,
    )(pltpu.with_memory_space_constraint(codes, pltpu.HBM), scales, after)


def join_kernel(count, pieces, *refs):
    outs = refs[-pieces:]
    rows, size = refs[0].shape[0], outs[0].shape[0]
    for p, out_ref in enumerate(outs):
        if size >= rows:
            for k in range(size // rows):
                out_ref[k * rows : (k + 1) * rows] = refs[p * (size // rows) + k][...]
        else:
            at = p * size % rows
            out_ref[...] = refs[p * size // rows][at : at + size]


def join(parts, after, pieces=1):
    rows, width = parts[0].shape
    count = len(parts)
    size = count * rows // pieces
    return pl.pallas_call(
        functools.partial(join_kernel, count, pieces),
        grid=(1,),
        in_specs=[pl.BlockSpec((rows, width), lambda i: (0, 0))] * count
        + [pl.BlockSpec(memory_space=pl.ANY)] * len(after),
        out_specs=[pl.BlockSpec((size, width), lambda i: (0, 0))] * pieces,
        out_shape=[jax.ShapeDtypeStruct((size, width), BF16)] * pieces,
        compiler_params=params(),
        cost_estimate=HINT,
    )(*parts, *after)


class Plan:
    def __init__(self, first, rows, holds, slots, subs, group, top, eps):
        self.first, self.rows = first, rows
        self.holds = holds
        self.slots, self.subs, self.group, self.top, self.eps = slots, subs, group, top, eps


def chosen(meta, expert, top):
    named = jnp.zeros((meta.shape[0], 1), F32)
    weight = jnp.zeros((meta.shape[0], 1), F32)
    for k in range(top):
        at = meta.shape[1] - META + k
        hit = (meta[:, at : at + 1] == expert).astype(F32)
        total = (
            meta[:, at + top : at + top + 1]
            + meta[:, at + 2 * top : at + 2 * top + 1]
            + meta[:, at + 3 * top : at + 3 * top + 1]
        )
        named = named + hit
        weight = weight + hit * total
    return named, weight


def order_mask(count, plan, sub):
    def key(dim):
        t = lax.broadcasted_iota(jnp.int32, (count, count), dim)
        block = lax.rem(lax.div(t, plan.group), plan.subs)
        return t + (jnp.bitwise_xor(block, sub) - block) * plan.group

    return (key(1) < key(0)).astype(BF16)


def route(metas, plan, ep, sub):
    count = metas[0].shape[0]
    earlier = order_mask(count, plan, sub)
    lane = lax.broadcasted_iota(jnp.int32, (count, LANES), 1)
    start = jnp.zeros((1, 1), F32)
    result = []
    bounds = []
    for column, meta in enumerate(metas):
        if column:
            start = jnp.maximum(start, float(plan.holds[column - 1]))
        found = []
        flags = jnp.zeros((count, LANES), F32)
        for slot in range(plan.slots):
            named, weight = chosen(meta, (ep * plan.slots + slot).astype(F32), plan.top)
            found.append((named, weight))
            flags = jnp.where(lane == slot, named, flags)
        prefix = dot(earlier, flags.astype(BF16), ((1,), (0,)))
        places = []
        for slot, (named, weight) in enumerate(found):
            place = jnp.where(named > 0.0, prefix[:, slot : slot + 1] + start, -1.0)
            places.append((place, weight))
            end = start + jnp.sum(named, axis=0, keepdims=True)
            bounds.append((slot, start, end))
            start = end
        result.append(places)
    return result, bounds


def slot_masks(bounds, plan):
    row = lax.broadcasted_iota(jnp.int32, (1, plan.rows), 1).astype(F32) + float(plan.first)
    masks = []
    for slot in range(plan.slots):
        mask = jnp.zeros((1, plan.rows), F32)
        for which, start, end in bounds:
            if which == slot:
                mask = mask + jnp.logical_and(row >= start, row < end).astype(F32)
        masks.append(mask)
    return masks


def rows_of(places, plan):
    return (
        lax.broadcasted_iota(jnp.int32, (places.shape[0], plan.rows), 1).astype(F32)
        + float(plan.first)
        == places
    )


def metas_of(layout, refs, width):
    metas, at = [], 0
    for count in layout:
        several = [ref[:, width:].astype(F32) for ref in refs[at : at + count]]
        metas.append(jnp.concatenate(several, axis=0))
        at += count
    return metas


def rows_kernel(plan, layout, place_ref, *refs):
    arrays = sum(layout)
    tokens = refs[:arrays]
    meta_ref, most_ref = refs[arrays : arrays + 2]
    outs = refs[arrays + 2 :]
    width = outs[0].shape[0]
    ep, sub = place_ref[0], place_ref[1]
    metas = metas_of(layout, tokens, width)
    at = 0
    for ref in tokens:
        meta_ref[at : at + ref.shape[0]] = ref[:, width - META :]
        at += ref.shape[0]
    columns, bounds = route(metas, plan, ep, sub)
    begin = 0
    for part, mask_ref in enumerate(outs[1::2]):
        mask_ref[...] = jnp.zeros_like(mask_ref)
        size = mask_ref.shape[1]
        for slot, mask in enumerate(slot_masks(bounds, plan)):
            mask_ref[slot : slot + 1] = mask[:, begin : begin + size]
        begin += size
    hots = []
    for places in columns:
        hot = None
        for place, _weight in places:
            hit = rows_of(place, plan).astype(F32)
            hot = hit if hot is None else hot + hit
        hots.append(hot.astype(BF16))
    hot = jnp.concatenate(hots, axis=0) if len(hots) > 1 else hots[0]
    chunk = 256
    for at in range(0, width, chunk):
        end = min(at + chunk, width)
        several = [ref[:, at:end] for ref in tokens]
        total = dot(jnp.concatenate(several, axis=0), hot, ((0,), (0,)))
        begin = 0
        for rows_ref in outs[::2]:
            rows_ref[at:end] = total[:, begin : begin + rows_ref.shape[1]].astype(BF16)
            begin += rows_ref.shape[1]
    lane = lax.broadcasted_iota(jnp.int32, (metas[0].shape[0], LANES), 1).astype(F32)
    owner = lax.div(lax.broadcasted_iota(jnp.int32, (1, LANES), 1), plan.slots)
    start = [jnp.zeros((1, 1), F32)] * plan.eps
    for column, meta in enumerate(metas):
        flags = jnp.zeros((meta.shape[0], LANES), F32)
        for k in range(plan.top):
            flags = flags + (meta[:, k : k + 1] == lane).astype(F32)
        counts = jnp.sum(flags, axis=0, keepdims=True)
        for e in range(plan.eps):
            if column:
                start[e] = jnp.maximum(start[e], float(plan.holds[column - 1]))
            start[e] = start[e] + jnp.sum(
                jnp.where(owner == e, counts, 0.0), axis=1, keepdims=True
            )
    most_ref[...] = jnp.broadcast_to(functools.reduce(jnp.maximum, start), most_ref.shape)


def rows_in(plan, place, held, split=None):
    layout = tuple(len(arrays) for arrays in held)
    tokens = [t for arrays in held for t in arrays]
    width = tokens[0].shape[1] - META
    total = sum(t.shape[0] for t in tokens)
    split = split or (plan.rows,)
    specs = [pl.BlockSpec((total, LANES), lambda i: (0, 0)), pl.BlockSpec((8, LANES), lambda i: (0, 0))]
    shapes = [
        jax.ShapeDtypeStruct((total, LANES), BF16),
        jax.ShapeDtypeStruct((8, LANES), F32),
    ]
    for size in split:
        specs.append(pl.BlockSpec((width, size), lambda i: (0, 0)))
        specs.append(pl.BlockSpec((8, size), lambda i: (0, 0)))
        shapes.append(jax.ShapeDtypeStruct((width, size), BF16))
        shapes.append(jax.ShapeDtypeStruct((8, size), F32))
    return pl.pallas_call(
        functools.partial(rows_kernel, plan, layout),
        grid=(1,),
        in_specs=[pl.BlockSpec(memory_space=pltpu.SMEM)]
        + [pl.BlockSpec(t.shape, lambda i: (0, 0)) for t in tokens],
        out_specs=specs,
        out_shape=shapes,
        compiler_params=params(),
        cost_estimate=HINT,
    )(place, *tokens)


def inner_kernel(plan, rows_ref, mask_ref, weight_ref, *refs):
    act_ref, mark_ref = refs[-2:]
    gating = upward = None
    for slot in range(plan.slots):
        gate = dot(weight_ref[slot, 0], rows_ref[...], ((1,), (0,)))
        up = dot(weight_ref[slot, 1], rows_ref[...], ((1,), (0,)))
        if slot == 0:
            gating, upward = gate, up
        else:
            mine = mask_ref[slot : slot + 1] > 0.0
            gating = jnp.where(mine, gate, gating)
            upward = jnp.where(mine, up, upward)
    act_ref[...] = (gating * jax.nn.sigmoid(swish_beta * gating) * (upward + 1.0)).astype(BF16)
    mark_ref[...] = jnp.zeros_like(mark_ref)


def piece(total):
    for size in (240, 120, 72, 40, 24, 16, 8):
        if total % size == 0:
            return size
    return total


def inner(plan, rows, mask, weights, after):
    slots, _two, units, width = weights.shape
    block = piece(units)
    return pl.pallas_call(
        functools.partial(inner_kernel, plan),
        grid=(units // block,),
        in_specs=[
            pl.BlockSpec(rows.shape, lambda i: (0, 0)),
            pl.BlockSpec(mask.shape, lambda i: (0, 0)),
            pl.BlockSpec((slots, 2, block, width), lambda i: (0, 0, i, 0)),
        ]
        + [pl.BlockSpec(memory_space=pl.ANY)] * len(after),
        out_specs=[
            pl.BlockSpec((block, rows.shape[1]), lambda i: (i, 0)),
            pl.BlockSpec((8, LANES), lambda i: (0, 0)),
        ],
        out_shape=[
            jax.ShapeDtypeStruct((units, rows.shape[1]), BF16),
            jax.ShapeDtypeStruct((8, LANES), F32),
        ],
        compiler_params=params(),
        cost_estimate=HINT,
    )(rows, mask, weights, *after)


def outer_kernel(plan, before, blocks, ends, place_ref, meta_ref, *refs):
    arrays = 0
    parts = refs[arrays : arrays + blocks]
    befores = refs[arrays + blocks : arrays + blocks + before]
    weight_ref = refs[arrays + blocks + before]
    keep_ref, send_ref, act_ref, sum_ref = refs[-4:]
    sub = place_ref[1]
    units = parts[0].shape[0]
    slot = pl.program_id(0)

    @pl.when(slot == 0)
    def _():
        for b in range(plan.subs):
            for k in range(plan.subs):

                @pl.when(jnp.bitwise_xor(sub, k) == b)
                def _():
                    at = slice(b * units, (b + 1) * units)
                    if k == 3 and ends:
                        inside = jnp.logical_or(sub == 1, sub == 2)

                        @pl.when(inside)
                        def _():
                            act_ref[at] = parts[3][...]

                        @pl.when(jnp.logical_not(inside))
                        def _():
                            act_ref[at] = parts[4][...]
                    else:
                        act_ref[at] = parts[k][...]

    ep = place_ref[0]

    def routed():
        count = 2 * keep_ref.shape[1]
        metas = []
        for c in range(keep_ref.shape[0]):
            metas.append(meta_ref[c * count : (c + 1) * count].astype(F32))
        return route(metas, plan, ep, sub)

    out = dot(weight_ref[0], act_ref[...], ((1,), (0,)))

    @pl.when(slot == 0)
    def _():
        sum_ref[...] = out.astype(BF16)

    @pl.when(slot > 0)
    def _():
        _columns, bounds = routed()
        masks = slot_masks(bounds, plan)
        mine = masks[0]
        for s in range(1, plan.slots):
            mine = jnp.where(slot == s, masks[s], mine)
        sum_ref[...] = jnp.where(mine > 0.0, out.astype(BF16), sum_ref[...])

    @pl.when(slot == plan.slots - 1)
    def _():
        columns, _bounds = routed()
        done = sum_ref[...]
        for c, places in enumerate(columns):
            mix = None
            for place, weight in places:
                part = jnp.where(rows_of(place, plan), weight, 0.0)
                mix = part if mix is None else mix + part
            high = mix.astype(BF16)
            low = (mix - high.astype(F32)).astype(BF16)
            total = dot(high, done, ((1,), (1,))) + dot(low, done, ((1,), (1,)))
            half = total.shape[0] // 2
            for h, ref in enumerate((keep_ref, send_ref)):
                value = total[h * half : (h + 1) * half]
                if before and c < befores[h].shape[0]:
                    value = value + befores[h][c].astype(F32)
                ref[c] = value.astype(BF16)


def outer(plan, place, meta, parts, befores, weights, after=()):
    slots, columns_out, width = weights.shape
    blocks = len(parts)
    half = plan.group * plan.subs
    result = jax.ShapeDtypeStruct((meta.shape[0] // (2 * half), half, columns_out), BF16)
    return pl.pallas_call(
        functools.partial(outer_kernel, plan, len(befores), blocks, blocks > plan.subs),
        grid=(slots,),
        in_specs=[pl.BlockSpec(memory_space=pltpu.SMEM)]
        + [pl.BlockSpec(meta.shape, lambda i: (0, 0))]
        + [pl.BlockSpec(p.shape, lambda i: (0, 0)) for p in parts]
        + [pl.BlockSpec(b.shape, lambda i: (0, 0, 0)) for b in befores]
        + [pl.BlockSpec((1, columns_out, width), lambda i: (i, 0, 0))]
        + [pl.BlockSpec(memory_space=pl.ANY)] * len(after),
        out_specs=[pl.BlockSpec(result.shape, lambda i: (0, 0, 0))] * 2,
        out_shape=[result, result],
        scratch_shapes=[
            pltpu.VMEM((width, plan.rows), BF16),
            pltpu.VMEM((columns_out, plan.rows), BF16),
        ],
        compiler_params=params(),
        cost_estimate=HINT,
    )(place, meta, *parts, *befores, weights, *after)


def finish_kernel(subs, columns, place_ref, *refs):
    out_ref = refs[-1]
    sub = place_ref[1]
    width = refs[0].shape[1]
    steps, rows, _ = out_ref.shape
    sums = []
    for k in range(subs):
        value = refs[k * columns][...].astype(F32)
        for j in range(1, columns):
            value = value + refs[k * columns + j][...].astype(F32)
        sums.append(value)
    for b in range(subs):
        value = sums[0]
        for k in range(1, subs):
            value = jnp.where(jnp.bitwise_xor(sub, k) == b, sums[k], value)
        value = value.astype(BF16)
        for s in range(steps):
            out_ref[s, :, b * width : (b + 1) * width] = value[s * rows : (s + 1) * rows]


def finish(place, parts, steps):
    subs, columns = len(parts), len(parts[0])
    rows, width = parts[0][0].shape
    return pl.pallas_call(
        functools.partial(finish_kernel, subs, columns),
        grid=(1,),
        in_specs=[pl.BlockSpec(memory_space=pltpu.SMEM)]
        + [pl.BlockSpec((rows, width), lambda i: (0, 0))] * (subs * columns),
        out_specs=pl.BlockSpec((steps, rows // steps, width * subs), lambda i: (0, 0, 0)),
        out_shape=jax.ShapeDtypeStruct((steps, rows // steps, width * subs), BF16),
        compiler_params=params(),
    )(place, *[p for several in parts for p in several])


def swap(x, axis, offset, count):
    return lax.ppermute(x, axis, [(i, i ^ offset) for i in range(count)])


def gather(x, subs):
    return [x] + [swap(x, "sub", k, subs) for k in range(1, subs)]


def gather_line(x):
    one = swap(x, "sub", 1, 4)
    two = swap(x, "sub", 2, 4)
    return [x, one, two, lax.ppermute(x, "sub", [(1, 2), (2, 1)])]


def gather_ends(two):
    return lax.ppermute(two, "sub", [(2, 3), (1, 0)])


def add(a, b):
    return (a.astype(F32) + b.astype(F32)).astype(BF16)


def local(
    tokens, norm_gain, copy_ids, gate_scores, inner_codes, inner_scales, down_codes, down_scales
):
    eps, subs, groups = lax.axis_size("ep"), lax.axis_size("sub"), lax.axis_size("grp")
    slots = inner_codes.shape[0]
    steps, rows, top = copy_ids.shape
    units = inner_codes.shape[3]
    experts = eps * slots
    capacity = (3 * rows * top + 2 * experts - 1) // (2 * experts)
    columns = eps // 2
    place = jnp.stack([lax.axis_index("ep"), lax.axis_index("sub")]).astype(jnp.int32)
    group = steps * rows

    packed = pack(tokens, norm_gain, copy_ids, gate_scores)
    near = [packed] + [swap(packed, "sub", k, subs) for k in range(1, subs)]
    codes = jnp.transpose(inner_codes, (0, 2, 3, 1)).reshape(slots * 2, units, -1)
    scales = jnp.transpose(inner_scales, (0, 2, 3, 1)).reshape(slots * 2, units, -1)
    inner_weights, mark = dequant(codes, scales, packed)
    inner_weights = inner_weights.reshape(slots, 2, units, -1)
    outer_codes = jnp.transpose(down_codes, (0, 2, 1))
    outer_scales = jnp.transpose(down_scales, (0, 2, 1))
    own = join(near, [mark])[0]
    other = swap(own, "ep", 1, eps)

    capacity_rows = group * subs * 2 // rows * slots * capacity

    def plan(first, count, holds):
        return Plan(first, count, holds, slots, subs, group, top, eps)

    if columns == 2 and subs == 4 and capacity_rows % 384 == 0:
        most = 2 * capacity_rows
        first = capacity_rows // 384 * 256
        second = capacity_rows
        last = most - first - second
        holds = (first,)
        plan0, plan1 = plan(0, first, holds), plan(first, second, holds)
        plan2 = plan(first + second, last, holds)
        pair = [own, other]
        meta0, _, rows0, mask0 = rows_in(plan0, place, [pair])
        act0, mark = inner(plan0, rows0, mask0, inner_weights, [])
        parts0 = gather_line(act0)
        moved = join([swap(n, "ep", 2, eps) for n in near], [mark], 4)
        everything = [pair, list(moved) + [swap(m, "ep", 1, eps) for m in moved]]
        meta1, longest, rows1, mask1, rows2, mask2 = rows_in(
            plan(first, second + last, holds), place, everything, (second, last)
        )
        act1, _ = inner(plan1, rows1, mask1, inner_weights, [])
        act1 = join([act1], parts0[1:])[0]
        parts0.append(gather_ends(parts0[2]))
        parts1 = gather(act1, subs)
        outer_weights, _ = dequant(outer_codes, outer_scales, parts1[1])
        sums = outer(plan0, place, meta0, parts0, [], outer_weights, parts1[1:3])
        for shift in range(1, groups):
            moved = lax.ppermute(
                longest, "grp", [(i, (i + shift) % groups) for i in range(groups)]
            )
            longest = jnp.maximum(longest, moved)
        sums = outer(plan1, place, meta1, parts1, sums, outer_weights)

        def more(kept, sent):
            act, _ = inner(plan2, rows2, mask2, inner_weights, [kept])
            parts = gather(act, subs)
            return tuple(outer(plan2, place, meta1, parts, [kept, sent], outer_weights))

        keep, send = lax.cond(
            longest[0, 0] > float(first + second), more, lambda a, b: (a, b), *sums
        )
    else:
        count = -(-capacity_rows // LANES) * LANES
        each = plan(0, count, ())
        outer_weights, _ = dequant(outer_codes, outer_scales, own)
        keeps, sends = [], []
        across = [swap(own, "ep", 2 * j, eps) for j in range(1, columns)]
        held = [[own, other]] + [[a, swap(a, "ep", 1, eps)] for a in across]
        for pair in held:
            meta, _, rows_here, mask = rows_in(each, place, [pair])
            act, _ = inner(each, rows_here, mask, inner_weights, [])
            kept, sent = outer(each, place, meta, gather(act, subs), [], outer_weights)
            keeps.append(kept)
            sends.append(sent)
        keep, send = jnp.concatenate(keeps, axis=0), jnp.concatenate(sends, axis=0)

    chip = add(keep, swap(send, "ep", 1, eps))
    chip = chip.reshape(columns, subs, group, -1)
    arrived = []
    for k in range(subs):
        arrived.append([])
        for j in range(columns):
            pairs = []
            for e in range(eps):
                for z in range(subs):
                    pairs.append((e * subs + z, (e ^ (2 * j)) * subs + (z ^ k)))
            block = chip[j, k]
            arrived[-1].append(lax.ppermute(block, ("ep", "sub"), pairs) if j + k else block)
    return finish(place, arrived, steps)


def solution(mesh):
    return jax.shard_map(
        local,
        mesh=mesh,
        in_specs=(
            P(None, ("grp", "ep", "sub"), None),
            P(),
            P(None, ("grp", "ep", "sub"), None),
            P(None, ("grp", "ep", "sub"), None),
            P("ep", None, None, "sub"),
            P("ep", None, None, "sub"),
            P("ep", None, "sub"),
            P("ep", None, "sub"),
        ),
        out_specs=P(None, ("grp", "ep", "sub"), None),
        check_vma=False,
    )
```

```python
import functools

import jax
import jax.numpy as jnp
from jax import lax
from jax.experimental import pallas as pl
from jax.experimental.pallas import tpu as pltpu
from jax.sharding import PartitionSpec as P

epsilon = 1e-05
swish_beta = 1.702
META = 64
LANES = 128
VMEM_LIMIT = 24 * 1024 * 1024
HINT = pl.CostEstimate(flops=1024, bytes_accessed=1024, transcendentals=0)
F32 = jnp.float32
BF16 = jnp.bfloat16


def params():
    return pltpu.CompilerParams(vmem_limit_bytes=VMEM_LIMIT)


def in_hbm(x):
    return pltpu.with_memory_space_constraint(x, pltpu.HBM)


def dot(a, b, contract):
    return lax.dot_general(a, b, (contract, ((), ())), preferred_element_type=F32)


def pack_kernel(tokens_ref, gain_ref, ids_ref, scores_ref, out_ref):
    steps, rows, width = tokens_ref.shape
    top = ids_ref.shape[1]
    gain = gain_ref[...].reshape(1, width)
    eye = (
        lax.broadcasted_iota(jnp.int32, (rows, rows), 0)
        == lax.broadcasted_iota(jnp.int32, (rows, rows), 1)
    ).astype(F32)

    def column(row):
        return jnp.sum(eye * row, axis=1, keepdims=True)

    for s in range(steps):
        values = tokens_ref[s].astype(F32)
        mean = jnp.mean(values * values, axis=-1, keepdims=True)
        normed = (values * lax.rsqrt(mean + epsilon) * gain).astype(BF16)
        at = slice(s * rows, (s + 1) * rows)
        out_ref[at, :width] = normed
        scores = scores_ref[s]
        weights = scores / jnp.sum(scores, axis=0, keepdims=True)
        high = weights.astype(BF16)
        rest = weights - high.astype(F32)
        middle = rest.astype(BF16)
        low = (rest - middle.astype(F32)).astype(BF16)
        lane = lax.broadcasted_iota(jnp.int32, (rows, META), 1)
        meta = jnp.zeros((rows, META), F32)
        parts = (ids_ref[s].astype(F32), high.astype(F32), middle.astype(F32), low.astype(F32))
        for p, part in enumerate(parts):
            for k in range(top):
                meta = jnp.where(lane == p * top + k, column(part[k : k + 1]), meta)
        out_ref[at, width:] = meta.astype(BF16)


def pack(tokens, gain, ids, scores):
    steps, rows, width = tokens.shape
    return pl.pallas_call(
        pack_kernel,
        out_shape=jax.ShapeDtypeStruct((steps * rows, width + META), BF16),
        compiler_params=params(),
    )(
        in_hbm(tokens),
        in_hbm(gain),
        in_hbm(jnp.transpose(ids, (0, 2, 1))),
        in_hbm(jnp.transpose(scores, (0, 2, 1))),
    )


def dequant_kernel(codes_ref, scales_ref, _after_ref, out_ref, mark_ref):
    width = codes_ref.shape[2]
    scales = scales_ref[0]
    blocks = scales.shape[1]
    chunk = 256
    for at in range(0, width, chunk):
        end = min(at + chunk, width)
        column = lax.broadcasted_iota(jnp.int32, (blocks, end - at), 1) + at
        block = lax.broadcasted_iota(jnp.int32, (blocks, end - at), 0)
        first = block * (width // blocks)
        inside = jnp.logical_and(column >= first, column < first + width // blocks)
        wide = dot(scales, inside.astype(F32).astype(BF16), ((1,), (0,)))
        out_ref[0, :, at:end] = (codes_ref[0, :, at:end].astype(F32) * wide).astype(BF16)
    mark_ref[...] = jnp.zeros_like(mark_ref)


def dequant(codes, scales, after):
    count, rows, width = codes.shape
    blocks = scales.shape[2]
    return pl.pallas_call(
        dequant_kernel,
        grid=(count,),
        in_specs=[
            pl.BlockSpec((1, rows, width), lambda i: (i, 0, 0)),
            pl.BlockSpec((1, rows, blocks), lambda i: (i, 0, 0)),
            pl.BlockSpec(memory_space=pl.ANY),
        ],
        out_specs=[
            pl.BlockSpec((1, rows, width), lambda i: (i, 0, 0)),
            pl.BlockSpec((8, LANES), lambda i: (0, 0)),
        ],
        out_shape=[
            jax.ShapeDtypeStruct(codes.shape, BF16),
            jax.ShapeDtypeStruct((8, LANES), F32),
        ],
        compiler_params=params(),
        cost_estimate=HINT,
    )(in_hbm(codes), scales, after)


def join_kernel(count, pieces, *refs):
    outs = refs[-pieces:]
    rows, size = refs[0].shape[0], outs[0].shape[0]
    for p, out_ref in enumerate(outs):
        if size >= rows:
            for k in range(size // rows):
                out_ref[k * rows : (k + 1) * rows] = refs[p * (size // rows) + k][...]
        else:
            at = p * size % rows
            out_ref[...] = refs[p * size // rows][at : at + size]


def join(parts, after, pieces=1):
    rows, width = parts[0].shape
    count = len(parts)
    size = count * rows // pieces
    return pl.pallas_call(
        functools.partial(join_kernel, count, pieces),
        grid=(1,),
        in_specs=[pl.BlockSpec((rows, width), lambda i: (0, 0))] * count
        + [pl.BlockSpec(memory_space=pl.ANY)] * len(after),
        out_specs=[pl.BlockSpec((size, width), lambda i: (0, 0))] * pieces,
        out_shape=[jax.ShapeDtypeStruct((size, width), BF16)] * pieces,
        compiler_params=params(),
        cost_estimate=HINT,
    )(*parts, *after)


class Plan:
    def __init__(self, first, rows, holds, slots, subs, group, top, eps):
        self.first, self.rows = first, rows
        self.holds = holds
        self.slots, self.subs, self.group, self.top, self.eps = slots, subs, group, top, eps

    def part(self, begin, rows):
        return Plan(
            self.first + begin, rows, self.holds, self.slots, self.subs, self.group, self.top, self.eps
        )


def chosen(meta, expert, top):
    named = jnp.zeros((meta.shape[0], 1), F32)
    weight = jnp.zeros((meta.shape[0], 1), F32)
    for k in range(top):
        at = meta.shape[1] - META + k
        hit = (meta[:, at : at + 1] == expert).astype(F32)
        total = (
            meta[:, at + top : at + top + 1]
            + meta[:, at + 2 * top : at + 2 * top + 1]
            + meta[:, at + 3 * top : at + 3 * top + 1]
        )
        named = named + hit
        weight = weight + hit * total
    return named, weight


def order_mask(count, plan, sub):
    def key(dim):
        t = lax.broadcasted_iota(jnp.int32, (count, count), dim)
        block = lax.rem(lax.div(t, plan.group), plan.subs)
        return t + (jnp.bitwise_xor(block, sub) - block) * plan.group

    return (key(1) < key(0)).astype(BF16)


def route(metas, plan, ep, sub):
    count = metas[0].shape[0]
    earlier = order_mask(count, plan, sub)
    lane = lax.broadcasted_iota(jnp.int32, (count, LANES), 1)
    start = jnp.zeros((1, 1), F32)
    result = []
    bounds = []
    for column, meta in enumerate(metas):
        if column:
            start = jnp.maximum(start, float(plan.holds[column - 1]))
        found = []
        flags = jnp.zeros((count, LANES), F32)
        for slot in range(plan.slots):
            named, weight = chosen(meta, (ep * plan.slots + slot).astype(F32), plan.top)
            found.append((named, weight))
            flags = jnp.where(lane == slot, named, flags)
        prefix = dot(earlier, flags.astype(BF16), ((1,), (0,)))
        places = []
        for slot, (named, weight) in enumerate(found):
            place = jnp.where(named > 0.0, prefix[:, slot : slot + 1] + start, -1.0)
            places.append((place, weight))
            end = start + jnp.sum(named, axis=0, keepdims=True)
            bounds.append((slot, start, end))
            start = end
        result.append(places)
    return result, bounds


def slot_masks(bounds, plan):
    row = lax.broadcasted_iota(jnp.int32, (1, plan.rows), 1).astype(F32) + float(plan.first)
    masks = []
    for slot in range(plan.slots):
        mask = jnp.zeros((1, plan.rows), F32)
        for which, start, end in bounds:
            if which == slot:
                mask = mask + jnp.logical_and(row >= start, row < end).astype(F32)
        masks.append(mask)
    return masks


def rows_of(places, plan):
    return (
        lax.broadcasted_iota(jnp.int32, (places.shape[0], plan.rows), 1).astype(F32)
        + float(plan.first)
        == places
    )


def metas_of(layout, refs, width):
    metas, at = [], 0
    for count in layout:
        several = [ref[:, width:].astype(F32) for ref in refs[at : at + count]]
        metas.append(jnp.concatenate(several, axis=0))
        at += count
    return metas


def rows_kernel(plan, layout, place_ref, *refs):
    arrays = sum(layout)
    tokens = refs[:arrays]
    most_ref = refs[arrays]
    outs = refs[arrays + 1 :]
    width = outs[0].shape[0]
    ep, sub = place_ref[0], place_ref[1]
    metas = metas_of(layout, tokens, width)
    columns, bounds = route(metas, plan, ep, sub)
    begin = 0
    masks = slot_masks(bounds, plan)
    for _rows, mask_ref, high_ref, low_ref in zip(*[iter(outs)] * 4):
        size = mask_ref.shape[1]
        part = plan.part(begin, size)
        mask_ref[...] = jnp.zeros_like(mask_ref)
        for slot, mask in enumerate(masks):
            mask_ref[slot : slot + 1] = mask[:, begin : begin + size]
        at = 0
        for places in columns:
            mix = None
            for place, weight in places:
                term = jnp.where(rows_of(place, part), weight, 0.0)
                mix = term if mix is None else mix + term
            high = mix.astype(BF16)
            here = slice(at, at + mix.shape[0])
            high_ref[here] = high
            low_ref[here] = (mix - high.astype(F32)).astype(BF16)
            at += mix.shape[0]
        begin += size
    hots = []
    for places in columns:
        hot = None
        for place, _weight in places:
            hit = rows_of(place, plan).astype(F32)
            hot = hit if hot is None else hot + hit
        hots.append(hot.astype(BF16))
    hot = jnp.concatenate(hots, axis=0) if len(hots) > 1 else hots[0]
    chunk = 256
    for at in range(0, width, chunk):
        end = min(at + chunk, width)
        several = [ref[:, at:end] for ref in tokens]
        total = dot(jnp.concatenate(several, axis=0), hot, ((0,), (0,)))
        begin = 0
        for rows_ref in outs[::4]:
            rows_ref[at:end] = total[:, begin : begin + rows_ref.shape[1]].astype(BF16)
            begin += rows_ref.shape[1]
    lane = lax.broadcasted_iota(jnp.int32, (metas[0].shape[0], LANES), 1).astype(F32)
    owner = lax.div(lax.broadcasted_iota(jnp.int32, (1, LANES), 1), plan.slots)
    start = [jnp.zeros((1, 1), F32)] * plan.eps
    for column, meta in enumerate(metas):
        flags = jnp.zeros((meta.shape[0], LANES), F32)
        for k in range(plan.top):
            flags = flags + (meta[:, k : k + 1] == lane).astype(F32)
        counts = jnp.sum(flags, axis=0, keepdims=True)
        for e in range(plan.eps):
            if column:
                start[e] = jnp.maximum(start[e], float(plan.holds[column - 1]))
            start[e] = start[e] + jnp.sum(
                jnp.where(owner == e, counts, 0.0), axis=1, keepdims=True
            )
    most_ref[...] = jnp.broadcast_to(functools.reduce(jnp.maximum, start), most_ref.shape)


def rows_in(plan, place, held, split=None):
    layout = tuple(len(arrays) for arrays in held)
    tokens = [t for arrays in held for t in arrays]
    width = tokens[0].shape[1] - META
    total = sum(t.shape[0] for t in tokens)
    split = split or (plan.rows,)
    shapes = [jax.ShapeDtypeStruct((8, LANES), F32)]
    for size in split:
        shapes.append(jax.ShapeDtypeStruct((width, size), BF16))
        shapes.append(jax.ShapeDtypeStruct((8, size), F32))
        shapes.append(jax.ShapeDtypeStruct((total, size), BF16))
        shapes.append(jax.ShapeDtypeStruct((total, size), BF16))
    specs = [pl.BlockSpec(shape.shape, lambda i: (0, 0)) for shape in shapes]
    return pl.pallas_call(
        functools.partial(rows_kernel, plan, layout),
        grid=(1,),
        in_specs=[pl.BlockSpec(memory_space=pltpu.SMEM)]
        + [pl.BlockSpec(t.shape, lambda i: (0, 0)) for t in tokens],
        out_specs=specs,
        out_shape=shapes,
        compiler_params=params(),
        cost_estimate=HINT,
    )(place, *tokens)


def inner_kernel(plan, rows_ref, mask_ref, weight_ref, *refs):
    act_ref, mark_ref = refs[-2:]
    gating = upward = None
    for slot in range(plan.slots):
        gate = dot(weight_ref[slot, 0], rows_ref[...], ((1,), (0,)))
        up = dot(weight_ref[slot, 1], rows_ref[...], ((1,), (0,)))
        if slot == 0:
            gating, upward = gate, up
        else:
            mine = mask_ref[slot : slot + 1] > 0.0
            gating = jnp.where(mine, gate, gating)
            upward = jnp.where(mine, up, upward)
    act_ref[...] = (gating * jax.nn.sigmoid(swish_beta * gating) * (upward + 1.0)).astype(BF16)
    mark_ref[...] = jnp.zeros_like(mark_ref)


def piece(total):
    for size in (240, 120, 72, 40, 24, 16, 8):
        if total % size == 0:
            return size
    return total


def inner(plan, rows, mask, weights, after):
    slots, _two, units, width = weights.shape
    block = piece(units)
    return pl.pallas_call(
        functools.partial(inner_kernel, plan),
        grid=(units // block,),
        in_specs=[
            pl.BlockSpec(rows.shape, lambda i: (0, 0)),
            pl.BlockSpec(mask.shape, lambda i: (0, 0)),
            pl.BlockSpec((slots, 2, block, width), lambda i: (0, 0, i, 0)),
        ]
        + [pl.BlockSpec(memory_space=pl.ANY)] * len(after),
        out_specs=[
            pl.BlockSpec((block, rows.shape[1]), lambda i: (i, 0)),
            pl.BlockSpec((8, LANES), lambda i: (0, 0)),
        ],
        out_shape=[
            jax.ShapeDtypeStruct((units, rows.shape[1]), BF16),
            jax.ShapeDtypeStruct((8, LANES), F32),
        ],
        compiler_params=params(),
        cost_estimate=HINT,
    )(rows, mask, weights, *after)


def outer_kernel(plan, before, blocks, ends, place_ref, mask_ref, high_ref, low_ref, *refs):
    parts = refs[:blocks]
    befores = refs[blocks : blocks + before]
    weight_ref = refs[blocks + before]
    keep_ref, send_ref, act_ref, sum_ref = refs[-4:]
    sub = place_ref[1]
    units = parts[0].shape[0]
    slot, chunk = pl.program_id(0), pl.program_id(1)
    size = weight_ref.shape[1]
    here = pl.ds(pl.multiple_of(chunk * size, size), size)

    @pl.when(jnp.logical_and(slot == 0, chunk == 0))
    def _():
        for b in range(plan.subs):
            for k in range(plan.subs):

                @pl.when(jnp.bitwise_xor(sub, k) == b)
                def _():
                    at = slice(b * units, (b + 1) * units)
                    if k == 3 and ends:
                        inside = jnp.logical_or(sub == 1, sub == 2)

                        @pl.when(inside)
                        def _():
                            act_ref[at] = parts[3][...]

                        @pl.when(jnp.logical_not(inside))
                        def _():
                            act_ref[at] = parts[4][...]
                    else:
                        act_ref[at] = parts[k][...]

    out = dot(weight_ref[0], act_ref[...], ((1,), (0,))).astype(BF16)

    @pl.when(slot == 0)
    def _():
        sum_ref[here] = out

    @pl.when(slot > 0)
    def _():
        mine = mask_ref[0:1]
        for s in range(1, plan.slots):
            mine = jnp.where(slot == s, mask_ref[s : s + 1], mine)
        sum_ref[here] = jnp.where(mine > 0.0, out, sum_ref[here])

    @pl.when(jnp.logical_and(slot == plan.slots - 1, chunk == pl.num_programs(1) - 1))
    def _():
        done = sum_ref[...]
        half = keep_ref.shape[1]
        for c in range(keep_ref.shape[0]):
            for h, ref in enumerate((keep_ref, send_ref)):
                if 2 * c * half >= high_ref.shape[0]:
                    ref[c] = jnp.zeros((half, ref.shape[2]), BF16)
                    continue
                at = slice((2 * c + h) * half, (2 * c + h + 1) * half)
                value = dot(high_ref[at], done, ((1,), (1,))) + dot(low_ref[at], done, ((1,), (1,)))
                if before and c < befores[h].shape[0]:
                    value = value + befores[h][c].astype(F32)
                ref[c] = value.astype(BF16)


def outer(plan, place, mixed, parts, befores, weights, columns, after=()):
    slots, columns_out, width = weights.shape
    mask, high, low = mixed
    blocks, rows = len(parts), parts[0].shape[1]
    half = plan.group * plan.subs
    size = 240 if columns_out % 240 == 0 else columns_out
    result = jax.ShapeDtypeStruct((columns, half, columns_out), BF16)
    return pl.pallas_call(
        functools.partial(outer_kernel, plan, len(befores), blocks, blocks > plan.subs),
        grid=(slots, columns_out // size),
        in_specs=[pl.BlockSpec(memory_space=pltpu.SMEM)]
        + [pl.BlockSpec(m.shape, lambda i, j: (0, 0)) for m in mixed]
        + [pl.BlockSpec(p.shape, lambda i, j: (0, 0)) for p in parts]
        + [pl.BlockSpec(b.shape, lambda i, j: (0, 0, 0)) for b in befores]
        + [pl.BlockSpec((1, size, width), lambda i, j: (i, j, 0))]
        + [pl.BlockSpec(memory_space=pl.ANY)] * len(after),
        out_specs=[pl.BlockSpec(result.shape, lambda i, j: (0, 0, 0))] * 2,
        out_shape=[result, result],
        scratch_shapes=[
            pltpu.VMEM((width, rows), BF16),
            pltpu.VMEM((columns_out, rows), BF16),
        ],
        compiler_params=params(),
        cost_estimate=HINT,
    )(place, mask, high, low, *parts, *befores, weights, *after)


def finish_kernel(subs, columns, place_ref, *refs):
    out_ref = refs[-1]
    sub = place_ref[1]
    width = refs[0].shape[1]
    steps, rows, _ = out_ref.shape
    sums = []
    for k in range(subs):
        value = refs[k * columns][...].astype(F32)
        for j in range(1, columns):
            value = value + refs[k * columns + j][...].astype(F32)
        sums.append(value)
    for b in range(subs):
        value = sums[0]
        for k in range(1, subs):
            value = jnp.where(jnp.bitwise_xor(sub, k) == b, sums[k], value)
        value = value.astype(BF16)
        for s in range(steps):
            out_ref[s, :, b * width : (b + 1) * width] = value[s * rows : (s + 1) * rows]


def finish(place, parts, steps):
    subs, columns = len(parts), len(parts[0])
    rows, width = parts[0][0].shape
    return pl.pallas_call(
        functools.partial(finish_kernel, subs, columns),
        grid=(1,),
        in_specs=[pl.BlockSpec(memory_space=pltpu.SMEM)]
        + [pl.BlockSpec((rows, width), lambda i: (0, 0))] * (subs * columns),
        out_specs=pl.BlockSpec((steps, rows // steps, width * subs), lambda i: (0, 0, 0)),
        out_shape=jax.ShapeDtypeStruct((steps, rows // steps, width * subs), BF16),
        compiler_params=params(),
    )(place, *[p for several in parts for p in several])


def swap(x, axis, offset, count):
    return lax.ppermute(x, axis, [(i, i ^ offset) for i in range(count)])


def gather(x, subs):
    return [x] + [swap(x, "sub", k, subs) for k in range(1, subs)]


def gather_line(x):
    one = swap(x, "sub", 1, 4)
    two = swap(x, "sub", 2, 4)
    return [x, one, two, lax.ppermute(x, "sub", [(1, 2), (2, 1)])]


def gather_ends(two):
    return lax.ppermute(two, "sub", [(2, 3), (1, 0)])


def add(a, b):
    return (a.astype(F32) + b.astype(F32)).astype(BF16)


def local(
    tokens, norm_gain, copy_ids, gate_scores, inner_codes, inner_scales, down_codes, down_scales
):
    eps, subs, groups = lax.axis_size("ep"), lax.axis_size("sub"), lax.axis_size("grp")
    slots = inner_codes.shape[0]
    steps, rows, top = copy_ids.shape
    units = inner_codes.shape[3]
    experts = eps * slots
    capacity = (3 * rows * top + 2 * experts - 1) // (2 * experts)
    columns = eps // 2
    place = jnp.stack([lax.axis_index("ep"), lax.axis_index("sub")]).astype(jnp.int32)
    group = steps * rows

    packed = pack(tokens, norm_gain, copy_ids, gate_scores)
    near = [packed] + [swap(packed, "sub", k, subs) for k in range(1, subs)]
    codes = jnp.transpose(inner_codes, (0, 2, 3, 1)).reshape(slots * 2, units, -1)
    scales = jnp.transpose(inner_scales, (0, 2, 3, 1)).reshape(slots * 2, units, -1)
    inner_weights, mark = dequant(codes, scales, packed)
    inner_weights = inner_weights.reshape(slots, 2, units, -1)
    outer_codes = jnp.transpose(down_codes, (0, 2, 1))
    outer_scales = jnp.transpose(down_scales, (0, 2, 1))
    line = columns == 2 and subs == 4
    first_across = [swap(packed, "ep", 2, eps)] if line else []
    own = join(near, [mark] + first_across)[0]
    other = swap(own, "ep", 1, eps)

    capacity_rows = group * subs * 2 // rows * slots * capacity

    def plan(first, count, holds):
        return Plan(first, count, holds, slots, subs, group, top, eps)

    if line and capacity_rows % 384 == 0:
        most = 2 * capacity_rows
        first = capacity_rows // 384 * 256
        second = capacity_rows
        last = most - first - second
        holds = (first,)
        plan0, plan1 = plan(0, first, holds), plan(first, second, holds)
        plan2 = plan(first + second, last, holds)
        pair = [own, other]
        _, rows0, *mixed0 = rows_in(plan0, place, [pair])
        act0, mark = inner(plan0, rows0, mixed0[0], inner_weights, [])
        parts0 = gather_line(act0)
        pieces = first_across + [swap(n, "ep", 2, eps) for n in near[1:]]
        moved = join(pieces, [mark], 4)
        everything = [pair, list(moved) + [swap(m, "ep", 1, eps) for m in moved]]
        longest, *several = rows_in(
            plan(first, second + last, holds), place, everything, (second, last)
        )
        rows1, rows2 = several[0], several[4]
        mixed1, mixed2 = several[1:4], several[5:]
        act1, _ = inner(plan1, rows1, mixed1[0], inner_weights, [])
        act1 = join([act1], parts0[1:2])[0]
        parts0.append(gather_ends(parts0[2]))
        parts1 = gather(act1, subs)
        for shift in range(1, groups):
            moved = lax.ppermute(
                longest, "grp", [(i, (i + shift) % groups) for i in range(groups)]
            )
            longest = jnp.maximum(longest, moved)
        outer_weights, _ = dequant(outer_codes, outer_scales, parts1[1])
        sums = outer(plan0, place, mixed0, parts0, [], outer_weights, columns)

        def more(kept, sent):
            act, _ = inner(plan2, rows2, mixed2[0], inner_weights, [kept])
            return tuple(
                outer(plan2, place, mixed2, gather(act, subs), [kept, sent], outer_weights, columns)
            )

        sums = lax.cond(
            longest[0, 0] > float(first + second), more, lambda a, b: (a, b), *sums
        )
        keep, send = outer(plan1, place, mixed1, parts1, sums, outer_weights, columns)
    else:
        count = -(-capacity_rows // LANES) * LANES
        each = plan(0, count, ())
        outer_weights, _ = dequant(outer_codes, outer_scales, own)
        keeps, sends = [], []
        across = [swap(own, "ep", 2 * j, eps) for j in range(1, columns)]
        held = [[own, other]] + [[a, swap(a, "ep", 1, eps)] for a in across]
        for pair in held:
            _, rows_here, *mixed = rows_in(each, place, [pair])
            act, _ = inner(each, rows_here, mixed[0], inner_weights, [])
            kept, sent = outer(each, place, mixed, gather(act, subs), [], outer_weights, 1)
            keeps.append(kept)
            sends.append(sent)
        keep, send = jnp.concatenate(keeps, axis=0), jnp.concatenate(sends, axis=0)

    chip = add(keep, swap(send, "ep", 1, eps))
    chip = chip.reshape(columns, subs, group, -1)
    arrived = []
    for k in range(subs):
        arrived.append([])
        for j in range(columns):
            pairs = []
            for e in range(eps):
                for z in range(subs):
                    pairs.append((e * subs + z, (e ^ (2 * j)) * subs + (z ^ k)))
            block = chip[j, k]
            arrived[-1].append(lax.ppermute(block, ("ep", "sub"), pairs) if j + k else block)
    return finish(place, arrived, steps)


def solution(mesh):
    return jax.shard_map(
        local,
        mesh=mesh,
        in_specs=(
            P(None, ("grp", "ep", "sub"), None),
            P(),
            P(None, ("grp", "ep", "sub"), None),
            P(None, ("grp", "ep", "sub"), None),
            P("ep", None, None, "sub"),
            P("ep", None, None, "sub"),
            P("ep", None, "sub"),
            P("ep", None, "sub"),
        ),
        out_specs=P(None, ("grp", "ep", "sub"), None),
        check_vma=False,
    )
```

```python
import functools

import jax
import jax.numpy as jnp
from jax import lax
from jax.experimental import pallas as pl
from jax.experimental.pallas import tpu as pltpu
from jax.sharding import PartitionSpec as P

epsilon = 1e-05
swish_beta = 1.702
META = 64
LANES = 128
VMEM_LIMIT = 24 * 1024 * 1024
HINT = pl.CostEstimate(flops=1024, bytes_accessed=1024, transcendentals=0)
F32 = jnp.float32
BF16 = jnp.bfloat16


def params():
    return pltpu.CompilerParams(vmem_limit_bytes=VMEM_LIMIT)


def in_hbm(x):
    return pltpu.with_memory_space_constraint(x, pltpu.HBM)


def dot(a, b, contract):
    return lax.dot_general(a, b, (contract, ((), ())), preferred_element_type=F32)


def pack_kernel(tokens_ref, gain_ref, ids_ref, scores_ref, out_ref):
    steps, rows, width = tokens_ref.shape
    top = ids_ref.shape[1]
    gain = gain_ref[...].reshape(1, width)
    eye = (
        lax.broadcasted_iota(jnp.int32, (rows, rows), 0)
        == lax.broadcasted_iota(jnp.int32, (rows, rows), 1)
    ).astype(F32)

    def column(row):
        return jnp.sum(eye * row, axis=1, keepdims=True)

    for s in range(steps):
        values = tokens_ref[s].astype(F32)
        mean = jnp.mean(values * values, axis=-1, keepdims=True)
        normed = (values * lax.rsqrt(mean + epsilon) * gain).astype(BF16)
        at = slice(s * rows, (s + 1) * rows)
        out_ref[at, :width] = normed
        scores = scores_ref[s]
        weights = scores / jnp.sum(scores, axis=0, keepdims=True)
        high = weights.astype(BF16)
        rest = weights - high.astype(F32)
        middle = rest.astype(BF16)
        low = (rest - middle.astype(F32)).astype(BF16)
        lane = lax.broadcasted_iota(jnp.int32, (rows, META), 1)
        meta = jnp.zeros((rows, META), F32)
        parts = (ids_ref[s].astype(F32), high.astype(F32), middle.astype(F32), low.astype(F32))
        for p, part in enumerate(parts):
            for k in range(top):
                meta = jnp.where(lane == p * top + k, column(part[k : k + 1]), meta)
        out_ref[at, width:] = meta.astype(BF16)


def pack(tokens, gain, ids, scores):
    steps, rows, width = tokens.shape
    return pl.pallas_call(
        pack_kernel,
        out_shape=jax.ShapeDtypeStruct((steps * rows, width + META), BF16),
        compiler_params=params(),
    )(
        in_hbm(tokens),
        in_hbm(gain),
        in_hbm(jnp.transpose(ids, (0, 2, 1))),
        in_hbm(jnp.transpose(scores, (0, 2, 1))),
    )


def dequant_kernel(codes_ref, scales_ref, _after_ref, out_ref, mark_ref):
    width = codes_ref.shape[2]
    scales = scales_ref[0]
    blocks = scales.shape[1]
    chunk = 256
    for at in range(0, width, chunk):
        end = min(at + chunk, width)
        column = lax.broadcasted_iota(jnp.int32, (blocks, end - at), 1) + at
        block = lax.broadcasted_iota(jnp.int32, (blocks, end - at), 0)
        first = block * (width // blocks)
        inside = jnp.logical_and(column >= first, column < first + width // blocks)
        wide = dot(scales, inside.astype(F32).astype(BF16), ((1,), (0,)))
        out_ref[0, :, at:end] = (codes_ref[0, :, at:end].astype(F32) * wide).astype(BF16)
    mark_ref[...] = jnp.zeros_like(mark_ref)


def dequant(codes, scales, after):
    count, rows, width = codes.shape
    blocks = scales.shape[2]
    return pl.pallas_call(
        dequant_kernel,
        grid=(count,),
        in_specs=[
            pl.BlockSpec((1, rows, width), lambda i: (i, 0, 0)),
            pl.BlockSpec((1, rows, blocks), lambda i: (i, 0, 0)),
            pl.BlockSpec(memory_space=pl.ANY),
        ],
        out_specs=[
            pl.BlockSpec((1, rows, width), lambda i: (i, 0, 0)),
            pl.BlockSpec((8, LANES), lambda i: (0, 0)),
        ],
        out_shape=[
            jax.ShapeDtypeStruct(codes.shape, BF16),
            jax.ShapeDtypeStruct((8, LANES), F32),
        ],
        compiler_params=params(),
        cost_estimate=HINT,
    )(in_hbm(codes), scales, after)


def join_kernel(count, pieces, *refs):
    outs = refs[-pieces:]
    rows, size = refs[0].shape[0], outs[0].shape[0]
    for p, out_ref in enumerate(outs):
        if size >= rows:
            for k in range(size // rows):
                out_ref[k * rows : (k + 1) * rows] = refs[p * (size // rows) + k][...]
        else:
            at = p * size % rows
            out_ref[...] = refs[p * size // rows][at : at + size]


def join(parts, after, pieces=1):
    rows, width = parts[0].shape
    count = len(parts)
    size = count * rows // pieces
    return pl.pallas_call(
        functools.partial(join_kernel, count, pieces),
        grid=(1,),
        in_specs=[pl.BlockSpec((rows, width), lambda i: (0, 0))] * count
        + [pl.BlockSpec(memory_space=pl.ANY)] * len(after),
        out_specs=[pl.BlockSpec((size, width), lambda i: (0, 0))] * pieces,
        out_shape=[jax.ShapeDtypeStruct((size, width), BF16)] * pieces,
        compiler_params=params(),
        cost_estimate=HINT,
    )(*parts, *after)


class Plan:
    def __init__(self, first, rows, holds, slots, subs, group, top, eps):
        self.first, self.rows = first, rows
        self.holds = holds
        self.slots, self.subs, self.group, self.top, self.eps = slots, subs, group, top, eps

    def part(self, begin, rows):
        return Plan(
            self.first + begin, rows, self.holds, self.slots, self.subs, self.group, self.top, self.eps
        )


def chosen(meta, expert, top):
    named = jnp.zeros((meta.shape[0], 1), F32)
    weight = jnp.zeros((meta.shape[0], 1), F32)
    for k in range(top):
        at = meta.shape[1] - META + k
        hit = (meta[:, at : at + 1] == expert).astype(F32)
        total = (
            meta[:, at + top : at + top + 1]
            + meta[:, at + 2 * top : at + 2 * top + 1]
            + meta[:, at + 3 * top : at + 3 * top + 1]
        )
        named = named + hit
        weight = weight + hit * total
    return named, weight


def order_mask(count, plan, sub):
    def key(dim):
        t = lax.broadcasted_iota(jnp.int32, (count, count), dim)
        block = lax.rem(lax.div(t, plan.group), plan.subs)
        return t + (jnp.bitwise_xor(block, sub) - block) * plan.group

    return (key(1) < key(0)).astype(BF16)


def route(metas, plan, ep, sub):
    count = metas[0].shape[0]
    earlier = order_mask(count, plan, sub)
    lane = lax.broadcasted_iota(jnp.int32, (count, LANES), 1)
    start = jnp.zeros((1, 1), F32)
    result = []
    bounds = []
    for column, meta in enumerate(metas):
        if column:
            start = jnp.maximum(start, float(plan.holds[column - 1]))
        found = []
        flags = jnp.zeros((count, LANES), F32)
        for slot in range(plan.slots):
            named, weight = chosen(meta, (ep * plan.slots + slot).astype(F32), plan.top)
            found.append((named, weight))
            flags = jnp.where(lane == slot, named, flags)
        prefix = dot(earlier, flags.astype(BF16), ((1,), (0,)))
        places = []
        for slot, (named, weight) in enumerate(found):
            place = jnp.where(named > 0.0, prefix[:, slot : slot + 1] + start, -1.0)
            places.append((place, weight))
            end = start + jnp.sum(named, axis=0, keepdims=True)
            bounds.append((slot, start, end))
            start = end
        result.append(places)
    return result, bounds


def slot_masks(bounds, plan):
    row = lax.broadcasted_iota(jnp.int32, (1, plan.rows), 1).astype(F32) + float(plan.first)
    masks = []
    for slot in range(plan.slots):
        mask = jnp.zeros((1, plan.rows), F32)
        for which, start, end in bounds:
            if which == slot:
                mask = mask + jnp.logical_and(row >= start, row < end).astype(F32)
        masks.append(mask)
    return masks


def rows_of(places, plan):
    return (
        lax.broadcasted_iota(jnp.int32, (places.shape[0], plan.rows), 1).astype(F32)
        + float(plan.first)
        == places
    )


def metas_of(layout, refs, width):
    metas, at = [], 0
    for count in layout:
        several = [ref[:, width:].astype(F32) for ref in refs[at : at + count]]
        metas.append(jnp.concatenate(several, axis=0))
        at += count
    return metas


def rows_kernel(plan, layout, place_ref, *refs):
    arrays = sum(layout)
    tokens = refs[:arrays]
    most_ref = refs[arrays]
    outs = refs[arrays + 1 :]
    width = outs[0].shape[0]
    ep, sub = place_ref[0], place_ref[1]
    metas = metas_of(layout, tokens, width)
    columns, bounds = route(metas, plan, ep, sub)
    begin = 0
    masks = slot_masks(bounds, plan)
    for _rows, mask_ref, high_ref, low_ref in zip(*[iter(outs)] * 4):
        size = mask_ref.shape[1]
        part = plan.part(begin, size)
        mask_ref[...] = jnp.zeros_like(mask_ref)
        for slot, mask in enumerate(masks):
            mask_ref[slot : slot + 1] = mask[:, begin : begin + size]
        at = 0
        for places in columns:
            mix = None
            for place, weight in places:
                term = jnp.where(rows_of(place, part), weight, 0.0)
                mix = term if mix is None else mix + term
            high = mix.astype(BF16)
            here = slice(at, at + mix.shape[0])
            high_ref[here] = high
            low_ref[here] = (mix - high.astype(F32)).astype(BF16)
            at += mix.shape[0]
        begin += size
    hots = []
    for places in columns:
        hot = None
        for place, _weight in places:
            hit = rows_of(place, plan).astype(F32)
            hot = hit if hot is None else hot + hit
        hots.append(hot.astype(BF16))
    hot = jnp.concatenate(hots, axis=0) if len(hots) > 1 else hots[0]
    chunk = 256
    for at in range(0, width, chunk):
        end = min(at + chunk, width)
        several = [ref[:, at:end] for ref in tokens]
        total = dot(jnp.concatenate(several, axis=0), hot, ((0,), (0,)))
        begin = 0
        for rows_ref in outs[::4]:
            rows_ref[at:end] = total[:, begin : begin + rows_ref.shape[1]].astype(BF16)
            begin += rows_ref.shape[1]
    lane = lax.broadcasted_iota(jnp.int32, (metas[0].shape[0], LANES), 1).astype(F32)
    owner = lax.div(lax.broadcasted_iota(jnp.int32, (1, LANES), 1), plan.slots)
    start = [jnp.zeros((1, 1), F32)] * plan.eps
    for column, meta in enumerate(metas):
        flags = jnp.zeros((meta.shape[0], LANES), F32)
        for k in range(plan.top):
            flags = flags + (meta[:, k : k + 1] == lane).astype(F32)
        counts = jnp.sum(flags, axis=0, keepdims=True)
        for e in range(plan.eps):
            if column:
                start[e] = jnp.maximum(start[e], float(plan.holds[column - 1]))
            start[e] = start[e] + jnp.sum(
                jnp.where(owner == e, counts, 0.0), axis=1, keepdims=True
            )
    most_ref[...] = jnp.broadcast_to(functools.reduce(jnp.maximum, start), most_ref.shape)


def rows_in(plan, place, held, split=None):
    layout = tuple(len(arrays) for arrays in held)
    tokens = [t for arrays in held for t in arrays]
    width = tokens[0].shape[1] - META
    total = sum(t.shape[0] for t in tokens)
    split = split or (plan.rows,)
    shapes = [jax.ShapeDtypeStruct((8, LANES), F32)]
    for size in split:
        shapes.append(jax.ShapeDtypeStruct((width, size), BF16))
        shapes.append(jax.ShapeDtypeStruct((8, size), F32))
        shapes.append(jax.ShapeDtypeStruct((total, size), BF16))
        shapes.append(jax.ShapeDtypeStruct((total, size), BF16))
    specs = [pl.BlockSpec(shape.shape, lambda i: (0, 0)) for shape in shapes]
    return pl.pallas_call(
        functools.partial(rows_kernel, plan, layout),
        grid=(1,),
        in_specs=[pl.BlockSpec(memory_space=pltpu.SMEM)]
        + [pl.BlockSpec(t.shape, lambda i: (0, 0)) for t in tokens],
        out_specs=specs,
        out_shape=shapes,
        compiler_params=params(),
        cost_estimate=HINT,
    )(place, *tokens)


def inner_kernel(plan, rows_ref, mask_ref, weight_ref, *refs):
    act_ref, mark_ref = refs[-2:]
    gating = upward = None
    for slot in range(plan.slots):
        gate = dot(weight_ref[slot, 0], rows_ref[...], ((1,), (0,)))
        up = dot(weight_ref[slot, 1], rows_ref[...], ((1,), (0,)))
        if slot == 0:
            gating, upward = gate, up
        else:
            mine = mask_ref[slot : slot + 1] > 0.0
            gating = jnp.where(mine, gate, gating)
            upward = jnp.where(mine, up, upward)
    act_ref[...] = (gating * jax.nn.sigmoid(swish_beta * gating) * (upward + 1.0)).astype(BF16)
    mark_ref[...] = jnp.zeros_like(mark_ref)


def piece(total):
    for size in (240, 120, 72, 40, 24, 16, 8):
        if total % size == 0:
            return size
    return total


def inner(plan, rows, mask, weights, after):
    slots, _two, units, width = weights.shape
    block = piece(units)
    return pl.pallas_call(
        functools.partial(inner_kernel, plan),
        grid=(units // block,),
        in_specs=[
            pl.BlockSpec(rows.shape, lambda i: (0, 0)),
            pl.BlockSpec(mask.shape, lambda i: (0, 0)),
            pl.BlockSpec((slots, 2, block, width), lambda i: (0, 0, i, 0)),
        ]
        + [pl.BlockSpec(memory_space=pl.ANY)] * len(after),
        out_specs=[
            pl.BlockSpec((block, rows.shape[1]), lambda i: (i, 0)),
            pl.BlockSpec((8, LANES), lambda i: (0, 0)),
        ],
        out_shape=[
            jax.ShapeDtypeStruct((units, rows.shape[1]), BF16),
            jax.ShapeDtypeStruct((8, LANES), F32),
        ],
        compiler_params=params(),
        cost_estimate=HINT,
    )(rows, mask, weights, *after)


def outer_kernel(plan, before, blocks, ends, place_ref, mask_ref, high_ref, low_ref, *refs):
    parts = refs[:blocks]
    befores = refs[blocks : blocks + before]
    weight_ref = refs[blocks + before]
    keep_ref, send_ref, act_ref, sum_ref = refs[-4:]
    sub = place_ref[1]
    units = parts[0].shape[0]
    slot, chunk = pl.program_id(0), pl.program_id(1)
    size = weight_ref.shape[1]
    here = pl.ds(pl.multiple_of(chunk * size, size), size)

    @pl.when(jnp.logical_and(slot == 0, chunk == 0))
    def _():
        for b in range(plan.subs):
            for k in range(plan.subs):

                @pl.when(jnp.bitwise_xor(sub, k) == b)
                def _():
                    at = slice(b * units, (b + 1) * units)
                    if k == 3 and ends:
                        inside = jnp.logical_or(sub == 1, sub == 2)

                        @pl.when(inside)
                        def _():
                            act_ref[at] = parts[3][...]

                        @pl.when(jnp.logical_not(inside))
                        def _():
                            act_ref[at] = parts[4][...]
                    else:
                        act_ref[at] = parts[k][...]

    out = dot(weight_ref[0], act_ref[...], ((1,), (0,))).astype(BF16)

    @pl.when(slot == 0)
    def _():
        sum_ref[here] = out

    @pl.when(slot > 0)
    def _():
        mine = mask_ref[0:1]
        for s in range(1, plan.slots):
            mine = jnp.where(slot == s, mask_ref[s : s + 1], mine)
        sum_ref[here] = jnp.where(mine > 0.0, out, sum_ref[here])

    @pl.when(jnp.logical_and(slot == plan.slots - 1, chunk == pl.num_programs(1) - 1))
    def _():
        done = sum_ref[...]
        half = keep_ref.shape[1]
        for c in range(keep_ref.shape[0]):
            for h, ref in enumerate((keep_ref, send_ref)):
                if 2 * c * half >= high_ref.shape[0]:
                    ref[c] = jnp.zeros((half, ref.shape[2]), BF16)
                    continue
                at = slice((2 * c + h) * half, (2 * c + h + 1) * half)
                value = dot(high_ref[at], done, ((1,), (1,))) + dot(low_ref[at], done, ((1,), (1,)))
                if before and c < befores[h].shape[0]:
                    value = value + befores[h][c].astype(F32)
                ref[c] = value.astype(BF16)


def outer(plan, place, mixed, parts, befores, weights, columns, after=()):
    slots, columns_out, width = weights.shape
    mask, high, low = mixed
    blocks, rows = len(parts), parts[0].shape[1]
    half = plan.group * plan.subs
    size = 240 if columns_out % 240 == 0 else columns_out
    result = jax.ShapeDtypeStruct((columns, half, columns_out), BF16)
    return pl.pallas_call(
        functools.partial(outer_kernel, plan, len(befores), blocks, blocks > plan.subs),
        grid=(slots, columns_out // size),
        in_specs=[pl.BlockSpec(memory_space=pltpu.SMEM)]
        + [pl.BlockSpec(m.shape, lambda i, j: (0, 0)) for m in mixed]
        + [pl.BlockSpec(p.shape, lambda i, j: (0, 0)) for p in parts]
        + [pl.BlockSpec(b.shape, lambda i, j: (0, 0, 0)) for b in befores]
        + [pl.BlockSpec((1, size, width), lambda i, j: (i, j, 0))]
        + [pl.BlockSpec(memory_space=pl.ANY)] * len(after),
        out_specs=[pl.BlockSpec(result.shape, lambda i, j: (0, 0, 0))] * 2,
        out_shape=[result, result],
        scratch_shapes=[
            pltpu.VMEM((width, rows), BF16),
            pltpu.VMEM((columns_out, rows), BF16),
        ],
        compiler_params=params(),
        cost_estimate=HINT,
    )(place, mask, high, low, *parts, *befores, weights, *after)


def finish_kernel(subs, columns, place_ref, *refs):
    out_ref = refs[-1]
    sub = place_ref[1]
    width = refs[0].shape[1]
    steps, rows, _ = out_ref.shape
    sums = []
    for k in range(subs):
        value = refs[k * columns][...].astype(F32)
        for j in range(1, columns):
            value = value + refs[k * columns + j][...].astype(F32)
        sums.append(value)
    for b in range(subs):
        value = sums[0]
        for k in range(1, subs):
            value = jnp.where(jnp.bitwise_xor(sub, k) == b, sums[k], value)
        value = value.astype(BF16)
        for s in range(steps):
            out_ref[s, :, b * width : (b + 1) * width] = value[s * rows : (s + 1) * rows]


def finish(place, parts, steps):
    subs, columns = len(parts), len(parts[0])
    rows, width = parts[0][0].shape
    return pl.pallas_call(
        functools.partial(finish_kernel, subs, columns),
        grid=(1,),
        in_specs=[pl.BlockSpec(memory_space=pltpu.SMEM)]
        + [pl.BlockSpec((rows, width), lambda i: (0, 0))] * (subs * columns),
        out_specs=pl.BlockSpec((steps, rows // steps, width * subs), lambda i: (0, 0, 0)),
        out_shape=jax.ShapeDtypeStruct((steps, rows // steps, width * subs), BF16),
        compiler_params=params(),
    )(place, *[p for several in parts for p in several])


def swap(x, axis, offset, count):
    return lax.ppermute(x, axis, [(i, i ^ offset) for i in range(count)])


def gather(x, subs):
    return [x] + [swap(x, "sub", k, subs) for k in range(1, subs)]


def gather_last(x, two):
    middle = lax.ppermute(x, "sub", [(1, 2), (2, 1)])
    return [middle, lax.ppermute(two, "sub", [(2, 3), (1, 0)])]


def add(a, b):
    return (a.astype(F32) + b.astype(F32)).astype(BF16)


def local(
    tokens, norm_gain, copy_ids, gate_scores, inner_codes, inner_scales, down_codes, down_scales
):
    eps, subs, groups = lax.axis_size("ep"), lax.axis_size("sub"), lax.axis_size("grp")
    slots = inner_codes.shape[0]
    steps, rows, top = copy_ids.shape
    units = inner_codes.shape[3]
    experts = eps * slots
    capacity = (3 * rows * top + 2 * experts - 1) // (2 * experts)
    columns = eps // 2
    place = jnp.stack([lax.axis_index("ep"), lax.axis_index("sub")]).astype(jnp.int32)
    group = steps * rows

    packed = pack(tokens, norm_gain, copy_ids, gate_scores)
    near = [packed] + [swap(packed, "sub", k, subs) for k in range(1, subs)]
    codes = jnp.transpose(inner_codes, (0, 2, 3, 1)).reshape(slots * 2, units, -1)
    scales = jnp.transpose(inner_scales, (0, 2, 3, 1)).reshape(slots * 2, units, -1)
    inner_weights, mark = dequant(codes, scales, packed)
    inner_weights = inner_weights.reshape(slots, 2, units, -1)
    outer_codes = jnp.transpose(down_codes, (0, 2, 1))
    outer_scales = jnp.transpose(down_scales, (0, 2, 1))
    line = columns == 2 and subs == 4
    first_across = [swap(packed, "ep", 2, eps)] if line else []
    own = join(near, [mark] + first_across)[0]
    other = swap(own, "ep", 1, eps)

    capacity_rows = group * subs * 2 // rows * slots * capacity

    def plan(first, count, holds):
        return Plan(first, count, holds, slots, subs, group, top, eps)

    if line and capacity_rows % 384 == 0:
        most = 2 * capacity_rows
        first = capacity_rows // 384 * 256
        second = capacity_rows
        last = most - first - second
        holds = (first,)
        plan0, plan1 = plan(0, first, holds), plan(first, second, holds)
        plan2 = plan(first + second, last, holds)
        pair = [own, other]
        _, rows0, *mixed0 = rows_in(plan0, place, [pair])
        act0, mark = inner(plan0, rows0, mixed0[0], inner_weights, [])
        one0, two0 = swap(act0, "sub", 1, subs), swap(act0, "sub", 2, subs)
        pieces = first_across + [swap(n, "ep", 2, eps) for n in near[1:]]
        moved = join(pieces, [mark], 4)
        everything = [pair, list(moved) + [swap(m, "ep", 1, eps) for m in moved]]
        longest, *several = rows_in(
            plan(first, second + last, holds), place, everything, (second, last)
        )
        rows1, rows2 = several[0], several[4]
        mixed1, mixed2 = several[1:4], several[5:]
        act1, _ = inner(plan1, rows1, mixed1[0], inner_weights, [])
        act1 = join([act1], [one0, two0])[0]
        one1, two1 = swap(act1, "sub", 1, subs), swap(act1, "sub", 2, subs)
        parts0 = [act0, one0, two0] + gather_last(join([act0], [act1])[0], two0)
        for shift in range(1, groups):
            moved = lax.ppermute(
                longest, "grp", [(i, (i + shift) % groups) for i in range(groups)]
            )
            longest = jnp.maximum(longest, moved)
        outer_weights, _ = dequant(outer_codes, outer_scales, act1)
        sums = outer(plan0, place, mixed0, parts0, [], outer_weights, columns)

        parts1 = [act1, one1, two1] + gather_last(join([act1], [two1, sums[0]])[0], two1)

        def more(kept, sent):
            act, _ = inner(plan2, rows2, mixed2[0], inner_weights, [kept])
            return tuple(
                outer(plan2, place, mixed2, gather(act, subs), [kept, sent], outer_weights, columns)
            )

        sums = lax.cond(
            longest[0, 0] > float(first + second), more, lambda a, b: (a, b), *sums
        )
        keep, send = outer(plan1, place, mixed1, parts1, sums, outer_weights, columns)
    else:
        count = -(-capacity_rows // LANES) * LANES
        each = plan(0, count, ())
        outer_weights, _ = dequant(outer_codes, outer_scales, own)
        keeps, sends = [], []
        across = [swap(own, "ep", 2 * j, eps) for j in range(1, columns)]
        held = [[own, other]] + [[a, swap(a, "ep", 1, eps)] for a in across]
        for pair in held:
            _, rows_here, *mixed = rows_in(each, place, [pair])
            act, _ = inner(each, rows_here, mixed[0], inner_weights, [])
            kept, sent = outer(each, place, mixed, gather(act, subs), [], outer_weights, 1)
            keeps.append(kept)
            sends.append(sent)
        keep, send = jnp.concatenate(keeps, axis=0), jnp.concatenate(sends, axis=0)

    chip = add(keep, swap(send, "ep", 1, eps))
    chip = chip.reshape(columns, subs, group, -1)
    arrived = []
    for k in range(subs):
        arrived.append([])
        for j in range(columns):
            pairs = []
            for e in range(eps):
                for z in range(subs):
                    pairs.append((e * subs + z, (e ^ (2 * j)) * subs + (z ^ k)))
            block = chip[j, k]
            arrived[-1].append(lax.ppermute(block, ("ep", "sub"), pairs) if j + k else block)
    return finish(place, arrived, steps)


def solution(mesh):
    return jax.shard_map(
        local,
        mesh=mesh,
        in_specs=(
            P(None, ("grp", "ep", "sub"), None),
            P(),
            P(None, ("grp", "ep", "sub"), None),
            P(None, ("grp", "ep", "sub"), None),
            P("ep", None, None, "sub"),
            P("ep", None, None, "sub"),
            P("ep", None, "sub"),
            P("ep", None, "sub"),
        ),
        out_specs=P(None, ("grp", "ep", "sub"), None),
        check_vma=False,
    )
```

```python
import functools

import jax
import jax.numpy as jnp
from jax import lax
from jax.experimental import pallas as pl
from jax.experimental.pallas import tpu as pltpu
from jax.sharding import PartitionSpec as P

epsilon = 1e-05
swish_beta = 1.702
META = 64
LANES = 128
VMEM_LIMIT = 24 * 1024 * 1024
HINT = pl.CostEstimate(flops=1024, bytes_accessed=1024, transcendentals=0)
F32 = jnp.float32
BF16 = jnp.bfloat16


def params():
    return pltpu.CompilerParams(vmem_limit_bytes=VMEM_LIMIT)


def in_hbm(x):
    return pltpu.with_memory_space_constraint(x, pltpu.HBM)


def dot(a, b, contract):
    return lax.dot_general(a, b, (contract, ((), ())), preferred_element_type=F32)


def pack_kernel(tokens_ref, gain_ref, ids_ref, scores_ref, out_ref):
    steps, rows, width = tokens_ref.shape
    top = ids_ref.shape[1]
    gain = gain_ref[...].reshape(1, width)
    eye = (
        lax.broadcasted_iota(jnp.int32, (rows, rows), 0)
        == lax.broadcasted_iota(jnp.int32, (rows, rows), 1)
    ).astype(F32)

    def column(row):
        return jnp.sum(eye * row, axis=1, keepdims=True)

    for s in range(steps):
        values = tokens_ref[s].astype(F32)
        mean = jnp.mean(values * values, axis=-1, keepdims=True)
        normed = (values * lax.rsqrt(mean + epsilon) * gain).astype(BF16)
        at = slice(s * rows, (s + 1) * rows)
        out_ref[at, :width] = normed
        scores = scores_ref[s]
        weights = scores / jnp.sum(scores, axis=0, keepdims=True)
        high = weights.astype(BF16)
        rest = weights - high.astype(F32)
        middle = rest.astype(BF16)
        low = (rest - middle.astype(F32)).astype(BF16)
        lane = lax.broadcasted_iota(jnp.int32, (rows, META), 1)
        meta = jnp.zeros((rows, META), F32)
        parts = (ids_ref[s].astype(F32), high.astype(F32), middle.astype(F32), low.astype(F32))
        for p, part in enumerate(parts):
            for k in range(top):
                meta = jnp.where(lane == p * top + k, column(part[k : k + 1]), meta)
        out_ref[at, width:] = meta.astype(BF16)


def pack(tokens, gain, ids, scores):
    steps, rows, width = tokens.shape
    return pl.pallas_call(
        pack_kernel,
        out_shape=jax.ShapeDtypeStruct((steps * rows, width + META), BF16),
        compiler_params=params(),
    )(
        in_hbm(tokens),
        in_hbm(gain),
        in_hbm(jnp.transpose(ids, (0, 2, 1))),
        in_hbm(jnp.transpose(scores, (0, 2, 1))),
    )


def dequant_kernel(codes_ref, scales_ref, _after_ref, out_ref, mark_ref):
    width = codes_ref.shape[2]
    scales = scales_ref[0]
    blocks = scales.shape[1]
    chunk = 256
    for at in range(0, width, chunk):
        end = min(at + chunk, width)
        column = lax.broadcasted_iota(jnp.int32, (blocks, end - at), 1) + at
        block = lax.broadcasted_iota(jnp.int32, (blocks, end - at), 0)
        first = block * (width // blocks)
        inside = jnp.logical_and(column >= first, column < first + width // blocks)
        wide = dot(scales, inside.astype(F32).astype(BF16), ((1,), (0,)))
        out_ref[0, :, at:end] = (codes_ref[0, :, at:end].astype(F32) * wide).astype(BF16)
    mark_ref[...] = jnp.zeros_like(mark_ref)


def dequant(codes, scales, after):
    count, rows, width = codes.shape
    blocks = scales.shape[2]
    return pl.pallas_call(
        dequant_kernel,
        grid=(count,),
        in_specs=[
            pl.BlockSpec((1, rows, width), lambda i: (i, 0, 0)),
            pl.BlockSpec((1, rows, blocks), lambda i: (i, 0, 0)),
            pl.BlockSpec(memory_space=pl.ANY),
        ],
        out_specs=[
            pl.BlockSpec((1, rows, width), lambda i: (i, 0, 0)),
            pl.BlockSpec((8, LANES), lambda i: (0, 0)),
        ],
        out_shape=[
            jax.ShapeDtypeStruct(codes.shape, BF16),
            jax.ShapeDtypeStruct((8, LANES), F32),
        ],
        compiler_params=params(),
        cost_estimate=HINT,
    )(in_hbm(codes), scales, after)


def join_kernel(count, pieces, *refs):
    outs = refs[-pieces:]
    rows, size = refs[0].shape[0], outs[0].shape[0]
    for p, out_ref in enumerate(outs):
        if size >= rows:
            for k in range(size // rows):
                out_ref[k * rows : (k + 1) * rows] = refs[p * (size // rows) + k][...]
        else:
            at = p * size % rows
            out_ref[...] = refs[p * size // rows][at : at + size]


def join(parts, after, pieces=1):
    rows, width = parts[0].shape
    count = len(parts)
    size = count * rows // pieces
    return pl.pallas_call(
        functools.partial(join_kernel, count, pieces),
        grid=(1,),
        in_specs=[pl.BlockSpec((rows, width), lambda i: (0, 0))] * count
        + [pl.BlockSpec(memory_space=pl.ANY)] * len(after),
        out_specs=[pl.BlockSpec((size, width), lambda i: (0, 0))] * pieces,
        out_shape=[jax.ShapeDtypeStruct((size, width), BF16)] * pieces,
        compiler_params=params(),
        cost_estimate=HINT,
    )(*parts, *after)


class Plan:
    def __init__(self, first, rows, holds, slots, subs, group, top, eps):
        self.first, self.rows = first, rows
        self.holds = holds
        self.slots, self.subs, self.group, self.top, self.eps = slots, subs, group, top, eps

    def part(self, begin, rows):
        return Plan(
            self.first + begin, rows, self.holds, self.slots, self.subs, self.group, self.top, self.eps
        )


def chosen(meta, expert, top):
    named = jnp.zeros((meta.shape[0], 1), F32)
    weight = jnp.zeros((meta.shape[0], 1), F32)
    for k in range(top):
        at = meta.shape[1] - META + k
        hit = (meta[:, at : at + 1] == expert).astype(F32)
        total = (
            meta[:, at + top : at + top + 1]
            + meta[:, at + 2 * top : at + 2 * top + 1]
            + meta[:, at + 3 * top : at + 3 * top + 1]
        )
        named = named + hit
        weight = weight + hit * total
    return named, weight


def order_mask(count, plan, sub):
    def key(dim):
        t = lax.broadcasted_iota(jnp.int32, (count, count), dim)
        block = lax.rem(lax.div(t, plan.group), plan.subs)
        return t + (jnp.bitwise_xor(block, sub) - block) * plan.group

    return (key(1) < key(0)).astype(BF16)


def route(metas, plan, ep, sub):
    count = metas[0].shape[0]
    earlier = order_mask(count, plan, sub)
    lane = lax.broadcasted_iota(jnp.int32, (count, LANES), 1)
    start = jnp.zeros((1, 1), F32)
    result = []
    bounds = []
    for column, meta in enumerate(metas):
        if column:
            start = jnp.maximum(start, float(plan.holds[column - 1]))
        found = []
        flags = jnp.zeros((count, LANES), F32)
        for slot in range(plan.slots):
            named, weight = chosen(meta, (ep * plan.slots + slot).astype(F32), plan.top)
            found.append((named, weight))
            flags = jnp.where(lane == slot, named, flags)
        prefix = dot(earlier, flags.astype(BF16), ((1,), (0,)))
        places = []
        for slot, (named, weight) in enumerate(found):
            place = jnp.where(named > 0.0, prefix[:, slot : slot + 1] + start, -1.0)
            places.append((place, weight))
            end = start + jnp.sum(named, axis=0, keepdims=True)
            bounds.append((slot, start, end))
            start = end
        result.append(places)
    return result, bounds


def slot_masks(bounds, plan):
    row = lax.broadcasted_iota(jnp.int32, (1, plan.rows), 1).astype(F32) + float(plan.first)
    masks = []
    for slot in range(plan.slots):
        mask = jnp.zeros((1, plan.rows), F32)
        for which, start, end in bounds:
            if which == slot:
                mask = mask + jnp.logical_and(row >= start, row < end).astype(F32)
        masks.append(mask)
    return masks


def rows_of(places, plan):
    return (
        lax.broadcasted_iota(jnp.int32, (places.shape[0], plan.rows), 1).astype(F32)
        + float(plan.first)
        == places
    )


def metas_of(layout, refs, width):
    metas, at = [], 0
    for count in layout:
        several = [ref[:, width:].astype(F32) for ref in refs[at : at + count]]
        metas.append(jnp.concatenate(several, axis=0))
        at += count
    return metas


def rows_kernel(plan, layout, place_ref, *refs):
    arrays = sum(layout)
    tokens = refs[:arrays]
    most_ref = refs[arrays]
    outs = refs[arrays + 1 :]
    width = outs[0].shape[0]
    ep, sub = place_ref[0], place_ref[1]
    metas = metas_of(layout, tokens, width)
    columns, bounds = route(metas, plan, ep, sub)
    begin = 0
    masks = slot_masks(bounds, plan)
    for _rows, mask_ref, high_ref, low_ref in zip(*[iter(outs)] * 4):
        size = mask_ref.shape[1]
        part = plan.part(begin, size)
        mask_ref[...] = jnp.zeros_like(mask_ref)
        for slot, mask in enumerate(masks):
            mask_ref[slot : slot + 1] = mask[:, begin : begin + size]
        at = 0
        for places in columns:
            mix = None
            for place, weight in places:
                term = jnp.where(rows_of(place, part), weight, 0.0)
                mix = term if mix is None else mix + term
            high = mix.astype(BF16)
            here = slice(at, at + mix.shape[0])
            high_ref[here] = high
            low_ref[here] = (mix - high.astype(F32)).astype(BF16)
            at += mix.shape[0]
        begin += size
    hots = []
    for places in columns:
        hot = None
        for place, _weight in places:
            hit = rows_of(place, plan).astype(F32)
            hot = hit if hot is None else hot + hit
        hots.append(hot.astype(BF16))
    hot = jnp.concatenate(hots, axis=0) if len(hots) > 1 else hots[0]
    chunk = 256
    for at in range(0, width, chunk):
        end = min(at + chunk, width)
        several = [ref[:, at:end] for ref in tokens]
        total = dot(jnp.concatenate(several, axis=0), hot, ((0,), (0,)))
        begin = 0
        for rows_ref in outs[::4]:
            rows_ref[at:end] = total[:, begin : begin + rows_ref.shape[1]].astype(BF16)
            begin += rows_ref.shape[1]
    lane = lax.broadcasted_iota(jnp.int32, (metas[0].shape[0], LANES), 1).astype(F32)
    owner = lax.div(lax.broadcasted_iota(jnp.int32, (1, LANES), 1), plan.slots)
    start = [jnp.zeros((1, 1), F32)] * plan.eps
    for column, meta in enumerate(metas):
        flags = jnp.zeros((meta.shape[0], LANES), F32)
        for k in range(plan.top):
            flags = flags + (meta[:, k : k + 1] == lane).astype(F32)
        counts = jnp.sum(flags, axis=0, keepdims=True)
        for e in range(plan.eps):
            if column:
                start[e] = jnp.maximum(start[e], float(plan.holds[column - 1]))
            start[e] = start[e] + jnp.sum(
                jnp.where(owner == e, counts, 0.0), axis=1, keepdims=True
            )
    most_ref[...] = jnp.broadcast_to(functools.reduce(jnp.maximum, start), most_ref.shape)


def rows_in(plan, place, held, split=None):
    layout = tuple(len(arrays) for arrays in held)
    tokens = [t for arrays in held for t in arrays]
    width = tokens[0].shape[1] - META
    total = sum(t.shape[0] for t in tokens)
    split = split or (plan.rows,)
    shapes = [jax.ShapeDtypeStruct((8, LANES), F32)]
    for size in split:
        shapes.append(jax.ShapeDtypeStruct((width, size), BF16))
        shapes.append(jax.ShapeDtypeStruct((8, size), F32))
        shapes.append(jax.ShapeDtypeStruct((total, size), BF16))
        shapes.append(jax.ShapeDtypeStruct((total, size), BF16))
    specs = [pl.BlockSpec(shape.shape, lambda i: (0, 0)) for shape in shapes]
    return pl.pallas_call(
        functools.partial(rows_kernel, plan, layout),
        grid=(1,),
        in_specs=[pl.BlockSpec(memory_space=pltpu.SMEM)]
        + [pl.BlockSpec(t.shape, lambda i: (0, 0)) for t in tokens],
        out_specs=specs,
        out_shape=shapes,
        compiler_params=params(),
        cost_estimate=HINT,
    )(place, *tokens)


def inner_kernel(plan, rows_ref, mask_ref, weight_ref, *refs):
    act_ref, mark_ref = refs[-2:]
    gating = upward = None
    for slot in range(plan.slots):
        gate = dot(weight_ref[slot, 0], rows_ref[...], ((1,), (0,)))
        up = dot(weight_ref[slot, 1], rows_ref[...], ((1,), (0,)))
        if slot == 0:
            gating, upward = gate, up
        else:
            mine = mask_ref[slot : slot + 1] > 0.0
            gating = jnp.where(mine, gate, gating)
            upward = jnp.where(mine, up, upward)
    act_ref[...] = (gating * jax.nn.sigmoid(swish_beta * gating) * (upward + 1.0)).astype(BF16)
    mark_ref[...] = jnp.zeros_like(mark_ref)


def piece(total):
    for size in (240, 120, 72, 40, 24, 16, 8):
        if total % size == 0:
            return size
    return total


def inner(plan, rows, mask, weights, after):
    slots, _two, units, width = weights.shape
    block = piece(units)
    return pl.pallas_call(
        functools.partial(inner_kernel, plan),
        grid=(units // block,),
        in_specs=[
            pl.BlockSpec(rows.shape, lambda i: (0, 0)),
            pl.BlockSpec(mask.shape, lambda i: (0, 0)),
            pl.BlockSpec((slots, 2, block, width), lambda i: (0, 0, i, 0)),
        ]
        + [pl.BlockSpec(memory_space=pl.ANY)] * len(after),
        out_specs=[
            pl.BlockSpec((block, rows.shape[1]), lambda i: (i, 0)),
            pl.BlockSpec((8, LANES), lambda i: (0, 0)),
        ],
        out_shape=[
            jax.ShapeDtypeStruct((units, rows.shape[1]), BF16),
            jax.ShapeDtypeStruct((8, LANES), F32),
        ],
        compiler_params=params(),
        cost_estimate=HINT,
    )(rows, mask, weights, *after)


def outer_kernel(plan, before, blocks, ends, place_ref, mask_ref, high_ref, low_ref, *refs):
    parts = refs[:blocks]
    befores = refs[blocks : blocks + before]
    weight_ref = refs[blocks + before]
    keep_ref, send_ref, act_ref, sum_ref = refs[-4:]
    sub = place_ref[1]
    units = parts[0].shape[0]
    slot, chunk = pl.program_id(0), pl.program_id(1)
    size = weight_ref.shape[1]
    here = pl.ds(pl.multiple_of(chunk * size, size), size)

    @pl.when(jnp.logical_and(slot == 0, chunk == 0))
    def _():
        for b in range(plan.subs):
            for k in range(plan.subs):

                @pl.when(jnp.bitwise_xor(sub, k) == b)
                def _():
                    at = slice(b * units, (b + 1) * units)
                    if k == 3 and ends:
                        inside = jnp.logical_or(sub == 1, sub == 2)

                        @pl.when(inside)
                        def _():
                            act_ref[at] = parts[3][...]

                        @pl.when(jnp.logical_not(inside))
                        def _():
                            act_ref[at] = parts[4][...]
                    else:
                        act_ref[at] = parts[k][...]

    out = dot(weight_ref[0], act_ref[...], ((1,), (0,))).astype(BF16)

    @pl.when(slot == 0)
    def _():
        sum_ref[here] = out

    @pl.when(slot > 0)
    def _():
        mine = mask_ref[0:1]
        for s in range(1, plan.slots):
            mine = jnp.where(slot == s, mask_ref[s : s + 1], mine)
        sum_ref[here] = jnp.where(mine > 0.0, out, sum_ref[here])

    @pl.when(jnp.logical_and(slot == plan.slots - 1, chunk == pl.num_programs(1) - 1))
    def _():
        done = sum_ref[...]
        half = keep_ref.shape[1]
        for c in range(keep_ref.shape[0]):
            for h, ref in enumerate((keep_ref, send_ref)):
                if 2 * c * half >= high_ref.shape[0]:
                    ref[c] = jnp.zeros((half, ref.shape[2]), BF16)
                    continue
                at = slice((2 * c + h) * half, (2 * c + h + 1) * half)
                value = dot(high_ref[at], done, ((1,), (1,))) + dot(low_ref[at], done, ((1,), (1,)))
                if before and c < befores[h].shape[0]:
                    value = value + befores[h][c].astype(F32)
                ref[c] = value.astype(BF16)


def outer(plan, place, mixed, parts, befores, weights, columns, after=()):
    slots, columns_out, width = weights.shape
    mask, high, low = mixed
    blocks, rows = len(parts), parts[0].shape[1]
    half = plan.group * plan.subs
    size = 240 if columns_out % 240 == 0 else columns_out
    result = jax.ShapeDtypeStruct((columns, half, columns_out), BF16)
    return pl.pallas_call(
        functools.partial(outer_kernel, plan, len(befores), blocks, blocks > plan.subs),
        grid=(slots, columns_out // size),
        in_specs=[pl.BlockSpec(memory_space=pltpu.SMEM)]
        + [pl.BlockSpec(m.shape, lambda i, j: (0, 0)) for m in mixed]
        + [pl.BlockSpec(p.shape, lambda i, j: (0, 0)) for p in parts]
        + [pl.BlockSpec(b.shape, lambda i, j: (0, 0, 0)) for b in befores]
        + [pl.BlockSpec((1, size, width), lambda i, j: (i, j, 0))]
        + [pl.BlockSpec(memory_space=pl.ANY)] * len(after),
        out_specs=[pl.BlockSpec(result.shape, lambda i, j: (0, 0, 0))] * 2,
        out_shape=[result, result],
        scratch_shapes=[
            pltpu.VMEM((width, rows), BF16),
            pltpu.VMEM((columns_out, rows), BF16),
        ],
        compiler_params=params(),
        cost_estimate=HINT,
    )(place, mask, high, low, *parts, *befores, weights, *after)


def finish_kernel(subs, columns, place_ref, *refs):
    out_ref = refs[-1]
    sub = place_ref[1]
    width = refs[0].shape[1]
    steps, rows, _ = out_ref.shape
    sums = []
    for k in range(subs):
        value = refs[k * columns][...].astype(F32)
        for j in range(1, columns):
            value = value + refs[k * columns + j][...].astype(F32)
        sums.append(value)
    for b in range(subs):
        value = sums[0]
        for k in range(1, subs):
            value = jnp.where(jnp.bitwise_xor(sub, k) == b, sums[k], value)
        value = value.astype(BF16)
        for s in range(steps):
            out_ref[s, :, b * width : (b + 1) * width] = value[s * rows : (s + 1) * rows]


def finish(place, parts, steps):
    subs, columns = len(parts), len(parts[0])
    rows, width = parts[0][0].shape
    return pl.pallas_call(
        functools.partial(finish_kernel, subs, columns),
        grid=(1,),
        in_specs=[pl.BlockSpec(memory_space=pltpu.SMEM)]
        + [pl.BlockSpec((rows, width), lambda i: (0, 0))] * (subs * columns),
        out_specs=pl.BlockSpec((steps, rows // steps, width * subs), lambda i: (0, 0, 0)),
        out_shape=jax.ShapeDtypeStruct((steps, rows // steps, width * subs), BF16),
        compiler_params=params(),
    )(place, *[p for several in parts for p in several])


def swap(x, axis, offset, count):
    return lax.ppermute(x, axis, [(i, i ^ offset) for i in range(count)])


def gather(x, subs):
    return [x] + [swap(x, "sub", k, subs) for k in range(1, subs)]


def gather_middle(x):
    return lax.ppermute(x, "sub", [(1, 2), (2, 1)])


def gather_ends(two):
    return lax.ppermute(two, "sub", [(2, 3), (1, 0)])


def add(a, b):
    return (a.astype(F32) + b.astype(F32)).astype(BF16)


def local(
    tokens, norm_gain, copy_ids, gate_scores, inner_codes, inner_scales, down_codes, down_scales
):
    eps, subs, groups = lax.axis_size("ep"), lax.axis_size("sub"), lax.axis_size("grp")
    slots = inner_codes.shape[0]
    steps, rows, top = copy_ids.shape
    units = inner_codes.shape[3]
    experts = eps * slots
    capacity = (3 * rows * top + 2 * experts - 1) // (2 * experts)
    columns = eps // 2
    place = jnp.stack([lax.axis_index("ep"), lax.axis_index("sub")]).astype(jnp.int32)
    group = steps * rows

    packed = pack(tokens, norm_gain, copy_ids, gate_scores)
    near = [packed] + [swap(packed, "sub", k, subs) for k in range(1, subs)]
    codes = jnp.transpose(inner_codes, (0, 2, 3, 1)).reshape(slots * 2, units, -1)
    scales = jnp.transpose(inner_scales, (0, 2, 3, 1)).reshape(slots * 2, units, -1)
    inner_weights, mark = dequant(codes, scales, packed)
    inner_weights = inner_weights.reshape(slots, 2, units, -1)
    outer_codes = jnp.transpose(down_codes, (0, 2, 1))
    outer_scales = jnp.transpose(down_scales, (0, 2, 1))
    line = columns == 2 and subs == 4
    first_across = [swap(packed, "ep", 2, eps)] if line else []
    own = join(near, [mark] + first_across)[0]
    other = swap(own, "ep", 1, eps)

    capacity_rows = group * subs * 2 // rows * slots * capacity

    def plan(first, count, holds):
        return Plan(first, count, holds, slots, subs, group, top, eps)

    if line and capacity_rows % 384 == 0:
        most = 2 * capacity_rows
        first = capacity_rows // 384 * 256
        second = capacity_rows
        last = most - first - second
        holds = (first,)
        plan0, plan1 = plan(0, first, holds), plan(first, second, holds)
        plan2 = plan(first + second, last, holds)
        pair = [own, other]
        _, rows0, *mixed0 = rows_in(plan0, place, [pair])
        act0, mark = inner(plan0, rows0, mixed0[0], inner_weights, [])
        one0, two0 = swap(act0, "sub", 1, subs), swap(act0, "sub", 2, subs)
        middle0 = gather_middle(act0)
        pieces = first_across + [swap(n, "ep", 2, eps) for n in near[1:]]
        moved = join(pieces, [mark], 4)
        everything = [pair, list(moved) + [swap(m, "ep", 1, eps) for m in moved]]
        longest, *several = rows_in(
            plan(first, second + last, holds), place, everything, (second, last)
        )
        rows1, rows2 = several[0], several[4]
        mixed1, mixed2 = several[1:4], several[5:]
        act1, _ = inner(plan1, rows1, mixed1[0], inner_weights, [])
        act1 = join([act1], [one0, two0, middle0])[0]
        one1, two1 = swap(act1, "sub", 1, subs), swap(act1, "sub", 2, subs)
        parts0 = [act0, one0, two0, middle0, gather_ends(two0)]
        for shift in range(1, groups):
            moved = lax.ppermute(
                longest, "grp", [(i, (i + shift) % groups) for i in range(groups)]
            )
            longest = jnp.maximum(longest, moved)
        outer_weights, _ = dequant(outer_codes, outer_scales, act1)
        sums = outer(plan0, place, mixed0, parts0, [], outer_weights, columns)

        passed = join([act1], [two1, sums[0]])[0]
        parts1 = [act1, one1, two1, gather_middle(passed), gather_ends(two1)]

        def more(kept, sent):
            act, _ = inner(plan2, rows2, mixed2[0], inner_weights, [kept])
            return tuple(
                outer(plan2, place, mixed2, gather(act, subs), [kept, sent], outer_weights, columns)
            )

        sums = lax.cond(
            longest[0, 0] > float(first + second), more, lambda a, b: (a, b), *sums
        )
        keep, send = outer(plan1, place, mixed1, parts1, sums, outer_weights, columns)
    else:
        count = -(-capacity_rows // LANES) * LANES
        each = plan(0, count, ())
        outer_weights, _ = dequant(outer_codes, outer_scales, own)
        keeps, sends = [], []
        across = [swap(own, "ep", 2 * j, eps) for j in range(1, columns)]
        held = [[own, other]] + [[a, swap(a, "ep", 1, eps)] for a in across]
        for pair in held:
            _, rows_here, *mixed = rows_in(each, place, [pair])
            act, _ = inner(each, rows_here, mixed[0], inner_weights, [])
            kept, sent = outer(each, place, mixed, gather(act, subs), [], outer_weights, 1)
            keeps.append(kept)
            sends.append(sent)
        keep, send = jnp.concatenate(keeps, axis=0), jnp.concatenate(sends, axis=0)

    chip = add(keep, swap(send, "ep", 1, eps))
    chip = chip.reshape(columns, subs, group, -1)
    arrived = []
    for k in range(subs):
        arrived.append([])
        for j in range(columns):
            pairs = []
            for e in range(eps):
                for z in range(subs):
                    pairs.append((e * subs + z, (e ^ (2 * j)) * subs + (z ^ k)))
            block = chip[j, k]
            arrived[-1].append(lax.ppermute(block, ("ep", "sub"), pairs) if j + k else block)
    return finish(place, arrived, steps)


def solution(mesh):
    return jax.shard_map(
        local,
        mesh=mesh,
        in_specs=(
            P(None, ("grp", "ep", "sub"), None),
            P(),
            P(None, ("grp", "ep", "sub"), None),
            P(None, ("grp", "ep", "sub"), None),
            P("ep", None, None, "sub"),
            P("ep", None, None, "sub"),
            P("ep", None, "sub"),
            P("ep", None, "sub"),
        ),
        out_specs=P(None, ("grp", "ep", "sub"), None),
        check_vma=False,
    )
```

```python
import functools

import jax
import jax.numpy as jnp
from jax import lax
from jax.experimental import pallas as pl
from jax.experimental.pallas import tpu as pltpu
from jax.sharding import PartitionSpec as P

epsilon = 1e-05
swish_beta = 1.702
META = 64
LANES = 128
VMEM_LIMIT = 24 * 1024 * 1024
HINT = pl.CostEstimate(flops=1024, bytes_accessed=1024, transcendentals=0)
F32 = jnp.float32
BF16 = jnp.bfloat16


def params():
    return pltpu.CompilerParams(vmem_limit_bytes=VMEM_LIMIT)


def in_hbm(x):
    return pltpu.with_memory_space_constraint(x, pltpu.HBM)


def dot(a, b, contract):
    return lax.dot_general(a, b, (contract, ((), ())), preferred_element_type=F32)


def pack_kernel(tokens_ref, gain_ref, ids_ref, scores_ref, out_ref):
    steps, rows, width = tokens_ref.shape
    top = ids_ref.shape[1]
    gain = gain_ref[...].reshape(1, width)
    eye = (
        lax.broadcasted_iota(jnp.int32, (rows, rows), 0)
        == lax.broadcasted_iota(jnp.int32, (rows, rows), 1)
    ).astype(F32)

    def column(row):
        return jnp.sum(eye * row, axis=1, keepdims=True)

    for s in range(steps):
        values = tokens_ref[s].astype(F32)
        mean = jnp.mean(values * values, axis=-1, keepdims=True)
        normed = (values * lax.rsqrt(mean + epsilon) * gain).astype(BF16)
        at = slice(s * rows, (s + 1) * rows)
        out_ref[at, :width] = normed
        scores = scores_ref[s]
        weights = scores / jnp.sum(scores, axis=0, keepdims=True)
        high = weights.astype(BF16)
        rest = weights - high.astype(F32)
        middle = rest.astype(BF16)
        low = (rest - middle.astype(F32)).astype(BF16)
        lane = lax.broadcasted_iota(jnp.int32, (rows, META), 1)
        meta = jnp.zeros((rows, META), F32)
        parts = (ids_ref[s].astype(F32), high.astype(F32), middle.astype(F32), low.astype(F32))
        for p, part in enumerate(parts):
            for k in range(top):
                meta = jnp.where(lane == p * top + k, column(part[k : k + 1]), meta)
        out_ref[at, width:] = meta.astype(BF16)


def pack(tokens, gain, ids, scores):
    steps, rows, width = tokens.shape
    return pl.pallas_call(
        pack_kernel,
        out_shape=jax.ShapeDtypeStruct((steps * rows, width + META), BF16),
        compiler_params=params(),
    )(
        in_hbm(tokens),
        in_hbm(gain),
        in_hbm(jnp.transpose(ids, (0, 2, 1))),
        in_hbm(jnp.transpose(scores, (0, 2, 1))),
    )


def dequant_kernel(codes_ref, scales_ref, _after_ref, out_ref, mark_ref):
    width = codes_ref.shape[2]
    scales = scales_ref[0]
    blocks = scales.shape[1]
    chunk = 256 if len(out_ref.shape) == 3 else out_ref.shape[3]
    for at in range(0, width, chunk):
        end = min(at + chunk, width)
        column = lax.broadcasted_iota(jnp.int32, (blocks, end - at), 1) + at
        block = lax.broadcasted_iota(jnp.int32, (blocks, end - at), 0)
        first = block * (width // blocks)
        inside = jnp.logical_and(column >= first, column < first + width // blocks)
        wide = dot(scales, inside.astype(F32).astype(BF16), ((1,), (0,)))
        value = (codes_ref[0, :, at:end].astype(F32) * wide).astype(BF16)
        if len(out_ref.shape) == 3:
            out_ref[0, :, at:end] = value
        else:
            out_ref[0, at // chunk] = value
    mark_ref[...] = jnp.zeros_like(mark_ref)


def dequant(codes, scales, after, pieces=1):
    count, rows, width = codes.shape
    blocks = scales.shape[2]
    shape = (count, rows, width) if pieces == 1 else (count, pieces, rows, width // pieces)
    return pl.pallas_call(
        dequant_kernel,
        grid=(count,),
        in_specs=[
            pl.BlockSpec((1, rows, width), lambda i: (i, 0, 0)),
            pl.BlockSpec((1, rows, blocks), lambda i: (i, 0, 0)),
            pl.BlockSpec(memory_space=pl.ANY),
        ],
        out_specs=[
            pl.BlockSpec((1,) + shape[1:], lambda i: (i,) + (0,) * (len(shape) - 1)),
            pl.BlockSpec((8, LANES), lambda i: (0, 0)),
        ],
        out_shape=[
            jax.ShapeDtypeStruct(shape, BF16),
            jax.ShapeDtypeStruct((8, LANES), F32),
        ],
        compiler_params=params(),
        cost_estimate=HINT,
    )(in_hbm(codes), scales, after)


def join_kernel(count, pieces, *refs):
    outs = refs[-pieces:]
    rows, size = refs[0].shape[0], outs[0].shape[0]
    for p, out_ref in enumerate(outs):
        if size >= rows:
            for k in range(size // rows):
                out_ref[k * rows : (k + 1) * rows] = refs[p * (size // rows) + k][...]
        else:
            at = p * size % rows
            out_ref[...] = refs[p * size // rows][at : at + size]


def join(parts, after, pieces=1):
    rows, width = parts[0].shape
    count = len(parts)
    size = count * rows // pieces
    return pl.pallas_call(
        functools.partial(join_kernel, count, pieces),
        grid=(1,),
        in_specs=[pl.BlockSpec((rows, width), lambda i: (0, 0))] * count
        + [pl.BlockSpec(memory_space=pl.ANY)] * len(after),
        out_specs=[pl.BlockSpec((size, width), lambda i: (0, 0))] * pieces,
        out_shape=[jax.ShapeDtypeStruct((size, width), BF16)] * pieces,
        compiler_params=params(),
        cost_estimate=HINT,
    )(*parts, *after)


class Plan:
    def __init__(self, first, rows, holds, slots, subs, group, top, eps):
        self.first, self.rows = first, rows
        self.holds = holds
        self.slots, self.subs, self.group, self.top, self.eps = slots, subs, group, top, eps

    def part(self, begin, rows):
        return Plan(
            self.first + begin, rows, self.holds, self.slots, self.subs, self.group, self.top, self.eps
        )


def chosen(meta, expert, top):
    named = jnp.zeros((meta.shape[0], 1), F32)
    weight = jnp.zeros((meta.shape[0], 1), F32)
    for k in range(top):
        at = meta.shape[1] - META + k
        hit = (meta[:, at : at + 1] == expert).astype(F32)
        total = (
            meta[:, at + top : at + top + 1]
            + meta[:, at + 2 * top : at + 2 * top + 1]
            + meta[:, at + 3 * top : at + 3 * top + 1]
        )
        named = named + hit
        weight = weight + hit * total
    return named, weight


def order_mask(count, plan, sub):
    def key(dim):
        t = lax.broadcasted_iota(jnp.int32, (count, count), dim)
        block = lax.rem(lax.div(t, plan.group), plan.subs)
        return t + (jnp.bitwise_xor(block, sub) - block) * plan.group

    return (key(1) < key(0)).astype(BF16)


def route(metas, plan, ep, sub):
    count = metas[0].shape[0]
    earlier = order_mask(count, plan, sub)
    lane = lax.broadcasted_iota(jnp.int32, (count, LANES), 1)
    start = jnp.zeros((1, 1), F32)
    result = []
    bounds = []
    for column, meta in enumerate(metas):
        if column:
            start = jnp.maximum(start, float(plan.holds[column - 1]))
        found = []
        flags = jnp.zeros((count, LANES), F32)
        for slot in range(plan.slots):
            named, weight = chosen(meta, (ep * plan.slots + slot).astype(F32), plan.top)
            found.append((named, weight))
            flags = jnp.where(lane == slot, named, flags)
        prefix = dot(earlier, flags.astype(BF16), ((1,), (0,)))
        places = []
        for slot, (named, weight) in enumerate(found):
            place = jnp.where(named > 0.0, prefix[:, slot : slot + 1] + start, -1.0)
            places.append((place, weight))
            end = start + jnp.sum(named, axis=0, keepdims=True)
            bounds.append((slot, start, end))
            start = end
        result.append(places)
    return result, bounds


def slot_masks(bounds, plan):
    row = lax.broadcasted_iota(jnp.int32, (1, plan.rows), 1).astype(F32) + float(plan.first)
    masks = []
    for slot in range(plan.slots):
        mask = jnp.zeros((1, plan.rows), F32)
        for which, start, end in bounds:
            if which == slot:
                mask = mask + jnp.logical_and(row >= start, row < end).astype(F32)
        masks.append(mask)
    return masks


def rows_of(places, plan):
    return (
        lax.broadcasted_iota(jnp.int32, (places.shape[0], plan.rows), 1).astype(F32)
        + float(plan.first)
        == places
    )


def metas_of(layout, refs, width):
    metas, at = [], 0
    for count in layout:
        several = [ref[:, width:].astype(F32) for ref in refs[at : at + count]]
        metas.append(jnp.concatenate(several, axis=0))
        at += count
    return metas


def rows_kernel(plan, layout, place_ref, *refs):
    arrays = sum(layout)
    tokens = refs[:arrays]
    most_ref = refs[arrays]
    outs = refs[arrays + 1 :]
    width = outs[0].shape[0]
    ep, sub = place_ref[0], place_ref[1]
    metas = metas_of(layout, tokens, width)
    columns, bounds = route(metas, plan, ep, sub)
    begin = 0
    masks = slot_masks(bounds, plan)
    for _rows, mask_ref, high_ref, low_ref in zip(*[iter(outs)] * 4):
        size = mask_ref.shape[1]
        part = plan.part(begin, size)
        mask_ref[...] = jnp.zeros_like(mask_ref)
        for slot, mask in enumerate(masks):
            mask_ref[slot : slot + 1] = mask[:, begin : begin + size]
        at = 0
        for places in columns:
            mix = None
            for place, weight in places:
                term = jnp.where(rows_of(place, part), weight, 0.0)
                mix = term if mix is None else mix + term
            high = mix.astype(BF16)
            here = slice(at, at + mix.shape[0])
            high_ref[here] = high
            low_ref[here] = (mix - high.astype(F32)).astype(BF16)
            at += mix.shape[0]
        begin += size
    hots = []
    for places in columns:
        hot = None
        for place, _weight in places:
            hit = rows_of(place, plan).astype(F32)
            hot = hit if hot is None else hot + hit
        hots.append(hot.astype(BF16))
    hot = jnp.concatenate(hots, axis=0) if len(hots) > 1 else hots[0]
    chunk = 256
    for at in range(0, width, chunk):
        end = min(at + chunk, width)
        several = [ref[:, at:end] for ref in tokens]
        total = dot(jnp.concatenate(several, axis=0), hot, ((0,), (0,)))
        begin = 0
        for rows_ref in outs[::4]:
            rows_ref[at:end] = total[:, begin : begin + rows_ref.shape[1]].astype(BF16)
            begin += rows_ref.shape[1]
    lane = lax.broadcasted_iota(jnp.int32, (metas[0].shape[0], LANES), 1).astype(F32)
    owner = lax.div(lax.broadcasted_iota(jnp.int32, (1, LANES), 1), plan.slots)
    start = [jnp.zeros((1, 1), F32)] * plan.eps
    for column, meta in enumerate(metas):
        flags = jnp.zeros((meta.shape[0], LANES), F32)
        for k in range(plan.top):
            flags = flags + (meta[:, k : k + 1] == lane).astype(F32)
        counts = jnp.sum(flags, axis=0, keepdims=True)
        for e in range(plan.eps):
            if column:
                start[e] = jnp.maximum(start[e], float(plan.holds[column - 1]))
            start[e] = start[e] + jnp.sum(
                jnp.where(owner == e, counts, 0.0), axis=1, keepdims=True
            )
    most_ref[...] = jnp.broadcast_to(functools.reduce(jnp.maximum, start), most_ref.shape)


def rows_in(plan, place, held, split=None):
    layout = tuple(len(arrays) for arrays in held)
    tokens = [t for arrays in held for t in arrays]
    width = tokens[0].shape[1] - META
    total = sum(t.shape[0] for t in tokens)
    split = split or (plan.rows,)
    shapes = [jax.ShapeDtypeStruct((8, LANES), F32)]
    for size in split:
        shapes.append(jax.ShapeDtypeStruct((width, size), BF16))
        shapes.append(jax.ShapeDtypeStruct((8, size), F32))
        shapes.append(jax.ShapeDtypeStruct((total, size), BF16))
        shapes.append(jax.ShapeDtypeStruct((total, size), BF16))
    specs = [pl.BlockSpec(shape.shape, lambda i: (0, 0)) for shape in shapes]
    return pl.pallas_call(
        functools.partial(rows_kernel, plan, layout),
        grid=(1,),
        in_specs=[pl.BlockSpec(memory_space=pltpu.SMEM)]
        + [pl.BlockSpec(t.shape, lambda i: (0, 0)) for t in tokens],
        out_specs=specs,
        out_shape=shapes,
        compiler_params=params(),
        cost_estimate=HINT,
    )(place, *tokens)


def inner_kernel(plan, rows_ref, mask_ref, weight_ref, *refs):
    act_ref, mark_ref = refs[-2:]
    gating = upward = None
    for slot in range(plan.slots):
        gate = dot(weight_ref[slot, 0], rows_ref[...], ((1,), (0,)))
        up = dot(weight_ref[slot, 1], rows_ref[...], ((1,), (0,)))
        if slot == 0:
            gating, upward = gate, up
        else:
            mine = mask_ref[slot : slot + 1] > 0.0
            gating = jnp.where(mine, gate, gating)
            upward = jnp.where(mine, up, upward)
    act_ref[...] = (gating * jax.nn.sigmoid(swish_beta * gating) * (upward + 1.0)).astype(BF16)
    mark_ref[...] = jnp.zeros_like(mark_ref)


def piece(total):
    for size in (240, 120, 72, 40, 24, 16, 8):
        if total % size == 0:
            return size
    return total


def inner(plan, rows, mask, weights, after):
    slots, _two, units, width = weights.shape
    block = piece(units)
    return pl.pallas_call(
        functools.partial(inner_kernel, plan),
        grid=(units // block,),
        in_specs=[
            pl.BlockSpec(rows.shape, lambda i: (0, 0)),
            pl.BlockSpec(mask.shape, lambda i: (0, 0)),
            pl.BlockSpec((slots, 2, block, width), lambda i: (0, 0, i, 0)),
        ]
        + [pl.BlockSpec(memory_space=pl.ANY)] * len(after),
        out_specs=[
            pl.BlockSpec((block, rows.shape[1]), lambda i: (i, 0)),
            pl.BlockSpec((8, LANES), lambda i: (0, 0)),
        ],
        out_shape=[
            jax.ShapeDtypeStruct((units, rows.shape[1]), BF16),
            jax.ShapeDtypeStruct((8, LANES), F32),
        ],
        compiler_params=params(),
        cost_estimate=HINT,
    )(rows, mask, weights, *after)


def add_blocks(plan, which, ends, sub, parts, weight_ref):
    total = None
    for at, k in enumerate(which):
        x = parts[at][...]
        if k == 3 and ends:
            inside = jnp.logical_or(sub == 1, sub == 2)
            x = jnp.where(inside, x, parts[at + 1][...])
        weights = weight_ref[0, 0 if len(which) == 1 else jnp.bitwise_xor(sub, k)]
        term = dot(weights, x, ((1,), (0,)))
        total = term if total is None else total + term
    return total


def pick(slot, plan, mask_ref, new, old_ref, here):
    @pl.when(slot == 0)
    def _():
        old_ref[here] = new.astype(old_ref.dtype)

    @pl.when(slot > 0)
    def _():
        mine = mask_ref[0:1]
        for s in range(1, plan.slots):
            mine = jnp.where(slot == s, mask_ref[s : s + 1], mine)
        old_ref[here] = jnp.where(mine > 0.0, new.astype(old_ref.dtype), old_ref[here])


def part_kernel(plan, which, place_ref, mask_ref, *refs):
    count = len(which)
    parts, weight_ref, out_ref = refs[:count], refs[count], refs[-1]
    slot, chunk = pl.program_id(0), pl.program_id(1)
    size = weight_ref.shape[2]
    here = pl.ds(pl.multiple_of(chunk * size, size), size)
    out = add_blocks(plan, which, False, place_ref[1], parts, weight_ref)
    pick(slot, plan, mask_ref, out, out_ref, here)


def outer_kernel(plan, which, ends, first, before, place_ref, mask_ref, high_ref, low_ref, *refs):
    count = len(which) + ends
    parts = refs[:count]
    first_ref = refs[count] if first else None
    befores = refs[count + first : count + first + before]
    weight_ref = refs[count + first + before]
    keep_ref, send_ref, sum_ref = refs[-3:]
    slot, chunk = pl.program_id(0), pl.program_id(1)
    size = weight_ref.shape[2]
    here = pl.ds(pl.multiple_of(chunk * size, size), size)
    out = add_blocks(plan, which, ends, place_ref[1], parts, weight_ref)
    if first:
        out = out + first_ref[here]
    pick(slot, plan, mask_ref, out, sum_ref, here)

    @pl.when(jnp.logical_and(slot == plan.slots - 1, chunk == pl.num_programs(1) - 1))
    def _():
        done = sum_ref[...]
        half = keep_ref.shape[1]
        for c in range(keep_ref.shape[0]):
            for h, ref in enumerate((keep_ref, send_ref)):
                if 2 * c * half >= high_ref.shape[0]:
                    ref[c] = jnp.zeros((half, ref.shape[2]), BF16)
                    continue
                at = slice((2 * c + h) * half, (2 * c + h + 1) * half)
                value = dot(high_ref[at], done, ((1,), (1,))) + dot(low_ref[at], done, ((1,), (1,)))
                if before and c < befores[h].shape[0]:
                    value = value + befores[h][c].astype(F32)
                ref[c] = value.astype(BF16)


def outer_call(kernel, place, operands, weights, which, after, shapes, scratch):
    slots, subs, columns_out, units = weights.shape
    size = 240 if columns_out % 240 == 0 else columns_out

    def whole(x):
        return pl.BlockSpec(x.shape, lambda i, j, p: (0,) * len(x.shape))

    if len(which) == 1:
        weight_spec = pl.BlockSpec(
            (1, 1, size, units), lambda i, j, p: (i, jnp.bitwise_xor(p[1], which[0]), j, 0)
        )
    else:
        weight_spec = pl.BlockSpec((1, subs, size, units), lambda i, j, p: (i, 0, j, 0))
    return pl.pallas_call(
        kernel,
        grid_spec=pltpu.PrefetchScalarGridSpec(
            num_scalar_prefetch=1,
            grid=(slots, columns_out // size),
            in_specs=[whole(x) for x in operands]
            + [weight_spec]
            + [pl.BlockSpec(memory_space=pl.ANY)] * len(after),
            out_specs=[whole(x) for x in shapes],
            scratch_shapes=scratch,
        ),
        out_shape=shapes,
        compiler_params=params(),
        cost_estimate=HINT,
    )(place, *operands, weights, *after)


def outer_part(plan, place, mask, parts, weights, after):
    which = tuple(range(len(parts)))
    shape = jax.ShapeDtypeStruct((weights.shape[2], parts[0].shape[1]), F32)
    kernel = functools.partial(part_kernel, plan, which)
    return outer_call(kernel, place, [mask, *parts], weights, which, after, [shape], [])[0]


def outer(plan, place, mixed, parts, befores, weights, columns, first=None):
    subs, columns_out = weights.shape[1:3]
    rows = parts[0].shape[1]
    half = plan.group * plan.subs
    which = tuple(range(subs)) if first is None else (subs - 1,)
    ends = len(parts) > len(which)
    firsts = [] if first is None else [first]
    result = jax.ShapeDtypeStruct((columns, half, columns_out), BF16)
    return outer_call(
        functools.partial(outer_kernel, plan, which, ends, len(firsts), len(befores)),
        place,
        [*mixed, *parts, *firsts, *befores],
        weights,
        which,
        (),
        [result, result],
        [pltpu.VMEM((columns_out, rows), BF16)],
    )


def finish_kernel(subs, columns, place_ref, *refs):
    out_ref = refs[-1]
    sub = place_ref[1]
    width = refs[0].shape[1]
    steps, rows, _ = out_ref.shape
    sums = []
    for k in range(subs):
        value = refs[k * columns][...].astype(F32)
        for j in range(1, columns):
            value = value + refs[k * columns + j][...].astype(F32)
        sums.append(value)
    for b in range(subs):
        value = sums[0]
        for k in range(1, subs):
            value = jnp.where(jnp.bitwise_xor(sub, k) == b, sums[k], value)
        value = value.astype(BF16)
        for s in range(steps):
            out_ref[s, :, b * width : (b + 1) * width] = value[s * rows : (s + 1) * rows]


def finish(place, parts, steps):
    subs, columns = len(parts), len(parts[0])
    rows, width = parts[0][0].shape
    return pl.pallas_call(
        functools.partial(finish_kernel, subs, columns),
        grid=(1,),
        in_specs=[pl.BlockSpec(memory_space=pltpu.SMEM)]
        + [pl.BlockSpec((rows, width), lambda i: (0, 0))] * (subs * columns),
        out_specs=pl.BlockSpec((steps, rows // steps, width * subs), lambda i: (0, 0, 0)),
        out_shape=jax.ShapeDtypeStruct((steps, rows // steps, width * subs), BF16),
        compiler_params=params(),
    )(place, *[p for several in parts for p in several])


def swap(x, axis, offset, count):
    return lax.ppermute(x, axis, [(i, i ^ offset) for i in range(count)])


def gather(x, subs):
    return [x] + [swap(x, "sub", k, subs) for k in range(1, subs)]


def gather_middle(x):
    return lax.ppermute(x, "sub", [(1, 2), (2, 1)])


def gather_ends(two):
    return lax.ppermute(two, "sub", [(2, 3), (1, 0)])


def add(a, b):
    return (a.astype(F32) + b.astype(F32)).astype(BF16)


def local(
    tokens, norm_gain, copy_ids, gate_scores, inner_codes, inner_scales, down_codes, down_scales
):
    eps, subs, groups = lax.axis_size("ep"), lax.axis_size("sub"), lax.axis_size("grp")
    slots = inner_codes.shape[0]
    steps, rows, top = copy_ids.shape
    units = inner_codes.shape[3]
    experts = eps * slots
    capacity = (3 * rows * top + 2 * experts - 1) // (2 * experts)
    columns = eps // 2
    place = jnp.stack([lax.axis_index("ep"), lax.axis_index("sub")]).astype(jnp.int32)
    group = steps * rows

    packed = pack(tokens, norm_gain, copy_ids, gate_scores)
    near = [packed] + [swap(packed, "sub", k, subs) for k in range(1, subs)]
    codes = jnp.transpose(inner_codes, (0, 2, 3, 1)).reshape(slots * 2, units, -1)
    scales = jnp.transpose(inner_scales, (0, 2, 3, 1)).reshape(slots * 2, units, -1)
    inner_weights, mark = dequant(codes, scales, packed)
    inner_weights = inner_weights.reshape(slots, 2, units, -1)
    outer_codes = jnp.transpose(down_codes, (0, 2, 1))
    outer_scales = jnp.transpose(down_scales, (0, 2, 1))
    line = columns == 2 and subs == 4
    first_across = [swap(packed, "ep", 2, eps)] if line else []
    own = join(near, [mark] + first_across)[0]
    other = swap(own, "ep", 1, eps)

    capacity_rows = group * subs * 2 // rows * slots * capacity

    def plan(first, count, holds):
        return Plan(first, count, holds, slots, subs, group, top, eps)

    if line and capacity_rows % 384 == 0:
        most = 2 * capacity_rows
        first = capacity_rows // 384 * 256
        second = capacity_rows
        last = most - first - second
        holds = (first,)
        plan0, plan1 = plan(0, first, holds), plan(first, second, holds)
        plan2 = plan(first + second, last, holds)
        pair = [own, other]
        _, rows0, *mixed0 = rows_in(plan0, place, [pair])
        act0, mark = inner(plan0, rows0, mixed0[0], inner_weights, [])
        one0, two0 = swap(act0, "sub", 1, subs), swap(act0, "sub", 2, subs)
        middle0 = gather_middle(act0)
        pieces = first_across + [swap(n, "ep", 2, eps) for n in near[1:]]
        moved = join(pieces, [mark], 4)
        everything = [pair, list(moved) + [swap(m, "ep", 1, eps) for m in moved]]
        longest, *several = rows_in(
            plan(first, second + last, holds), place, everything, (second, last)
        )
        rows1, rows2 = several[0], several[4]
        mixed1, mixed2 = several[1:4], several[5:]
        act1, _ = inner(plan1, rows1, mixed1[0], inner_weights, [])
        act1 = join([act1], [one0, two0, middle0])[0]
        one1, two1 = swap(act1, "sub", 1, subs), swap(act1, "sub", 2, subs)
        parts0 = [act0, one0, two0, middle0, gather_ends(two0)]
        for shift in range(1, groups):
            moved = lax.ppermute(
                longest, "grp", [(i, (i + shift) % groups) for i in range(groups)]
            )
            longest = jnp.maximum(longest, moved)
        outer_weights, _ = dequant(outer_codes, outer_scales, act1, subs)
        sums = outer(plan0, place, mixed0, parts0, [], outer_weights, columns)

        passed = join([act1], [two1, sums[0]])[0]
        parts1 = [gather_middle(passed), gather_ends(two1)]
        first1 = outer_part(plan1, place, mixed1[0], [act1, one1, two1], outer_weights, [passed])

        def more(kept, sent):
            act, _ = inner(plan2, rows2, mixed2[0], inner_weights, [kept])
            return tuple(
                outer(plan2, place, mixed2, gather(act, subs), [kept, sent], outer_weights, columns)
            )

        sums = lax.cond(
            longest[0, 0] > float(first + second), more, lambda a, b: (a, b), *sums
        )
        keep, send = outer(plan1, place, mixed1, parts1, sums, outer_weights, columns, first1)
    else:
        count = -(-capacity_rows // LANES) * LANES
        each = plan(0, count, ())
        outer_weights, _ = dequant(outer_codes, outer_scales, own, subs)
        keeps, sends = [], []
        across = [swap(own, "ep", 2 * j, eps) for j in range(1, columns)]
        held = [[own, other]] + [[a, swap(a, "ep", 1, eps)] for a in across]
        for pair in held:
            _, rows_here, *mixed = rows_in(each, place, [pair])
            act, _ = inner(each, rows_here, mixed[0], inner_weights, [])
            kept, sent = outer(each, place, mixed, gather(act, subs), [], outer_weights, 1)
            keeps.append(kept)
            sends.append(sent)
        keep, send = jnp.concatenate(keeps, axis=0), jnp.concatenate(sends, axis=0)

    chip = add(keep, swap(send, "ep", 1, eps))
    chip = chip.reshape(columns, subs, group, -1)
    arrived = []
    for k in range(subs):
        arrived.append([])
        for j in range(columns):
            pairs = []
            for e in range(eps):
                for z in range(subs):
                    pairs.append((e * subs + z, (e ^ (2 * j)) * subs + (z ^ k)))
            block = chip[j, k]
            arrived[-1].append(lax.ppermute(block, ("ep", "sub"), pairs) if j + k else block)
    return finish(place, arrived, steps)


def solution(mesh):
    return jax.shard_map(
        local,
        mesh=mesh,
        in_specs=(
            P(None, ("grp", "ep", "sub"), None),
            P(),
            P(None, ("grp", "ep", "sub"), None),
            P(None, ("grp", "ep", "sub"), None),
            P("ep", None, None, "sub"),
            P("ep", None, None, "sub"),
            P("ep", None, "sub"),
            P("ep", None, "sub"),
        ),
        out_specs=P(None, ("grp", "ep", "sub"), None),
        check_vma=False,
    )
```

```python
import functools

import jax
import jax.numpy as jnp
from jax import lax
from jax.experimental import pallas as pl
from jax.experimental.pallas import tpu as pltpu
from jax.sharding import PartitionSpec as P

epsilon = 1e-05
swish_beta = 1.702
META = 64
LANES = 128
VMEM_LIMIT = 24 * 1024 * 1024
HINT = pl.CostEstimate(flops=1024, bytes_accessed=1024, transcendentals=0)
F32 = jnp.float32
BF16 = jnp.bfloat16


def params():
    return pltpu.CompilerParams(vmem_limit_bytes=VMEM_LIMIT)


def in_hbm(x):
    return pltpu.with_memory_space_constraint(x, pltpu.HBM)


def dot(a, b, contract):
    return lax.dot_general(a, b, (contract, ((), ())), preferred_element_type=F32)


def pack_kernel(tokens_ref, gain_ref, ids_ref, scores_ref, out_ref):
    steps, rows, width = tokens_ref.shape
    top = ids_ref.shape[1]
    gain = gain_ref[...].reshape(1, width)
    eye = (
        lax.broadcasted_iota(jnp.int32, (rows, rows), 0)
        == lax.broadcasted_iota(jnp.int32, (rows, rows), 1)
    ).astype(F32)

    def column(row):
        return jnp.sum(eye * row, axis=1, keepdims=True)

    for s in range(steps):
        values = tokens_ref[s].astype(F32)
        mean = jnp.mean(values * values, axis=-1, keepdims=True)
        normed = (values * lax.rsqrt(mean + epsilon) * gain).astype(BF16)
        at = slice(s * rows, (s + 1) * rows)
        out_ref[at, :width] = normed
        scores = scores_ref[s]
        weights = scores / jnp.sum(scores, axis=0, keepdims=True)
        high = weights.astype(BF16)
        rest = weights - high.astype(F32)
        middle = rest.astype(BF16)
        low = (rest - middle.astype(F32)).astype(BF16)
        lane = lax.broadcasted_iota(jnp.int32, (rows, META), 1)
        meta = jnp.zeros((rows, META), F32)
        parts = (ids_ref[s].astype(F32), high.astype(F32), middle.astype(F32), low.astype(F32))
        for p, part in enumerate(parts):
            for k in range(top):
                meta = jnp.where(lane == p * top + k, column(part[k : k + 1]), meta)
        out_ref[at, width:] = meta.astype(BF16)


def pack(tokens, gain, ids, scores):
    steps, rows, width = tokens.shape
    return pl.pallas_call(
        pack_kernel,
        out_shape=jax.ShapeDtypeStruct((steps * rows, width + META), BF16),
        compiler_params=params(),
    )(
        in_hbm(tokens),
        in_hbm(gain),
        in_hbm(jnp.transpose(ids, (0, 2, 1))),
        in_hbm(jnp.transpose(scores, (0, 2, 1))),
    )


def dequant_kernel(codes_ref, scales_ref, _after_ref, out_ref, mark_ref):
    width = codes_ref.shape[2]
    scales = scales_ref[0]
    blocks = scales.shape[1]
    chunk = 256 if len(out_ref.shape) == 3 else out_ref.shape[3]
    for at in range(0, width, chunk):
        end = min(at + chunk, width)
        column = lax.broadcasted_iota(jnp.int32, (blocks, end - at), 1) + at
        block = lax.broadcasted_iota(jnp.int32, (blocks, end - at), 0)
        first = block * (width // blocks)
        inside = jnp.logical_and(column >= first, column < first + width // blocks)
        wide = dot(scales, inside.astype(F32).astype(BF16), ((1,), (0,)))
        value = (codes_ref[0, :, at:end].astype(F32) * wide).astype(BF16)
        if len(out_ref.shape) == 3:
            out_ref[0, :, at:end] = value
        else:
            out_ref[0, at // chunk] = value
    mark_ref[...] = jnp.zeros_like(mark_ref)


def dequant(codes, scales, after, pieces=1):
    count, rows, width = codes.shape
    blocks = scales.shape[2]
    shape = (count, rows, width) if pieces == 1 else (count, pieces, rows, width // pieces)
    return pl.pallas_call(
        dequant_kernel,
        grid=(count,),
        in_specs=[
            pl.BlockSpec((1, rows, width), lambda i: (i, 0, 0)),
            pl.BlockSpec((1, rows, blocks), lambda i: (i, 0, 0)),
            pl.BlockSpec(memory_space=pl.ANY),
        ],
        out_specs=[
            pl.BlockSpec((1,) + shape[1:], lambda i: (i,) + (0,) * (len(shape) - 1)),
            pl.BlockSpec((8, LANES), lambda i: (0, 0)),
        ],
        out_shape=[
            jax.ShapeDtypeStruct(shape, BF16),
            jax.ShapeDtypeStruct((8, LANES), F32),
        ],
        compiler_params=params(),
        cost_estimate=HINT,
    )(in_hbm(codes), scales, after)


def join_kernel(count, pieces, *refs):
    outs = refs[-pieces:]
    rows, size = refs[0].shape[0], outs[0].shape[0]
    for p, out_ref in enumerate(outs):
        if size >= rows:
            for k in range(size // rows):
                out_ref[k * rows : (k + 1) * rows] = refs[p * (size // rows) + k][...]
        else:
            at = p * size % rows
            out_ref[...] = refs[p * size // rows][at : at + size]


def join(parts, after, pieces=1):
    rows, width = parts[0].shape
    count = len(parts)
    size = count * rows // pieces
    return pl.pallas_call(
        functools.partial(join_kernel, count, pieces),
        grid=(1,),
        in_specs=[pl.BlockSpec((rows, width), lambda i: (0, 0))] * count
        + [pl.BlockSpec(memory_space=pl.ANY)] * len(after),
        out_specs=[pl.BlockSpec((size, width), lambda i: (0, 0))] * pieces,
        out_shape=[jax.ShapeDtypeStruct((size, width), BF16)] * pieces,
        compiler_params=params(),
        cost_estimate=HINT,
    )(*parts, *after)


class Plan:
    def __init__(self, first, rows, holds, slots, subs, group, top, eps):
        self.first, self.rows = first, rows
        self.holds = holds
        self.slots, self.subs, self.group, self.top, self.eps = slots, subs, group, top, eps

    def part(self, begin, rows):
        return Plan(
            self.first + begin, rows, self.holds, self.slots, self.subs, self.group, self.top, self.eps
        )


def chosen(meta, expert, top):
    named = jnp.zeros((meta.shape[0], 1), F32)
    weight = jnp.zeros((meta.shape[0], 1), F32)
    for k in range(top):
        at = meta.shape[1] - META + k
        hit = (meta[:, at : at + 1] == expert).astype(F32)
        total = (
            meta[:, at + top : at + top + 1]
            + meta[:, at + 2 * top : at + 2 * top + 1]
            + meta[:, at + 3 * top : at + 3 * top + 1]
        )
        named = named + hit
        weight = weight + hit * total
    return named, weight


def order_mask(count, plan, sub):
    def key(dim):
        t = lax.broadcasted_iota(jnp.int32, (count, count), dim)
        block = lax.rem(lax.div(t, plan.group), plan.subs)
        return t + (jnp.bitwise_xor(block, sub) - block) * plan.group

    return (key(1) < key(0)).astype(BF16)


def route(metas, plan, ep, sub):
    count = metas[0].shape[0]
    earlier = order_mask(count, plan, sub)
    lane = lax.broadcasted_iota(jnp.int32, (count, LANES), 1)
    start = jnp.zeros((1, 1), F32)
    result = []
    bounds = []
    for column, meta in enumerate(metas):
        if column:
            start = jnp.maximum(start, float(plan.holds[column - 1]))
        found = []
        flags = jnp.zeros((count, LANES), F32)
        for slot in range(plan.slots):
            named, weight = chosen(meta, (ep * plan.slots + slot).astype(F32), plan.top)
            found.append((named, weight))
            flags = jnp.where(lane == slot, named, flags)
        prefix = dot(earlier, flags.astype(BF16), ((1,), (0,)))
        places = []
        for slot, (named, weight) in enumerate(found):
            place = jnp.where(named > 0.0, prefix[:, slot : slot + 1] + start, -1.0)
            places.append((place, weight))
            end = start + jnp.sum(named, axis=0, keepdims=True)
            bounds.append((slot, start, end))
            start = end
        result.append(places)
    return result, bounds


def slot_masks(bounds, plan):
    row = lax.broadcasted_iota(jnp.int32, (1, plan.rows), 1).astype(F32) + float(plan.first)
    masks = []
    for slot in range(plan.slots):
        mask = jnp.zeros((1, plan.rows), F32)
        for which, start, end in bounds:
            if which == slot:
                mask = mask + jnp.logical_and(row >= start, row < end).astype(F32)
        masks.append(mask)
    return masks


def rows_of(places, plan):
    return (
        lax.broadcasted_iota(jnp.int32, (places.shape[0], plan.rows), 1).astype(F32)
        + float(plan.first)
        == places
    )


def metas_of(layout, refs, width):
    metas, at = [], 0
    for count in layout:
        several = [ref[:, width:].astype(F32) for ref in refs[at : at + count]]
        metas.append(jnp.concatenate(several, axis=0))
        at += count
    return metas


def rows_kernel(plan, layout, place_ref, *refs):
    arrays = sum(layout)
    tokens = refs[:arrays]
    most_ref = refs[arrays]
    outs = refs[arrays + 1 :]
    width = outs[0].shape[0]
    ep, sub = place_ref[0], place_ref[1]
    metas = metas_of(layout, tokens, width)
    columns, bounds = route(metas, plan, ep, sub)
    begin = 0
    masks = slot_masks(bounds, plan)
    for _rows, mask_ref, high_ref, low_ref in zip(*[iter(outs)] * 4):
        size = mask_ref.shape[1]
        part = plan.part(begin, size)
        mask_ref[...] = jnp.zeros_like(mask_ref)
        for slot, mask in enumerate(masks):
            mask_ref[slot : slot + 1] = mask[:, begin : begin + size]
        at = 0
        for places in columns:
            mix = None
            for place, weight in places:
                term = jnp.where(rows_of(place, part), weight, 0.0)
                mix = term if mix is None else mix + term
            high = mix.astype(BF16)
            here = slice(at, at + mix.shape[0])
            high_ref[here] = high
            low_ref[here] = (mix - high.astype(F32)).astype(BF16)
            at += mix.shape[0]
        begin += size
    hots = []
    for places in columns:
        hot = None
        for place, _weight in places:
            hit = rows_of(place, plan).astype(F32)
            hot = hit if hot is None else hot + hit
        hots.append(hot.astype(BF16))
    hot = jnp.concatenate(hots, axis=0) if len(hots) > 1 else hots[0]
    chunk = 256
    for at in range(0, width, chunk):
        end = min(at + chunk, width)
        several = [ref[:, at:end] for ref in tokens]
        total = dot(jnp.concatenate(several, axis=0), hot, ((0,), (0,)))
        begin = 0
        for rows_ref in outs[::4]:
            rows_ref[at:end] = total[:, begin : begin + rows_ref.shape[1]].astype(BF16)
            begin += rows_ref.shape[1]
    lane = lax.broadcasted_iota(jnp.int32, (metas[0].shape[0], LANES), 1).astype(F32)
    owner = lax.div(lax.broadcasted_iota(jnp.int32, (1, LANES), 1), plan.slots)
    start = [jnp.zeros((1, 1), F32)] * plan.eps
    for column, meta in enumerate(metas):
        flags = jnp.zeros((meta.shape[0], LANES), F32)
        for k in range(plan.top):
            flags = flags + (meta[:, k : k + 1] == lane).astype(F32)
        counts = jnp.sum(flags, axis=0, keepdims=True)
        for e in range(plan.eps):
            if column:
                start[e] = jnp.maximum(start[e], float(plan.holds[column - 1]))
            start[e] = start[e] + jnp.sum(
                jnp.where(owner == e, counts, 0.0), axis=1, keepdims=True
            )
    most_ref[...] = jnp.broadcast_to(functools.reduce(jnp.maximum, start), most_ref.shape)


def rows_in(plan, place, held, split=None):
    layout = tuple(len(arrays) for arrays in held)
    tokens = [t for arrays in held for t in arrays]
    width = tokens[0].shape[1] - META
    total = sum(t.shape[0] for t in tokens)
    split = split or (plan.rows,)
    shapes = [jax.ShapeDtypeStruct((8, LANES), F32)]
    for size in split:
        shapes.append(jax.ShapeDtypeStruct((width, size), BF16))
        shapes.append(jax.ShapeDtypeStruct((8, size), F32))
        shapes.append(jax.ShapeDtypeStruct((total, size), BF16))
        shapes.append(jax.ShapeDtypeStruct((total, size), BF16))
    specs = [pl.BlockSpec(shape.shape, lambda i: (0, 0)) for shape in shapes]
    return pl.pallas_call(
        functools.partial(rows_kernel, plan, layout),
        grid=(1,),
        in_specs=[pl.BlockSpec(memory_space=pltpu.SMEM)]
        + [pl.BlockSpec(t.shape, lambda i: (0, 0)) for t in tokens],
        out_specs=specs,
        out_shape=shapes,
        compiler_params=params(),
        cost_estimate=HINT,
    )(place, *tokens)


def inner_kernel(plan, rows_ref, mask_ref, weight_ref, *refs):
    act_ref, mark_ref = refs[-2:]
    gating = upward = None
    for slot in range(plan.slots):
        gate = dot(weight_ref[slot, 0], rows_ref[...], ((1,), (0,)))
        up = dot(weight_ref[slot, 1], rows_ref[...], ((1,), (0,)))
        if slot == 0:
            gating, upward = gate, up
        else:
            mine = mask_ref[slot : slot + 1] > 0.0
            gating = jnp.where(mine, gate, gating)
            upward = jnp.where(mine, up, upward)
    act_ref[...] = (gating * jax.nn.sigmoid(swish_beta * gating) * (upward + 1.0)).astype(BF16)
    mark_ref[...] = jnp.zeros_like(mark_ref)


def piece(total):
    for size in (240, 120, 72, 40, 24, 16, 8):
        if total % size == 0:
            return size
    return total


def inner(plan, rows, mask, weights, after):
    slots, _two, units, width = weights.shape
    block = piece(units)
    return pl.pallas_call(
        functools.partial(inner_kernel, plan),
        grid=(units // block,),
        in_specs=[
            pl.BlockSpec(rows.shape, lambda i: (0, 0)),
            pl.BlockSpec(mask.shape, lambda i: (0, 0)),
            pl.BlockSpec((slots, 2, block, width), lambda i: (0, 0, i, 0)),
        ]
        + [pl.BlockSpec(memory_space=pl.ANY)] * len(after),
        out_specs=[
            pl.BlockSpec((block, rows.shape[1]), lambda i: (i, 0)),
            pl.BlockSpec((8, LANES), lambda i: (0, 0)),
        ],
        out_shape=[
            jax.ShapeDtypeStruct((units, rows.shape[1]), BF16),
            jax.ShapeDtypeStruct((8, LANES), F32),
        ],
        compiler_params=params(),
        cost_estimate=HINT,
    )(rows, mask, weights, *after)


def add_blocks(plan, which, ends, sub, parts, weight_ref):
    total = None
    for at, k in enumerate(which):
        x = parts[at][...]
        if k == 3 and ends:
            inside = jnp.logical_or(sub == 1, sub == 2)
            x = jnp.where(inside, x, parts[at + 1][...])
        weights = weight_ref[0, 0 if len(which) == 1 else jnp.bitwise_xor(sub, k)]
        term = dot(weights, x, ((1,), (0,)))
        total = term if total is None else total + term
    return total


def pick(slot, plan, mask_ref, new, old_ref, here):
    @pl.when(slot == 0)
    def _():
        old_ref[here] = new.astype(old_ref.dtype)

    @pl.when(slot > 0)
    def _():
        mine = mask_ref[0:1]
        for s in range(1, plan.slots):
            mine = jnp.where(slot == s, mask_ref[s : s + 1], mine)
        old_ref[here] = jnp.where(mine > 0.0, new.astype(old_ref.dtype), old_ref[here])


def part_kernel(plan, which, place_ref, mask_ref, *refs):
    count = len(which)
    parts, weight_ref, out_ref = refs[:count], refs[count], refs[-1]
    slot, chunk = pl.program_id(0), pl.program_id(1)
    size = weight_ref.shape[2]
    here = pl.ds(pl.multiple_of(chunk * size, size), size)
    out = add_blocks(plan, which, False, place_ref[1], parts, weight_ref)
    pick(slot, plan, mask_ref, out, out_ref, here)


def outer_kernel(plan, which, ends, first, before, place_ref, mask_ref, high_ref, low_ref, *refs):
    count = len(which) + ends
    parts = refs[:count]
    first_ref = refs[count] if first else None
    befores = refs[count + first : count + first + before]
    weight_ref = refs[count + first + before]
    keep_ref, send_ref, sum_ref = refs[-3:]
    slot, chunk = pl.program_id(0), pl.program_id(1)
    size = weight_ref.shape[2]
    here = pl.ds(pl.multiple_of(chunk * size, size), size)
    out = add_blocks(plan, which, ends, place_ref[1], parts, weight_ref)
    if first:
        out = out + first_ref[here]
    pick(slot, plan, mask_ref, out, sum_ref, here)

    @pl.when(jnp.logical_and(slot == plan.slots - 1, chunk == pl.num_programs(1) - 1))
    def _():
        done = sum_ref[...]
        half = keep_ref.shape[1]
        for c in range(keep_ref.shape[0]):
            for h, ref in enumerate((keep_ref, send_ref)):
                if 2 * c * half >= high_ref.shape[0]:
                    ref[c] = jnp.zeros((half, ref.shape[2]), BF16)
                    continue
                at = slice((2 * c + h) * half, (2 * c + h + 1) * half)
                value = dot(high_ref[at], done, ((1,), (1,))) + dot(low_ref[at], done, ((1,), (1,)))
                if before and c < befores[h].shape[0]:
                    value = value + befores[h][c].astype(F32)
                ref[c] = value.astype(BF16)


def outer_call(kernel, place, operands, weights, which, after, shapes, scratch):
    slots, subs, columns_out, units = weights.shape
    size = 240 if columns_out % 240 == 0 else columns_out

    def whole(x):
        return pl.BlockSpec(x.shape, lambda i, j, p: (0,) * len(x.shape))

    if len(which) == 1:
        weight_spec = pl.BlockSpec(
            (1, 1, size, units), lambda i, j, p: (i, jnp.bitwise_xor(p[1], which[0]), j, 0)
        )
    else:
        weight_spec = pl.BlockSpec((1, subs, size, units), lambda i, j, p: (i, 0, j, 0))
    return pl.pallas_call(
        kernel,
        grid_spec=pltpu.PrefetchScalarGridSpec(
            num_scalar_prefetch=1,
            grid=(slots, columns_out // size),
            in_specs=[whole(x) for x in operands]
            + [weight_spec]
            + [pl.BlockSpec(memory_space=pl.ANY)] * len(after),
            out_specs=[whole(x) for x in shapes],
            scratch_shapes=scratch,
        ),
        out_shape=shapes,
        compiler_params=params(),
        cost_estimate=HINT,
    )(place, *operands, in_hbm(weights), *after)


def outer_part(plan, place, mask, parts, weights, after):
    which = tuple(range(len(parts)))
    shape = jax.ShapeDtypeStruct((weights.shape[2], parts[0].shape[1]), F32)
    kernel = functools.partial(part_kernel, plan, which)
    return outer_call(kernel, place, [mask, *parts], weights, which, after, [shape], [])[0]


def outer(plan, place, mixed, parts, befores, weights, columns, first=None):
    subs, columns_out = weights.shape[1:3]
    rows = parts[0].shape[1]
    half = plan.group * plan.subs
    which = tuple(range(subs)) if first is None else (subs - 1,)
    ends = len(parts) > len(which)
    firsts = [] if first is None else [first]
    result = jax.ShapeDtypeStruct((columns, half, columns_out), BF16)
    return outer_call(
        functools.partial(outer_kernel, plan, which, ends, len(firsts), len(befores)),
        place,
        [mixed[0], in_hbm(mixed[1]), in_hbm(mixed[2]), *parts, *firsts, *befores],
        weights,
        which,
        (),
        [result, result],
        [pltpu.VMEM((columns_out, rows), BF16)],
    )


def finish_kernel(subs, columns, place_ref, *refs):
    out_ref = refs[-1]
    sub = place_ref[1]
    width = refs[0].shape[1]
    steps, rows, _ = out_ref.shape
    sums = []
    for k in range(subs):
        value = refs[k * columns][...].astype(F32)
        for j in range(1, columns):
            value = value + refs[k * columns + j][...].astype(F32)
        sums.append(value)
    for b in range(subs):
        value = sums[0]
        for k in range(1, subs):
            value = jnp.where(jnp.bitwise_xor(sub, k) == b, sums[k], value)
        value = value.astype(BF16)
        for s in range(steps):
            out_ref[s, :, b * width : (b + 1) * width] = value[s * rows : (s + 1) * rows]


def finish(place, parts, steps):
    subs, columns = len(parts), len(parts[0])
    rows, width = parts[0][0].shape
    return pl.pallas_call(
        functools.partial(finish_kernel, subs, columns),
        grid=(1,),
        in_specs=[pl.BlockSpec(memory_space=pltpu.SMEM)]
        + [pl.BlockSpec((rows, width), lambda i: (0, 0))] * (subs * columns),
        out_specs=pl.BlockSpec((steps, rows // steps, width * subs), lambda i: (0, 0, 0)),
        out_shape=jax.ShapeDtypeStruct((steps, rows // steps, width * subs), BF16),
        compiler_params=params(),
    )(place, *[p for several in parts for p in several])


def swap(x, axis, offset, count):
    return lax.ppermute(x, axis, [(i, i ^ offset) for i in range(count)])


def gather(x, subs):
    return [x] + [swap(x, "sub", k, subs) for k in range(1, subs)]


def gather_middle(x):
    return lax.ppermute(x, "sub", [(1, 2), (2, 1)])


def gather_ends(two):
    return lax.ppermute(two, "sub", [(2, 3), (1, 0)])


def add(a, b):
    return (a.astype(F32) + b.astype(F32)).astype(BF16)


def local(
    tokens, norm_gain, copy_ids, gate_scores, inner_codes, inner_scales, down_codes, down_scales
):
    eps, subs, groups = lax.axis_size("ep"), lax.axis_size("sub"), lax.axis_size("grp")
    slots = inner_codes.shape[0]
    steps, rows, top = copy_ids.shape
    units = inner_codes.shape[3]
    experts = eps * slots
    capacity = (3 * rows * top + 2 * experts - 1) // (2 * experts)
    columns = eps // 2
    place = jnp.stack([lax.axis_index("ep"), lax.axis_index("sub")]).astype(jnp.int32)
    group = steps * rows

    packed = pack(tokens, norm_gain, copy_ids, gate_scores)
    near = [packed] + [swap(packed, "sub", k, subs) for k in range(1, subs)]
    codes = jnp.transpose(inner_codes, (0, 2, 3, 1)).reshape(slots * 2, units, -1)
    scales = jnp.transpose(inner_scales, (0, 2, 3, 1)).reshape(slots * 2, units, -1)
    inner_weights, mark = dequant(codes, scales, packed)
    inner_weights = inner_weights.reshape(slots, 2, units, -1)
    outer_codes = jnp.transpose(down_codes, (0, 2, 1))
    outer_scales = jnp.transpose(down_scales, (0, 2, 1))
    line = columns == 2 and subs == 4
    first_across = [swap(packed, "ep", 2, eps)] if line else []
    own = join(near, [mark] + first_across)[0]
    other = swap(own, "ep", 1, eps)

    capacity_rows = group * subs * 2 // rows * slots * capacity

    def plan(first, count, holds):
        return Plan(first, count, holds, slots, subs, group, top, eps)

    if line and capacity_rows % 384 == 0:
        most = 2 * capacity_rows
        first = capacity_rows // 384 * 256
        second = capacity_rows
        last = most - first - second
        holds = (first,)
        plan0, plan1 = plan(0, first, holds), plan(first, second, holds)
        plan2 = plan(first + second, last, holds)
        pair = [own, other]
        _, rows0, *mixed0 = rows_in(plan0, place, [pair])
        act0, mark = inner(plan0, rows0, mixed0[0], inner_weights, [])
        one0, two0 = swap(act0, "sub", 1, subs), swap(act0, "sub", 2, subs)
        middle0 = gather_middle(act0)
        pieces = first_across + [swap(n, "ep", 2, eps) for n in near[1:]]
        moved = join(pieces, [mark], 4)
        everything = [pair, list(moved) + [swap(m, "ep", 1, eps) for m in moved]]
        longest, *several = rows_in(
            plan(first, second + last, holds), place, everything, (second, last)
        )
        rows1, rows2 = several[0], several[4]
        mixed1, mixed2 = several[1:4], several[5:]
        act1, _ = inner(plan1, rows1, mixed1[0], inner_weights, [])
        act1 = join([act1], [one0, two0, middle0])[0]
        one1, two1 = swap(act1, "sub", 1, subs), swap(act1, "sub", 2, subs)
        parts0 = [act0, one0, two0, middle0, gather_ends(two0)]
        for shift in range(1, groups):
            moved = lax.ppermute(
                longest, "grp", [(i, (i + shift) % groups) for i in range(groups)]
            )
            longest = jnp.maximum(longest, moved)
        outer_weights, _ = dequant(outer_codes, outer_scales, act1, subs)
        sums = outer(plan0, place, mixed0, parts0, [], outer_weights, columns)

        passed = join([act1], [two1, sums[0]])[0]
        parts1 = [gather_middle(passed), gather_ends(two1)]
        first1 = outer_part(plan1, place, mixed1[0], [act1, one1, two1], outer_weights, [passed])

        def more(kept, sent):
            act, _ = inner(plan2, rows2, mixed2[0], inner_weights, [kept])
            return tuple(
                outer(plan2, place, mixed2, gather(act, subs), [kept, sent], outer_weights, columns)
            )

        sums = lax.cond(
            longest[0, 0] > float(first + second), more, lambda a, b: (a, b), *sums
        )
        keep, send = outer(plan1, place, mixed1, parts1, sums, outer_weights, columns, first1)
    else:
        count = -(-capacity_rows // LANES) * LANES
        each = plan(0, count, ())
        outer_weights, _ = dequant(outer_codes, outer_scales, own, subs)
        keeps, sends = [], []
        across = [swap(own, "ep", 2 * j, eps) for j in range(1, columns)]
        held = [[own, other]] + [[a, swap(a, "ep", 1, eps)] for a in across]
        for pair in held:
            _, rows_here, *mixed = rows_in(each, place, [pair])
            act, _ = inner(each, rows_here, mixed[0], inner_weights, [])
            kept, sent = outer(each, place, mixed, gather(act, subs), [], outer_weights, 1)
            keeps.append(kept)
            sends.append(sent)
        keep, send = jnp.concatenate(keeps, axis=0), jnp.concatenate(sends, axis=0)

    chip = add(keep, swap(send, "ep", 1, eps))
    chip = chip.reshape(columns, subs, group, -1)
    arrived = []
    for k in range(subs):
        arrived.append([])
        for j in range(columns):
            pairs = []
            for e in range(eps):
                for z in range(subs):
                    pairs.append((e * subs + z, (e ^ (2 * j)) * subs + (z ^ k)))
            block = chip[j, k]
            arrived[-1].append(lax.ppermute(block, ("ep", "sub"), pairs) if j + k else block)
    return finish(place, arrived, steps)


def solution(mesh):
    return jax.shard_map(
        local,
        mesh=mesh,
        in_specs=(
            P(None, ("grp", "ep", "sub"), None),
            P(),
            P(None, ("grp", "ep", "sub"), None),
            P(None, ("grp", "ep", "sub"), None),
            P("ep", None, None, "sub"),
            P("ep", None, None, "sub"),
            P("ep", None, "sub"),
            P("ep", None, "sub"),
        ),
        out_specs=P(None, ("grp", "ep", "sub"), None),
        check_vma=False,
    )
```

```python
import functools

import jax
import jax.numpy as jnp
from jax import lax
from jax.experimental import pallas as pl
from jax.experimental.pallas import tpu as pltpu
from jax.sharding import PartitionSpec as P

epsilon = 1e-05
swish_beta = 1.702
META = 64
LANES = 128
VMEM_LIMIT = 24 * 1024 * 1024
HINT = pl.CostEstimate(flops=1024, bytes_accessed=1024, transcendentals=0)
F32 = jnp.float32
BF16 = jnp.bfloat16


def params():
    return pltpu.CompilerParams(vmem_limit_bytes=VMEM_LIMIT)


def in_hbm(x):
    return pltpu.with_memory_space_constraint(x, pltpu.HBM)


def dot(a, b, contract):
    return lax.dot_general(a, b, (contract, ((), ())), preferred_element_type=F32)


def pack_kernel(tokens_ref, gain_ref, ids_ref, scores_ref, out_ref):
    steps, rows, width = tokens_ref.shape
    top = ids_ref.shape[1]
    gain = gain_ref[...].reshape(1, width)
    eye = (
        lax.broadcasted_iota(jnp.int32, (rows, rows), 0)
        == lax.broadcasted_iota(jnp.int32, (rows, rows), 1)
    ).astype(F32)

    def column(row):
        return jnp.sum(eye * row, axis=1, keepdims=True)

    for s in range(steps):
        values = tokens_ref[s].astype(F32)
        mean = jnp.mean(values * values, axis=-1, keepdims=True)
        normed = (values * lax.rsqrt(mean + epsilon) * gain).astype(BF16)
        at = slice(s * rows, (s + 1) * rows)
        out_ref[at, :width] = normed
        scores = scores_ref[s]
        weights = scores / jnp.sum(scores, axis=0, keepdims=True)
        high = weights.astype(BF16)
        rest = weights - high.astype(F32)
        middle = rest.astype(BF16)
        low = (rest - middle.astype(F32)).astype(BF16)
        lane = lax.broadcasted_iota(jnp.int32, (rows, META), 1)
        meta = jnp.zeros((rows, META), F32)
        parts = (ids_ref[s].astype(F32), high.astype(F32), middle.astype(F32), low.astype(F32))
        for p, part in enumerate(parts):
            for k in range(top):
                meta = jnp.where(lane == p * top + k, column(part[k : k + 1]), meta)
        out_ref[at, width:] = meta.astype(BF16)


def pack(tokens, gain, ids, scores):
    steps, rows, width = tokens.shape
    return pl.pallas_call(
        pack_kernel,
        out_shape=jax.ShapeDtypeStruct((steps * rows, width + META), BF16),
        compiler_params=params(),
    )(
        in_hbm(tokens),
        in_hbm(gain),
        in_hbm(jnp.transpose(ids, (0, 2, 1))),
        in_hbm(jnp.transpose(scores, (0, 2, 1))),
    )


def dequant_kernel(codes_ref, scales_ref, _after_ref, out_ref, mark_ref):
    width = codes_ref.shape[2]
    scales = scales_ref[0]
    blocks = scales.shape[1]
    chunk = 256 if len(out_ref.shape) == 3 else out_ref.shape[3]
    for at in range(0, width, chunk):
        end = min(at + chunk, width)
        column = lax.broadcasted_iota(jnp.int32, (blocks, end - at), 1) + at
        block = lax.broadcasted_iota(jnp.int32, (blocks, end - at), 0)
        first = block * (width // blocks)
        inside = jnp.logical_and(column >= first, column < first + width // blocks)
        wide = dot(scales, inside.astype(F32).astype(BF16), ((1,), (0,)))
        value = (codes_ref[0, :, at:end].astype(F32) * wide).astype(BF16)
        if len(out_ref.shape) == 3:
            out_ref[0, :, at:end] = value
        else:
            out_ref[0, at // chunk] = value
    mark_ref[...] = jnp.zeros_like(mark_ref)


def dequant(codes, scales, after, pieces=1):
    count, rows, width = codes.shape
    blocks = scales.shape[2]
    shape = (count, rows, width) if pieces == 1 else (count, pieces, rows, width // pieces)
    return pl.pallas_call(
        dequant_kernel,
        grid=(count,),
        in_specs=[
            pl.BlockSpec((1, rows, width), lambda i: (i, 0, 0)),
            pl.BlockSpec((1, rows, blocks), lambda i: (i, 0, 0)),
            pl.BlockSpec(memory_space=pl.ANY),
        ],
        out_specs=[
            pl.BlockSpec((1,) + shape[1:], lambda i: (i,) + (0,) * (len(shape) - 1)),
            pl.BlockSpec((8, LANES), lambda i: (0, 0)),
        ],
        out_shape=[
            jax.ShapeDtypeStruct(shape, BF16),
            jax.ShapeDtypeStruct((8, LANES), F32),
        ],
        compiler_params=params(),
        cost_estimate=HINT,
    )(in_hbm(codes), scales, after)


def join_kernel(count, pieces, *refs):
    outs = refs[-pieces:]
    rows, size = refs[0].shape[0], outs[0].shape[0]
    for p, out_ref in enumerate(outs):
        if size >= rows:
            for k in range(size // rows):
                out_ref[k * rows : (k + 1) * rows] = refs[p * (size // rows) + k][...]
        else:
            at = p * size % rows
            out_ref[...] = refs[p * size // rows][at : at + size]


def join(parts, after, pieces=1):
    rows, width = parts[0].shape
    count = len(parts)
    size = count * rows // pieces
    return pl.pallas_call(
        functools.partial(join_kernel, count, pieces),
        grid=(1,),
        in_specs=[pl.BlockSpec((rows, width), lambda i: (0, 0))] * count
        + [pl.BlockSpec(memory_space=pl.ANY)] * len(after),
        out_specs=[pl.BlockSpec((size, width), lambda i: (0, 0))] * pieces,
        out_shape=[jax.ShapeDtypeStruct((size, width), BF16)] * pieces,
        compiler_params=params(),
        cost_estimate=HINT,
    )(*parts, *after)


class Plan:
    def __init__(self, first, rows, holds, slots, subs, group, top, eps):
        self.first, self.rows = first, rows
        self.holds = holds
        self.slots, self.subs, self.group, self.top, self.eps = slots, subs, group, top, eps

    def part(self, begin, rows):
        return Plan(
            self.first + begin, rows, self.holds, self.slots, self.subs, self.group, self.top, self.eps
        )


def chosen(meta, expert, top):
    named = jnp.zeros((meta.shape[0], 1), F32)
    weight = jnp.zeros((meta.shape[0], 1), F32)
    for k in range(top):
        at = meta.shape[1] - META + k
        hit = (meta[:, at : at + 1] == expert).astype(F32)
        total = (
            meta[:, at + top : at + top + 1]
            + meta[:, at + 2 * top : at + 2 * top + 1]
            + meta[:, at + 3 * top : at + 3 * top + 1]
        )
        named = named + hit
        weight = weight + hit * total
    return named, weight


def order_mask(count, plan, sub):
    def key(dim):
        t = lax.broadcasted_iota(jnp.int32, (count, count), dim)
        block = lax.rem(lax.div(t, plan.group), plan.subs)
        return t + (jnp.bitwise_xor(block, sub) - block) * plan.group

    return (key(1) < key(0)).astype(BF16)


def route(metas, plan, ep, sub):
    count = metas[0].shape[0]
    earlier = order_mask(count, plan, sub)
    lane = lax.broadcasted_iota(jnp.int32, (count, LANES), 1)
    start = jnp.zeros((1, 1), F32)
    result = []
    bounds = []
    for column, meta in enumerate(metas):
        if column:
            start = jnp.maximum(start, float(plan.holds[column - 1]))
        found = []
        flags = jnp.zeros((count, LANES), F32)
        for slot in range(plan.slots):
            named, weight = chosen(meta, (ep * plan.slots + slot).astype(F32), plan.top)
            found.append((named, weight))
            flags = jnp.where(lane == slot, named, flags)
        prefix = dot(earlier, flags.astype(BF16), ((1,), (0,)))
        places = []
        for slot, (named, weight) in enumerate(found):
            place = jnp.where(named > 0.0, prefix[:, slot : slot + 1] + start, -1.0)
            places.append((place, weight))
            end = start + jnp.sum(named, axis=0, keepdims=True)
            bounds.append((slot, start, end))
            start = end
        result.append(places)
    return result, bounds


def slot_masks(bounds, plan):
    row = lax.broadcasted_iota(jnp.int32, (1, plan.rows), 1).astype(F32) + float(plan.first)
    masks = []
    for slot in range(plan.slots):
        mask = jnp.zeros((1, plan.rows), F32)
        for which, start, end in bounds:
            if which == slot:
                mask = mask + jnp.logical_and(row >= start, row < end).astype(F32)
        masks.append(mask)
    return masks


def rows_of(places, plan):
    return (
        lax.broadcasted_iota(jnp.int32, (places.shape[0], plan.rows), 1).astype(F32)
        + float(plan.first)
        == places
    )


def metas_of(layout, refs, width):
    metas, at = [], 0
    for count in layout:
        several = [ref[:, width:].astype(F32) for ref in refs[at : at + count]]
        metas.append(jnp.concatenate(several, axis=0))
        at += count
    return metas


def rows_kernel(plan, layout, place_ref, *refs):
    arrays = sum(layout)
    tokens = refs[:arrays]
    most_ref = refs[arrays]
    outs = refs[arrays + 1 :]
    width = outs[0].shape[0]
    ep, sub = place_ref[0], place_ref[1]
    metas = metas_of(layout, tokens, width)
    columns, bounds = route(metas, plan, ep, sub)
    begin = 0
    masks = slot_masks(bounds, plan)
    for _rows, mask_ref, high_ref, low_ref in zip(*[iter(outs)] * 4):
        size = mask_ref.shape[1]
        part = plan.part(begin, size)
        mask_ref[...] = jnp.zeros_like(mask_ref)
        for slot, mask in enumerate(masks):
            mask_ref[slot : slot + 1] = mask[:, begin : begin + size]
        at = 0
        for places in columns:
            mix = None
            for place, weight in places:
                term = jnp.where(rows_of(place, part), weight, 0.0)
                mix = term if mix is None else mix + term
            high = mix.astype(BF16)
            here = slice(at, at + mix.shape[0])
            high_ref[here] = high
            low_ref[here] = (mix - high.astype(F32)).astype(BF16)
            at += mix.shape[0]
        begin += size
    hots = []
    for places in columns:
        hot = None
        for place, _weight in places:
            hit = rows_of(place, plan).astype(F32)
            hot = hit if hot is None else hot + hit
        hots.append(hot.astype(BF16))
    hot = jnp.concatenate(hots, axis=0) if len(hots) > 1 else hots[0]
    chunk = 256
    for at in range(0, width, chunk):
        end = min(at + chunk, width)
        several = [ref[:, at:end] for ref in tokens]
        total = dot(jnp.concatenate(several, axis=0), hot, ((0,), (0,)))
        begin = 0
        for rows_ref in outs[::4]:
            rows_ref[at:end] = total[:, begin : begin + rows_ref.shape[1]].astype(BF16)
            begin += rows_ref.shape[1]
    lane = lax.broadcasted_iota(jnp.int32, (metas[0].shape[0], LANES), 1).astype(F32)
    owner = lax.div(lax.broadcasted_iota(jnp.int32, (1, LANES), 1), plan.slots)
    start = [jnp.zeros((1, 1), F32)] * plan.eps
    for column, meta in enumerate(metas):
        flags = jnp.zeros((meta.shape[0], LANES), F32)
        for k in range(plan.top):
            flags = flags + (meta[:, k : k + 1] == lane).astype(F32)
        counts = jnp.sum(flags, axis=0, keepdims=True)
        for e in range(plan.eps):
            if column:
                start[e] = jnp.maximum(start[e], float(plan.holds[column - 1]))
            start[e] = start[e] + jnp.sum(
                jnp.where(owner == e, counts, 0.0), axis=1, keepdims=True
            )
    most_ref[...] = jnp.broadcast_to(functools.reduce(jnp.maximum, start), most_ref.shape)


def rows_in(plan, place, held, split=None):
    layout = tuple(len(arrays) for arrays in held)
    tokens = [t for arrays in held for t in arrays]
    width = tokens[0].shape[1] - META
    total = sum(t.shape[0] for t in tokens)
    split = split or (plan.rows,)
    shapes = [jax.ShapeDtypeStruct((8, LANES), F32)]
    for size in split:
        shapes.append(jax.ShapeDtypeStruct((width, size), BF16))
        shapes.append(jax.ShapeDtypeStruct((8, size), F32))
        shapes.append(jax.ShapeDtypeStruct((total, size), BF16))
        shapes.append(jax.ShapeDtypeStruct((total, size), BF16))
    specs = [pl.BlockSpec(shape.shape, lambda i: (0, 0)) for shape in shapes]
    return pl.pallas_call(
        functools.partial(rows_kernel, plan, layout),
        grid=(1,),
        in_specs=[pl.BlockSpec(memory_space=pltpu.SMEM)]
        + [pl.BlockSpec(t.shape, lambda i: (0, 0)) for t in tokens],
        out_specs=specs,
        out_shape=shapes,
        compiler_params=params(),
        cost_estimate=HINT,
    )(place, *tokens)


def inner_kernel(plan, rows_ref, mask_ref, weight_ref, *refs):
    act_ref, mark_ref = refs[-2:]
    gating = upward = None
    for slot in range(plan.slots):
        gate = dot(weight_ref[slot, 0], rows_ref[...], ((1,), (0,)))
        up = dot(weight_ref[slot, 1], rows_ref[...], ((1,), (0,)))
        if slot == 0:
            gating, upward = gate, up
        else:
            mine = mask_ref[slot : slot + 1] > 0.0
            gating = jnp.where(mine, gate, gating)
            upward = jnp.where(mine, up, upward)
    act_ref[...] = (gating * jax.nn.sigmoid(swish_beta * gating) * (upward + 1.0)).astype(BF16)
    mark_ref[...] = jnp.zeros_like(mark_ref)


def piece(total):
    for size in (240, 120, 72, 40, 24, 16, 8):
        if total % size == 0:
            return size
    return total


def inner(plan, rows, mask, weights, after):
    slots, _two, units, width = weights.shape
    block = piece(units)
    return pl.pallas_call(
        functools.partial(inner_kernel, plan),
        grid=(units // block,),
        in_specs=[
            pl.BlockSpec(rows.shape, lambda i: (0, 0)),
            pl.BlockSpec(mask.shape, lambda i: (0, 0)),
            pl.BlockSpec((slots, 2, block, width), lambda i: (0, 0, i, 0)),
        ]
        + [pl.BlockSpec(memory_space=pl.ANY)] * len(after),
        out_specs=[
            pl.BlockSpec((block, rows.shape[1]), lambda i: (i, 0)),
            pl.BlockSpec((8, LANES), lambda i: (0, 0)),
        ],
        out_shape=[
            jax.ShapeDtypeStruct((units, rows.shape[1]), BF16),
            jax.ShapeDtypeStruct((8, LANES), F32),
        ],
        compiler_params=params(),
        cost_estimate=HINT,
    )(rows, mask, weights, *after)


def add_blocks(plan, which, ends, sub, parts, weight_ref):
    total = None
    for at, k in enumerate(which):
        x = parts[at][...]
        if k == 3 and ends:
            inside = jnp.logical_or(sub == 1, sub == 2)
            x = jnp.where(inside, x, parts[at + 1][...])
        weights = weight_ref[0, 0 if len(which) == 1 else jnp.bitwise_xor(sub, k)]
        term = dot(weights, x, ((1,), (0,)))
        total = term if total is None else total + term
    return total


def pick(slot, plan, mask_ref, new, old_ref, here):
    @pl.when(slot == 0)
    def _():
        old_ref[here] = new.astype(old_ref.dtype)

    @pl.when(slot > 0)
    def _():
        mine = mask_ref[0:1]
        for s in range(1, plan.slots):
            mine = jnp.where(slot == s, mask_ref[s : s + 1], mine)
        old_ref[here] = jnp.where(mine > 0.0, new.astype(old_ref.dtype), old_ref[here])


def part_kernel(plan, which, place_ref, mask_ref, *refs):
    count = len(which)
    parts, weight_ref, out_ref = refs[:count], refs[count], refs[-1]
    slot, chunk = pl.program_id(0), pl.program_id(1)
    size = weight_ref.shape[2]
    here = pl.ds(pl.multiple_of(chunk * size, size), size)
    out = add_blocks(plan, which, False, place_ref[1], parts, weight_ref)
    pick(slot, plan, mask_ref, out, out_ref, here)


def outer_kernel(plan, which, ends, first, before, place_ref, mask_ref, high_ref, low_ref, *refs):
    count = len(which) + ends
    parts = refs[:count]
    first_ref = refs[count] if first else None
    befores = refs[count + first : count + first + before]
    weight_ref = refs[count + first + before]
    keep_ref, send_ref, sum_ref = refs[-3:]
    slot, chunk = pl.program_id(0), pl.program_id(1)
    size = weight_ref.shape[2]
    here = pl.ds(pl.multiple_of(chunk * size, size), size)
    out = add_blocks(plan, which, ends, place_ref[1], parts, weight_ref)
    if first:
        out = out + first_ref[here]
    pick(slot, plan, mask_ref, out, sum_ref, here)

    @pl.when(jnp.logical_and(slot == plan.slots - 1, chunk == pl.num_programs(1) - 1))
    def _():
        done = sum_ref[...]
        half = keep_ref.shape[1]
        for c in range(keep_ref.shape[0]):
            for h, ref in enumerate((keep_ref, send_ref)):
                if 2 * c * half >= high_ref.shape[0]:
                    ref[c] = jnp.zeros((half, ref.shape[2]), BF16)
                    continue
                at = slice((2 * c + h) * half, (2 * c + h + 1) * half)
                value = dot(high_ref[at], done, ((1,), (1,))) + dot(low_ref[at], done, ((1,), (1,)))
                if before and c < befores[h].shape[0]:
                    value = value + befores[h][c].astype(F32)
                ref[c] = value.astype(BF16)


def outer_call(kernel, place, operands, weights, which, after, shapes, scratch):
    slots, subs, columns_out, units = weights.shape
    size = 240 if columns_out % 240 == 0 else columns_out

    def whole(x):
        return pl.BlockSpec(x.shape, lambda i, j, p: (0,) * len(x.shape))

    if len(which) == 1:
        weight_spec = pl.BlockSpec(
            (1, 1, size, units), lambda i, j, p: (i, jnp.bitwise_xor(p[1], which[0]), j, 0)
        )
    else:
        weight_spec = pl.BlockSpec((1, subs, size, units), lambda i, j, p: (i, 0, j, 0))
    return pl.pallas_call(
        kernel,
        grid_spec=pltpu.PrefetchScalarGridSpec(
            num_scalar_prefetch=1,
            grid=(slots, columns_out // size),
            in_specs=[whole(x) for x in operands]
            + [weight_spec]
            + [pl.BlockSpec(memory_space=pl.ANY)] * len(after),
            out_specs=[whole(x) for x in shapes],
            scratch_shapes=scratch,
        ),
        out_shape=shapes,
        compiler_params=params(),
        cost_estimate=HINT,
    )(place, *operands, weights, *after)


def outer_part(plan, place, mask, parts, weights, after):
    which = tuple(range(len(parts)))
    shape = jax.ShapeDtypeStruct((weights.shape[2], parts[0].shape[1]), F32)
    kernel = functools.partial(part_kernel, plan, which)
    return outer_call(kernel, place, [mask, *parts], weights, which, after, [shape], [])[0]


def outer(plan, place, mixed, parts, befores, weights, columns, first=None):
    subs, columns_out = weights.shape[1:3]
    rows = parts[0].shape[1]
    half = plan.group * plan.subs
    which = tuple(range(subs)) if first is None else (subs - 1,)
    ends = len(parts) > len(which)
    firsts = [] if first is None else [first]
    result = jax.ShapeDtypeStruct((columns, half, columns_out), BF16)
    return outer_call(
        functools.partial(outer_kernel, plan, which, ends, len(firsts), len(befores)),
        place,
        [mixed[0], in_hbm(mixed[1]), in_hbm(mixed[2]), *parts, *firsts, *befores],
        weights,
        which,
        (),
        [result, result],
        [pltpu.VMEM((columns_out, rows), BF16)],
    )


def finish_kernel(subs, columns, place_ref, *refs):
    out_ref = refs[-1]
    sub = place_ref[1]
    width = refs[0].shape[1]
    steps, rows, _ = out_ref.shape
    sums = []
    for k in range(subs):
        value = refs[k * columns][...].astype(F32)
        for j in range(1, columns):
            value = value + refs[k * columns + j][...].astype(F32)
        sums.append(value)
    for b in range(subs):
        value = sums[0]
        for k in range(1, subs):
            value = jnp.where(jnp.bitwise_xor(sub, k) == b, sums[k], value)
        value = value.astype(BF16)
        for s in range(steps):
            out_ref[s, :, b * width : (b + 1) * width] = value[s * rows : (s + 1) * rows]


def finish(place, parts, steps):
    subs, columns = len(parts), len(parts[0])
    rows, width = parts[0][0].shape
    return pl.pallas_call(
        functools.partial(finish_kernel, subs, columns),
        grid=(1,),
        in_specs=[pl.BlockSpec(memory_space=pltpu.SMEM)]
        + [pl.BlockSpec((rows, width), lambda i: (0, 0))] * (subs * columns),
        out_specs=pl.BlockSpec((steps, rows // steps, width * subs), lambda i: (0, 0, 0)),
        out_shape=jax.ShapeDtypeStruct((steps, rows // steps, width * subs), BF16),
        compiler_params=params(),
    )(place, *[p for several in parts for p in several])


def swap(x, axis, offset, count):
    return lax.ppermute(x, axis, [(i, i ^ offset) for i in range(count)])


def gather(x, subs):
    return [x] + [swap(x, "sub", k, subs) for k in range(1, subs)]


def gather_middle(x):
    return lax.ppermute(x, "sub", [(1, 2), (2, 1)])


def gather_ends(two):
    return lax.ppermute(two, "sub", [(2, 3), (1, 0)])


def add(a, b):
    return (a.astype(F32) + b.astype(F32)).astype(BF16)


def local(
    tokens, norm_gain, copy_ids, gate_scores, inner_codes, inner_scales, down_codes, down_scales
):
    eps, subs, groups = lax.axis_size("ep"), lax.axis_size("sub"), lax.axis_size("grp")
    slots = inner_codes.shape[0]
    steps, rows, top = copy_ids.shape
    units = inner_codes.shape[3]
    experts = eps * slots
    capacity = (3 * rows * top + 2 * experts - 1) // (2 * experts)
    columns = eps // 2
    place = jnp.stack([lax.axis_index("ep"), lax.axis_index("sub")]).astype(jnp.int32)
    group = steps * rows

    packed = pack(tokens, norm_gain, copy_ids, gate_scores)
    near = [packed] + [swap(packed, "sub", k, subs) for k in range(1, subs)]
    codes = jnp.transpose(inner_codes, (0, 2, 3, 1)).reshape(slots * 2, units, -1)
    scales = jnp.transpose(inner_scales, (0, 2, 3, 1)).reshape(slots * 2, units, -1)
    inner_weights, mark = dequant(codes, scales, packed)
    inner_weights = inner_weights.reshape(slots, 2, units, -1)
    outer_codes = jnp.transpose(down_codes, (0, 2, 1))
    outer_scales = jnp.transpose(down_scales, (0, 2, 1))
    line = columns == 2 and subs == 4
    first_across = [swap(packed, "ep", 2, eps)] if line else []
    own = join(near, [mark] + first_across)[0]
    other = swap(own, "ep", 1, eps)

    capacity_rows = group * subs * 2 // rows * slots * capacity

    def plan(first, count, holds):
        return Plan(first, count, holds, slots, subs, group, top, eps)

    if line and capacity_rows % 384 == 0:
        most = 2 * capacity_rows
        first = capacity_rows // 384 * 256
        second = capacity_rows
        last = most - first - second
        holds = (first,)
        plan0, plan1 = plan(0, first, holds), plan(first, second, holds)
        plan2 = plan(first + second, last, holds)
        pair = [own, other]
        _, rows0, *mixed0 = rows_in(plan0, place, [pair])
        act0, mark = inner(plan0, rows0, mixed0[0], inner_weights, [])
        one0, two0 = swap(act0, "sub", 1, subs), swap(act0, "sub", 2, subs)
        middle0 = gather_middle(act0)
        pieces = first_across + [swap(n, "ep", 2, eps) for n in near[1:]]
        moved = join(pieces, [mark], 4)
        everything = [pair, list(moved) + [swap(m, "ep", 1, eps) for m in moved]]
        longest, *several = rows_in(
            plan(first, second + last, holds), place, everything, (second, last)
        )
        rows1, rows2 = several[0], several[4]
        mixed1, mixed2 = several[1:4], several[5:]
        act1, _ = inner(plan1, rows1, mixed1[0], inner_weights, [])
        act1 = join([act1], [one0, two0, middle0])[0]
        one1, two1 = swap(act1, "sub", 1, subs), swap(act1, "sub", 2, subs)
        parts0 = [act0, one0, two0, middle0, gather_ends(two0)]
        for shift in range(1, groups):
            moved = lax.ppermute(
                longest, "grp", [(i, (i + shift) % groups) for i in range(groups)]
            )
            longest = jnp.maximum(longest, moved)
        outer_weights, _ = dequant(outer_codes, outer_scales, act1, subs)
        sums = outer(plan0, place, mixed0, parts0, [], outer_weights, columns)

        passed = join([act1], [two1, sums[0]])[0]
        parts1 = [gather_middle(passed), gather_ends(two1)]
        first1 = outer_part(plan1, place, mixed1[0], [act1, one1, two1], outer_weights, [passed])

        def more(kept, sent):
            act, _ = inner(plan2, rows2, mixed2[0], inner_weights, [kept])
            return tuple(
                outer(plan2, place, mixed2, gather(act, subs), [kept, sent], outer_weights, columns)
            )

        sums = lax.cond(
            longest[0, 0] > float(first + second), more, lambda a, b: (a, b), *sums
        )
        keep, send = outer(plan1, place, mixed1, parts1, sums, outer_weights, columns, first1)
    else:
        count = -(-capacity_rows // LANES) * LANES
        each = plan(0, count, ())
        outer_weights, _ = dequant(outer_codes, outer_scales, own, subs)
        keeps, sends = [], []
        across = [swap(own, "ep", 2 * j, eps) for j in range(1, columns)]
        held = [[own, other]] + [[a, swap(a, "ep", 1, eps)] for a in across]
        for pair in held:
            _, rows_here, *mixed = rows_in(each, place, [pair])
            act, _ = inner(each, rows_here, mixed[0], inner_weights, [])
            kept, sent = outer(each, place, mixed, gather(act, subs), [], outer_weights, 1)
            keeps.append(kept)
            sends.append(sent)
        keep, send = jnp.concatenate(keeps, axis=0), jnp.concatenate(sends, axis=0)

    chip = add(keep, swap(send, "ep", 1, eps))
    chip = chip.reshape(columns, subs, group, -1)
    arrived = []
    for k in range(subs):
        arrived.append([])
        for j in range(columns):
            pairs = []
            for e in range(eps):
                for z in range(subs):
                    pairs.append((e * subs + z, (e ^ (2 * j)) * subs + (z ^ k)))
            block = chip[j, k]
            arrived[-1].append(lax.ppermute(block, ("ep", "sub"), pairs) if j + k else block)
    return finish(place, arrived, steps)


def solution(mesh):
    return jax.shard_map(
        local,
        mesh=mesh,
        in_specs=(
            P(None, ("grp", "ep", "sub"), None),
            P(),
            P(None, ("grp", "ep", "sub"), None),
            P(None, ("grp", "ep", "sub"), None),
            P("ep", None, None, "sub"),
            P("ep", None, None, "sub"),
            P("ep", None, "sub"),
            P("ep", None, "sub"),
        ),
        out_specs=P(None, ("grp", "ep", "sub"), None),
        check_vma=False,
    )
```
